32 devices in a mesh: fsdp: 8 (over z, y), seq: 4 (over x, core).
Axes of the slice: x: 2, y: 2, z: 4, core: 2. Of those that a mesh axis runs over, the one named last changes fastest.
Arguments:
- tokens: bfloat16 [16384, 1152], P(('fsdp', 'seq')), may hold values from -6 to 6
- cotangent: bfloat16 [16384, 1152], P(('fsdp', 'seq')), may hold values from -6 to 6
- positions: int32 [16384], P('fsdp'), may hold values from 0 to 1535, as said below
- segment: int32 [16384], P('fsdp'), may hold values from 0 to 2, as said below
- query_weight: float32 [1152, 1024], P('fsdp'), may hold values from -0.1875 to 0.1875
- key_weight: float32 [1152, 256], P('fsdp'), may hold values from -0.1875 to 0.1875
- value_weight: float32 [1152, 256], P('fsdp'), may hold values from -0.1875 to 0.1875
- out_weight: float32 [1024, 1152], P('fsdp'), may hold values from -0.1875 to 0.1875
- gate_weight: float32 [1152, 6912], P('fsdp'), may hold values from -0.1875 to 0.1875
- up_weight: float32 [1152, 6912], P('fsdp'), may hold values from -0.1875 to 0.1875
- down_weight: float32 [6912, 1152], P('fsdp'), may hold values from -0.078125 to 0.078125
- gain_input: float32 [1152], P('fsdp'), may hold values from 0.25 to 1.75
- gain_query: float32 [256], P('fsdp'), may hold values from 0.25 to 1.75
- gain_key: float32 [256], P('fsdp'), may hold values from 0.25 to 1.75
- gain_mixed: float32 [1152], P('fsdp'), may hold values from 0.25 to 1.75
- gain_feed: float32 [1152], P('fsdp'), may hold values from 0.25 to 1.75
- gain_final: float32 [1152], P('fsdp'), may hold values from 0.25 to 1.75
Outputs:
- output: bfloat16 [16384, 1152], P(('fsdp', 'seq'))
- grad_tokens: float32 [16384, 1152], P(('fsdp', 'seq'))
- grad_query: float32 [1152, 1024], P('fsdp')
- grad_key: float32 [1152, 256], P('fsdp')
- grad_value: float32 [1152, 256], P('fsdp')
- grad_out: float32 [1024, 1152], P('fsdp')
- grad_gate: float32 [1152, 6912], P('fsdp')
- grad_up: float32 [1152, 6912], P('fsdp')
- grad_down: float32 [6912, 1152], P('fsdp')
- grad_gain_input: float32 [1152], P('fsdp')
- grad_gain_query: float32 [256], P('fsdp')
- grad_gain_key: float32 [256], P('fsdp')
- grad_gain_mixed: float32 [1152], P('fsdp')
- grad_gain_feed: float32 [1152], P('fsdp')
- grad_gain_final: float32 [1152], P('fsdp')
The draws below stay inside these ranges and needn't reach their ends.
Inputs may be any that keep to these rules, and one draw needn't show every extreme that they name: `segment`: in each group of 2048 consecutive entries, 1024 are 0 and 512 are c for each c from 1 to 2; each block of 512 entries holds the same number of each value. In each group, the tokens of segment 0 carry the positions 0 to 1023 once each, and the tokens of each continuation the positions 1024 to 1535 once each.
All inputs are finite; a program needn't handle non-finite values.
Results may differ from the reference program's by a relative error of at most 0.018.
The reference program's roundings to bfloat16 on the way count: a program that leaves them out, or rounds other values in their place, can miss the bound.
Values may be sent and summed in bfloat16 or wider, within the bound.
No kernel may reach another device: no remote copies, remote signals or barrier semaphores. Data moves between devices by JAX's collectives and lax.ppermute only.
A program may use at most 320 MiB of HBM per device.

```python
from functools import partial
import jax
import jax.numpy as jnp
from jax import lax

D = 1152
FF = 6912
HEADS = 4
HEAD = 256
PROMPT = 1024
CONT = 512
CONTS = 2
GROUP_TOK = 2048
TOK_DEV = 512
TOKENS = 16384


def shuffled_order(shuffle_key, length):
    return jax.random.permutation(shuffle_key, length)


def group_layout(group_key):
    shards = GROUP_TOK // TOK_DEV
    prompt_part = PROMPT // shards
    cont_part = CONT // shards
    first_key, second_key, third_key = jax.random.split(group_key, 3)
    prompt_order = jax.random.permutation(first_key, PROMPT)
    cont_order = jax.vmap(partial_cont)(jax.random.split(second_key, CONTS))
    device = jnp.arange(shards)[:, None]
    slot = jnp.arange(TOK_DEV)[None, :]
    is_prompt = slot < prompt_part
    rest = jnp.maximum(slot - prompt_part, 0)
    which = jnp.minimum(rest // cont_part, CONTS - 1)
    within = rest % cont_part
    prompt_pos = prompt_order[jnp.minimum(device * prompt_part + slot, PROMPT - 1)]
    cont_pos = PROMPT + cont_order[which, device * cont_part + within]
    seg_table = jnp.where(is_prompt, 0, which + 1).astype(jnp.int32)
    pos_table = jnp.where(is_prompt, prompt_pos, cont_pos).astype(jnp.int32)
    shuffle = jax.vmap(partial_dev)(jax.random.split(third_key, shards))
    seg_table = jnp.take_along_axis(seg_table, shuffle, axis=1)
    pos_table = jnp.take_along_axis(pos_table, shuffle, axis=1)
    return (seg_table.reshape(-1), pos_table.reshape(-1))


def partial_cont(cont_key):
    return shuffled_order(cont_key, CONT)


def partial_dev(dev_key):
    return shuffled_order(dev_key, TOK_DEV)


def token_layout(key):
    group_count = TOKENS // GROUP_TOK
    keys = jax.random.split(jax.random.fold_in(key, 11), group_count)
    seg_all, pos_all = jax.vmap(group_layout)(keys)
    return (seg_all.reshape(-1).astype(jnp.int32), pos_all.reshape(-1).astype(jnp.int32))


def draw_segment(key, part):
    return token_layout(key)[0]


def draw_positions(key, part):
    return token_layout(key)[1]


def shard_levels(key, dims, cuts, smallest, largest):
    level, own = 1.0, jax.random.fold_in(key, 6)
    for axis_at, shards_of in cuts:
        draws = jnp.exp(jax.random.uniform(jax.random.fold_in(own, axis_at), (shards_of,), jnp.float32, smallest / len(cuts), largest / len(cuts)))
        level = level * jnp.repeat(draws, dims[axis_at] // shards_of).reshape([-1 if axis == axis_at else 1 for axis in range(len(dims))])
    return level


def gaussian(rng, dims, spread, reach, cuts=(), held_as=jnp.bfloat16):
    drawn = spread * jax.random.normal(rng, dims, jnp.float32)
    if cuts:
        drawn = drawn * shard_levels(rng, dims, cuts, -0.22, 0.18)
    return jnp.clip(drawn, -reach, reach).astype(held_as)


def setup_inputs(seed: int = 0) -> dict:
    key_of = jax.random.split(jax.random.key(seed), 18)
    tokens = gaussian(key_of[0], (TOKENS, D), 1.0, 6.0, ((0, 32),))
    cotangent = gaussian(key_of[1], (TOKENS, D), 1.0, 6.0, ((0, 32),))
    positions = draw_positions(jax.random.fold_in(key_of[17], 71), 0)
    segment = draw_segment(jax.random.fold_in(key_of[17], 71), 0)
    query_weight = gaussian(key_of[4], (D, HEADS * HEAD), D ** -0.5, 0.1875, ((0, 8),), jnp.float32)
    key_weight = gaussian(key_of[5], (D, HEAD), D ** -0.5, 0.1875, ((0, 8),), jnp.float32)
    value_weight = gaussian(key_of[6], (D, HEAD), D ** -0.5, 0.1875, ((0, 8),), jnp.float32)
    out_weight = gaussian(key_of[7], (HEADS * HEAD, D), (HEADS * HEAD) ** -0.5, 0.1875, ((0, 8),), jnp.float32)
    gate_weight = gaussian(key_of[8], (D, FF), D ** -0.5, 0.1875, ((0, 8),), jnp.float32)
    up_weight = gaussian(key_of[9], (D, FF), D ** -0.5, 0.1875, ((0, 8),), jnp.float32)
    down_weight = gaussian(key_of[10], (FF, D), FF ** -0.5, 0.078125, ((0, 8),), jnp.float32)
    gain_input = jnp.clip(1.0 + 0.15 * jax.random.normal(key_of[11], (D,), jnp.float32), 0.25, 1.75)
    gain_query = jnp.clip(1.0 + 0.15 * jax.random.normal(key_of[12], (HEAD,), jnp.float32), 0.25, 1.75)
    gain_key = jnp.clip(1.0 + 0.15 * jax.random.normal(key_of[13], (HEAD,), jnp.float32), 0.25, 1.75)
    gain_mixed = jnp.clip(1.0 + 0.15 * jax.random.normal(key_of[14], (D,), jnp.float32), 0.25, 1.75)
    gain_feed = jnp.clip(1.0 + 0.15 * jax.random.normal(key_of[15], (D,), jnp.float32), 0.25, 1.75)
    gain_final = jnp.clip(1.0 + 0.15 * jax.random.normal(key_of[16], (D,), jnp.float32), 0.25, 1.75)
    return dict(tokens=tokens, cotangent=cotangent, positions=positions, segment=segment, query_weight=query_weight, key_weight=key_weight, value_weight=value_weight, out_weight=out_weight, gate_weight=gate_weight, up_weight=up_weight, down_weight=down_weight, gain_input=gain_input, gain_query=gain_query, gain_key=gain_key, gain_mixed=gain_mixed, gain_feed=gain_feed, gain_final=gain_final)


@jax.custom_vjp
def low(v):
    return lax.optimization_barrier(v.astype(jnp.bfloat16)).astype(jnp.float32)

@jax.custom_vjp
def low_back(v):
    return v

def low_keep(v):
    return (low(v), None)

def low_pass(kept, grad):
    return (grad,)

def back_keep(v):
    return (v, None)

def back_low(kept, grad):
    return (low(grad),)
low.defvjp(low_keep, low_pass)
low_back.defvjp(back_keep, back_low)
epsilon = 1e-06
highest = lax.Precision.HIGHEST

def rms_scale(values, gain):
    return values * lax.rsqrt(lax.optimization_barrier(jnp.mean(values * values, axis=-1, keepdims=True)) + epsilon) * gain

def rotate(values, cosine, sine):
    half_width = values.shape[-1] // 2
    first_half = values[..., :half_width]
    second_half = values[..., half_width:]
    return jnp.concatenate([first_half * cosine - second_half * sine, second_half * cosine + first_half * sine], axis=-1)

def rope_tables(places, width):
    half_width = width // 2
    inverse = 1.0 / 1000000.0 ** (jnp.arange(half_width, dtype=jnp.float32) * 2.0 / width)
    angles = places.astype(jnp.float32)[:, None] * inverse[None, :]
    return (jnp.cos(angles), jnp.sin(angles))

def allowed_pairs(query_pos, query_seg, key_pos, key_seg):
    causal = key_pos[None, :] <= query_pos[:, None]
    related = (key_seg[None, :] == query_seg[:, None]) | (key_seg[None, :] == 0)
    return causal & related

def product(left, right):
    return jnp.dot(left, right, precision=highest, preferred_element_type=jnp.float32)

def attend_block(query_block, pos_block, seg_block, keys, values, key_pos, key_seg):
    scale_factor = keys.shape[-1] ** (-0.5)
    scores = low_back(jnp.einsum('bhe,ke->hbk', query_block, keys, precision=highest) * scale_factor)
    permitted = allowed_pairs(pos_block, seg_block, key_pos, key_seg)
    scores = jnp.where(permitted[None], scores, -1e+30)
    top = lax.optimization_barrier(jnp.max(scores, axis=-1, keepdims=True))
    expd = jnp.exp(scores - top)
    weights = expd / lax.optimization_barrier(jnp.sum(expd, axis=-1, keepdims=True))
    attended = jnp.einsum('hbk,ke->bhe', low(weights), values, precision=highest)
    return low(low_back(attended))

def attention(queries, keys, values, positions, segment):
    group_count = TOKENS // GROUP_TOK
    block_len = min(512, GROUP_TOK)
    block_count = GROUP_TOK // block_len
    checked = jax.checkpoint(attend_block)

    def one_group(ignored, inputs):
        group_q, group_k, group_v, group_pos, group_seg = inputs

        def one_block(block_inputs):
            query_block, pos_block, seg_block = block_inputs
            return checked(query_block, pos_block, seg_block, group_k, group_v, group_pos, group_seg)
        outputs = lax.map(one_block, (group_q.reshape(block_count, block_len, HEADS, HEAD), group_pos.reshape(block_count, block_len), group_seg.reshape(block_count, block_len)))
        return (ignored, outputs.reshape(GROUP_TOK, HEADS * HEAD))
    ignored, result = lax.scan(one_group, None, (queries.reshape(group_count, GROUP_TOK, HEADS, HEAD), keys.reshape(group_count, GROUP_TOK, HEAD), values.reshape(group_count, GROUP_TOK, HEAD), positions.reshape(group_count, GROUP_TOK), segment.reshape(group_count, GROUP_TOK)))
    return result.reshape(TOKENS, HEADS * HEAD)

def layer_forward(positions, segment, inputs, w_query, w_key, w_value, w_out, w_gate, w_up, w_down, g_input, g_query, g_key, g_mixed, g_feed, g_final):
    w_query, w_key, w_value, w_out = (low(w_query), low(w_key), low(w_value), low(w_out))
    w_gate, w_up, w_down = (low(w_gate), low(w_up), low(w_down))
    g_input, g_query, g_key = (low(g_input), low(g_query), low(g_key))
    g_mixed, g_feed, g_final = (low(g_mixed), low(g_feed), low(g_final))
    normed = low(rms_scale(inputs, g_input))
    query_raw = low_back(product(normed, w_query))
    key_raw = low_back(product(normed, w_key))
    values = low(low_back(product(normed, w_value)))
    cosine, sine = rope_tables(positions, HEAD)
    query_heads = rms_scale(query_raw.reshape(TOKENS, HEADS, HEAD), g_query)
    queries = low(low_back(rotate(query_heads, cosine[:, None, :], sine[:, None, :])))
    keys = low(low_back(rotate(rms_scale(key_raw, g_key), cosine, sine)))
    heads_out = attention(queries, keys, values, positions, segment)
    attn = low_back(product(heads_out, w_out))
    mixed = inputs + rms_scale(attn, g_mixed)
    fed = low(rms_scale(mixed, g_feed))
    gate = low_back(product(fed, w_gate))
    upper = low_back(product(fed, w_up))
    act = low(jax.nn.gelu(gate, approximate=True) * upper)
    ffo = low_back(product(act, w_down))
    return mixed + rms_scale(ffo, g_final)

def reference(tokens, cotangent, positions, segment, query_weight, key_weight, value_weight, out_weight, gate_weight, up_weight, down_weight, gain_input, gain_query, gain_key, gain_mixed, gain_feed, gain_final):
    as_float = jnp.float32
    output, pull = jax.vjp(partial(layer_forward, positions, segment), tokens.astype(as_float), query_weight.astype(as_float), key_weight.astype(as_float), value_weight.astype(as_float), out_weight.astype(as_float), gate_weight.astype(as_float), up_weight.astype(as_float), down_weight.astype(as_float), gain_input.astype(as_float), gain_query.astype(as_float), gain_key.astype(as_float), gain_mixed.astype(as_float), gain_feed.astype(as_float), gain_final.astype(as_float))
    grads = pull(cotangent.astype(as_float))
    return (output.astype(jnp.bfloat16), grads[0], grads[1], grads[2], grads[3], grads[4], grads[5], grads[6], grads[7], grads[8], grads[9], grads[10], grads[11], grads[12], grads[13])
```

```python
from functools import partial

import jax
import jax.numpy as jnp
from jax import lax
from jax.experimental import pallas as pl
from jax.experimental.pallas import tpu as pltpu
from jax.sharding import PartitionSpec as P

epsilon = 1e-06
f32 = jnp.float32
bf16 = jnp.bfloat16
SEQ = 4


def rms_scale(values, gain):
    return values * lax.rsqrt(jnp.mean(values * values, axis=-1, keepdims=True) + epsilon) * gain


def rotate(values, cosine, sine):
    half_width = values.shape[-1] // 2
    first_half = values[..., :half_width]
    second_half = values[..., half_width:]
    return jnp.concatenate(
        [first_half * cosine - second_half * sine, second_half * cosine + first_half * sine],
        axis=-1,
    )


def rope_tables(places, width):
    half_width = width // 2
    inverse = 1.0 / 1000000.0 ** (jnp.arange(half_width, dtype=f32) * 2.0 / width)
    angles = places.astype(f32)[:, None] * inverse[None, :]
    return (jnp.cos(angles), jnp.sin(angles))


def head_norm(raw, gain, cosine, sine):
    return rotate(rms_scale(raw, gain), cosine, sine)


def mult(left, right):
    return jnp.dot(left, right, preferred_element_type=f32)


def inner_rows(left, right):
    return lax.dot_general(left, right, (((0,), (0,)), ((), ())), preferred_element_type=f32)


def outer_cols(left, right):
    return lax.dot_general(left, right, (((1,), (1,)), ((), ())), preferred_element_type=f32)


def to_half(values):
    return values.astype(bf16)


def gated(gate_in, up_in):
    return jax.nn.gelu(gate_in, approximate=True) * up_in


def attend_kernel(scale, q_ref, k_ref, v_ref, code_ref, low_ref, high_ref, out_ref, probs_ref):
    scores = outer_cols(q_ref[...], k_ref[...])
    code = code_ref[...]
    seen = (code >= low_ref[...]) & (code <= high_ref[...])
    expd = jnp.where(seen, jnp.exp2(scores * (scale * 1.4426950408889634)), 0.0)
    total = jnp.sum(expd, axis=1, keepdims=True)
    probs = to_half(expd * (1.0 / total))
    probs_ref[...] = probs
    out_ref[...] = to_half(mult(probs, v_ref[...]))


def attend(queries, keys, values, code, low, high, scale, block):
    rows, width = queries.shape
    count = keys.shape[0]
    whole = pl.BlockSpec((count, width), lambda i: (0, 0))
    slab = pl.BlockSpec((block, width), lambda i: (i, 0))
    thin = pl.BlockSpec((block, 1), lambda i: (i, 0))
    return pl.pallas_call(
        partial(attend_kernel, scale),
        grid=(rows // block,),
        in_specs=[slab, whole, whole, pl.BlockSpec((1, count), lambda i: (0, 0)), thin, thin],
        out_specs=[slab, pl.BlockSpec((block, count), lambda i: (i, 0))],
        out_shape=[
            jax.ShapeDtypeStruct((rows, width), bf16),
            jax.ShapeDtypeStruct((rows, count), bf16),
        ],
        compiler_params=pltpu.CompilerParams(vmem_limit_bytes=40 * 2**20),
        cost_estimate=pl.CostEstimate(
            flops=4 * rows * count * width,
            bytes_accessed=2 * rows * count + 8 * rows * width,
            transcendentals=rows * count,
        ),
    )(queries, keys, values, code, low, high)


def attend_back_kernel(scale, q_ref, k_ref, v_ref, p_ref, g_ref, dq_ref, dk_ref, dv_ref):
    @pl.when(pl.program_id(0) == 0)
    def _():
        dk_ref[...] = jnp.zeros_like(dk_ref)
        dv_ref[...] = jnp.zeros_like(dv_ref)

    probs = p_ref[...]
    grads = g_ref[...]
    wide = probs.astype(f32)
    grad_probs = outer_cols(grads, v_ref[...])
    centre = jnp.sum(wide * grad_probs, axis=1, keepdims=True)
    grad_scores = to_half(wide * (grad_probs - centre))
    dq_ref[...] = to_half(scale * mult(grad_scores, k_ref[...]))
    dk_ref[...] += scale * inner_rows(grad_scores, q_ref[...])
    dv_ref[...] += inner_rows(probs, grads)


def attend_back(queries, keys, values, probs, grads, scale, block):
    rows, width = queries.shape
    count = keys.shape[0]
    whole = pl.BlockSpec((count, width), lambda i: (0, 0))
    slab = pl.BlockSpec((block, width), lambda i: (i, 0))
    return pl.pallas_call(
        partial(attend_back_kernel, scale),
        grid=(rows // block,),
        in_specs=[slab, whole, whole, pl.BlockSpec((block, count), lambda i: (i, 0)), slab],
        out_specs=[slab, whole, whole],
        out_shape=[
            jax.ShapeDtypeStruct((rows, width), bf16),
            jax.ShapeDtypeStruct((count, width), f32),
            jax.ShapeDtypeStruct((count, width), f32),
        ],
        compiler_params=pltpu.CompilerParams(vmem_limit_bytes=48 * 2**20),
        cost_estimate=pl.CostEstimate(
            flops=8 * rows * count * width,
            bytes_accessed=2 * rows * count + 20 * rows * width,
            transcendentals=0,
        ),
    )(queries, keys, values, probs, grads)


def swap_seq(values, bits):
    return lax.ppermute(values, "seq", [(i, i ^ bits) for i in range(SEQ)])


def gather_seq(own):
    one = swap_seq(own, 1)
    two = swap_seq(own, 2)
    return [own, one, two, swap_seq(two, 1)]


def natural(blocks, me):
    stack = jnp.stack(blocks)
    return [lax.dynamic_index_in_dim(stack, me ^ j, 0, keepdims=False) for j in range(SEQ)]


def reduce_seq(blocks):
    three = swap_seq(blocks[3], 1)
    pair = to_half(blocks[2].astype(f32) + three.astype(f32))
    two = swap_seq(pair, 2)
    one = swap_seq(blocks[1], 1)
    return blocks[0].astype(f32) + one.astype(f32) + two.astype(f32)


class Owners:
    def __init__(self, count):
        self.count = count
        self.rows = count // 2
        self.groups = [[2 * z + y for z in range(self.rows)] for y in range(2)]
        index = lax.axis_index("fsdp")
        self.low = index % 2
        self.high = index // 2
        self.direct = self.rows <= 4

    def swap(self, values):
        return lax.ppermute(values, "fsdp", [(i, i ^ 1) for i in range(self.count)])

    def shift(self, values, by):
        return lax.ppermute(
            values, "fsdp", [(i, (i + 2 * by) % self.count) for i in range(self.count)]
        )

    def gather_row(self, values):
        return lax.all_gather(values, "fsdp", axis=0, tiled=True, axis_index_groups=self.groups)

    def pair(self, mine, other, axis):
        first = jnp.where(self.low == 0, mine, other)
        second = jnp.where(self.low == 0, other, mine)
        return jnp.stack([first, second], axis=axis)

    def gather_small(self, own):
        if not self.direct:
            return lax.all_gather(own, "fsdp", axis=0, tiled=True)
        size, width = own.shape
        whole = jnp.zeros((self.rows, 2, size, width), own.dtype)

        def put(whole, block, by, flip):
            z = lax.rem(self.high - by + self.rows, self.rows)
            y = self.low ^ flip
            return lax.dynamic_update_slice(whole, block[None, None], (z, y, 0, 0))

        far = [self.shift(own, by) for by in range(1, self.rows)]
        parts = [own] + far
        flipped = [self.swap(p) for p in parts]
        for by in range(self.rows):
            whole = put(whole, parts[by], by, 0)
            whole = put(whole, flipped[by], by, 1)
        return whole.reshape(self.count * size, width)

    def gather_wide(self, own):
        size, width = own.shape
        mine = self.gather_row(own).reshape(self.rows, size, width)
        other = self.swap(mine)
        return self.pair(mine, other, 1).reshape(self.count * size, width)

    def gather_pair_first(self, own):
        size, width = own.shape
        both = self.pair(own, self.swap(own), 0).reshape(2 * size, width)
        return self.gather_row(both)

    def fold(self, whole):
        size = whole.shape[0] // self.count
        view = whole.reshape(self.rows, 2, size, whole.shape[1])
        away = lax.dynamic_index_in_dim(view, 1 - self.low, 1, keepdims=False)
        here = lax.dynamic_index_in_dim(view, self.low, 1, keepdims=False)
        come = self.swap(away)
        return to_half(here.astype(f32) + come.astype(f32))

    def scatter_wide(self, whole):
        half = self.fold(whole)
        return lax.psum_scatter(
            half.reshape(-1, half.shape[2]),
            "fsdp",
            scatter_dimension=0,
            axis_index_groups=self.groups,
            tiled=True,
        ).astype(f32)

    def scatter_small(self, whole):
        half = self.fold(whole)
        if not self.direct:
            return lax.psum_scatter(
                half.reshape(-1, half.shape[2]),
                "fsdp",
                scatter_dimension=0,
                axis_index_groups=self.groups,
                tiled=True,
            ).astype(f32)
        total = lax.dynamic_index_in_dim(half, self.high, 0, keepdims=False).astype(f32)
        for by in range(1, self.rows):
            z = lax.rem(self.high + by, self.rows)
            away = lax.dynamic_index_in_dim(half, z, 0, keepdims=False)
            total = total + self.shift(away, by).astype(f32)
        return total


def body(
    tokens,
    cotangent,
    positions,
    segment,
    query_weight,
    key_weight,
    value_weight,
    out_weight,
    gate_weight,
    up_weight,
    down_weight,
    gain_input,
    gain_query,
    gain_key,
    gain_mixed,
    gain_feed,
    gain_final,
    fsdp,
):
    owners = Owners(fsdp)
    me = lax.axis_index("seq")
    core = me & 1
    tok_rows, model = tokens.shape
    group_len = positions.shape[0]
    rows = query_weight.shape[0]
    head_width = key_weight.shape[1]
    hidden = gate_weight.shape[1]
    slab = hidden // fsdp
    part = slab // SEQ
    scale = head_width ** (-0.5)

    head_cols = lax.dynamic_slice_in_dim(query_weight, me * head_width, head_width, axis=1)
    key_or_value = jnp.where(core == 0, key_weight, value_weight)
    short = jnp.stack([gain_query, gain_key], axis=1)
    short = jnp.pad(short, ((0, rows - short.shape[0]), (0, 0)))
    gains_own = jnp.concatenate(
        [jnp.stack([gain_input, gain_mixed, gain_feed, gain_final], axis=1), short], axis=1
    )
    gains_own = jnp.pad(gains_own, ((0, 0), (0, 128 - gains_own.shape[1])))
    attn_own = to_half(jnp.concatenate([head_cols, key_or_value, gains_own], axis=1))

    def columns(weight):
        return to_half(
            jnp.concatenate(
                [
                    lax.dynamic_slice_in_dim(weight, f * slab + me * part, part, axis=1)
                    for f in range(fsdp)
                ],
                axis=1,
            )
        )

    gate_own = columns(gate_weight)
    up_own = columns(up_weight)
    down_own = to_half(lax.dynamic_slice_in_dim(down_weight, me * part, part, axis=0))
    out_rows = out_weight.shape[0]
    out_half = out_rows // 2
    out_own = to_half(lax.dynamic_slice_in_dim(out_weight, core * out_half, out_half, axis=0))

    token_blocks = gather_seq(tokens)
    attn_pack = owners.gather_small(attn_own)
    w_gate = owners.gather_wide(gate_own)
    w_out_half = owners.gather_pair_first(out_own)
    w_up = owners.gather_wide(up_own)
    w_down = owners.gather_pair_first(down_own)

    gains = attn_pack[:, 2 * head_width :].astype(f32).T
    g_input, g_mixed, g_feed, g_final = gains[0], gains[1], gains[2], gains[3]
    short_rows = head_width // fsdp
    g_query = gains[4].reshape(fsdp, rows)[:, :short_rows].reshape(head_width)
    g_key = gains[5].reshape(fsdp, rows)[:, :short_rows].reshape(head_width)
    mine_kv = attn_pack[:, head_width : 2 * head_width]
    other_kv = swap_seq(mine_kv, 1)
    w_qkv = jnp.concatenate(
        [
            attn_pack[:, :head_width],
            jnp.where(core == 0, mine_kv, other_kv),
            jnp.where(core == 0, other_kv, mine_kv),
        ],
        axis=1,
    )

    def own_order(values):
        return jnp.concatenate(
            [
                lax.dynamic_slice_in_dim(values, (me ^ r) * tok_rows, tok_rows)
                for r in range(SEQ)
            ]
        )

    places = own_order(positions)
    kinds = own_order(segment)
    cosine, sine = rope_tables(places, head_width)
    second = kinds == 2
    code = jnp.where(second, -places, places).astype(f32)[None, :]
    low = jnp.where(second, -places, 0).astype(f32)[:, None]
    high = jnp.where(second, group_len // 2 - 1, places).astype(f32)[:, None]

    all_tokens = jnp.concatenate(token_blocks).astype(f32)
    normed16 = to_half(rms_scale(all_tokens, g_input))
    qkv = mult(normed16, w_qkv)
    query_raw = qkv[:, :head_width]
    key_raw = qkv[:, head_width : 2 * head_width]
    values = to_half(qkv[:, 2 * head_width :])
    normer = partial(head_norm, cosine=cosine, sine=sine)
    queries, query_back = jax.vjp(normer, query_raw, g_query)
    keys, key_back = jax.vjp(normer, key_raw, g_key)
    queries = to_half(queries)
    keys = to_half(keys)
    attended, probs = attend(queries, keys, values, code, low, high, scale, 256)

    heads = [attended[:tok_rows]] + [
        swap_seq(attended[r * tok_rows : (r + 1) * tok_rows], r) for r in range(1, SEQ)
    ]
    heads16 = jnp.concatenate(natural(heads, me), axis=1)

    other_half = swap_seq(w_out_half, 1).reshape(fsdp, out_half, model)
    mine_half = w_out_half.reshape(fsdp, out_half, model)
    w_out = jnp.stack(
        [
            jnp.where(core == 0, mine_half, other_half),
            jnp.where(core == 0, other_half, mine_half),
        ],
        axis=1,
    ).reshape(fsdp * out_rows, model)
    attn = mult(heads16, w_out)
    inputs32 = tokens.astype(f32)
    post_attn, mixed_back = jax.vjp(rms_scale, attn, g_mixed)
    mixed = inputs32 + post_attn
    fed, feed_back = jax.vjp(lambda v: rms_scale(v, g_feed), mixed)

    fed16 = jnp.concatenate(gather_seq(to_half(fed)))
    gate16 = to_half(mult(fed16, w_gate))
    upper = mult(fed16, w_up)
    act16 = to_half(gated(gate16.astype(f32), upper))
    upper16 = to_half(upper)
    share = to_half(mult(act16, w_down))
    ffo = reduce_seq([share[r * tok_rows : (r + 1) * tok_rows] for r in range(SEQ)])
    post_feed, final_back = jax.vjp(rms_scale, ffo, g_final)
    output = to_half(mixed + post_feed)

    grad_rows = cotangent.astype(f32)
    grad_ffo, gain_final_part = final_back(grad_rows)
    grad_ffo16 = jnp.concatenate(gather_seq(to_half(grad_ffo)))
    grad_act = outer_cols(grad_ffo16, w_down)
    _, act_back = jax.vjp(gated, gate16.astype(f32), upper16.astype(f32))
    grad_gate_in, grad_up_in = act_back(grad_act)
    grad_gate16 = to_half(grad_gate_in)
    grad_up16 = to_half(grad_up_in)
    grad_fed_share = to_half(outer_cols(grad_gate16, w_gate) + outer_cols(grad_up16, w_up))
    grad_gate = owners.scatter_wide(to_half(inner_rows(fed16, grad_gate16)))
    grad_up = owners.scatter_wide(to_half(inner_rows(fed16, grad_up16)))
    grad_down_share = to_half(inner_rows(act16, grad_ffo16))
    grad_fed = reduce_seq([grad_fed_share[r * tok_rows : (r + 1) * tok_rows] for r in range(SEQ)])
    (grad_mixed_part,) = feed_back(grad_fed)
    grad_mixed = grad_rows + grad_mixed_part

    grad_attn, gain_mixed_part = mixed_back(grad_mixed)
    grad_attn16 = to_half(grad_attn)
    grad_heads16 = to_half(outer_cols(grad_attn16, w_out))
    grad_heads = [
        lax.dynamic_slice_in_dim(grad_heads16, (me ^ r) * head_width, head_width, axis=1)
        for r in range(SEQ)
    ]
    grad_heads = [grad_heads[0]] + [swap_seq(grad_heads[r], r) for r in range(1, SEQ)]
    grad_heads = jnp.concatenate(grad_heads)

    grad_out_share = to_half(inner_rows(heads16, grad_attn16))
    out_part = out_rows // SEQ
    grad_out_view = grad_out_share.reshape(fsdp, SEQ, out_part, model)
    grad_out_part = reduce_seq(
        [
            lax.dynamic_index_in_dim(grad_out_view, me ^ r, 1, keepdims=False)
            for r in range(SEQ)
        ]
    )
    grad_rest = owners.scatter_wide(
        jnp.concatenate(
            [grad_down_share.reshape(fsdp, part, model), to_half(grad_out_part)], axis=1
        ).reshape(fsdp * (part + out_part), model)
    )

    grad_queries, grad_keys, grad_values = attend_back(
        queries, keys, values, probs, grad_heads, scale, 256
    )
    grad_query_raw, gain_query_part = query_back(grad_queries.astype(f32))
    grad_key_raw, gain_key_part = key_back(grad_keys)
    grad_qkv16 = jnp.concatenate(
        [to_half(grad_query_raw), to_half(grad_key_raw), to_half(grad_values)], axis=1
    )
    grad_normed_share = to_half(outer_cols(grad_qkv16, w_qkv))
    grad_proj = to_half(inner_rows(normed16, grad_qkv16))
    grad_k = grad_proj[:, head_width : 2 * head_width]
    grad_v = grad_proj[:, 2 * head_width :]
    come = swap_seq(jnp.where(core == 0, grad_v, grad_k), 1)
    grad_kv = jnp.where(core == 0, grad_k, grad_v).astype(f32) + come.astype(f32)
    short = jnp.stack([gain_query_part, gain_key_part], axis=1).reshape(fsdp, short_rows, 2)
    short = jnp.pad(short, ((0, 0), (0, rows - short_rows), (0, 0))).reshape(model, 2)
    gain_parts = jnp.concatenate(
        [jnp.stack([gain_mixed_part, gain_final_part], axis=1), short], axis=1
    )
    gain_parts = jnp.pad(gain_parts, ((0, 0), (0, 128 - gain_parts.shape[1])))
    grad_small = owners.scatter_small(
        jnp.concatenate(
            [grad_proj[:, :head_width], to_half(grad_kv), to_half(gain_parts)], axis=1
        )
    )

    grad_normed = reduce_seq(
        [grad_normed_share[r * tok_rows : (r + 1) * tok_rows] for r in range(SEQ)]
    )
    _, input_back = jax.vjp(lambda v: rms_scale(v, g_input), inputs32)
    (grad_input_part,) = input_back(grad_normed)
    grad_tokens = grad_mixed + grad_input_part

    wide = jnp.concatenate([to_half(grad_gate), to_half(grad_up)], axis=1)
    wide = natural(gather_seq(wide), me)
    rest = natural(gather_seq(to_half(grad_rest)), me)

    def spread(blocks, at):
        width = fsdp * part
        if fsdp <= 8:
            pieces = [
                blocks[t][:, at * width + f * part : at * width + (f + 1) * part]
                for f in range(fsdp)
                for t in range(SEQ)
            ]
            return jnp.concatenate(pieces, axis=1).astype(f32)
        stack = jnp.stack([b[:, at * width : (at + 1) * width].reshape(rows, fsdp, part) for b in blocks], axis=2)
        return stack.reshape(rows, hidden).astype(f32)

    out_gate = spread(wide, 0)
    out_up = spread(wide, 1)
    out_down = jnp.concatenate([b[:part] for b in rest]).astype(f32)
    out_out = jnp.concatenate([b[part:] for b in rest]).astype(f32)

    feed_sum = jnp.sum(grad_gate * gate_own.astype(f32) + grad_up * up_own.astype(f32), axis=1)
    input_sum = jnp.sum(
        grad_small[:, : 2 * head_width] * attn_own[:, : 2 * head_width].astype(f32), axis=1
    )
    tail = jnp.concatenate(
        [grad_small[:, 2 * head_width : 2 * head_width + 4], jnp.stack([input_sum, feed_sum], axis=1)],
        axis=1,
    )
    tail = jnp.pad(tail, ((0, 0), (0, 128 - tail.shape[1])))
    small = gather_seq(to_half(jnp.concatenate([grad_small[:, : 2 * head_width], tail], axis=1)))
    out_query = jnp.concatenate([b[:, :head_width] for b in natural(small, me)], axis=1).astype(f32)
    kv = [b[:, head_width : 2 * head_width].astype(f32) for b in small]
    same, cross = kv[0] + kv[2], kv[1] + kv[3]
    out_key = jnp.where(core == 0, same, cross)
    out_value = jnp.where(core == 0, cross, same)
    tails = sum(b[:, 2 * head_width :].astype(f32) for b in small)
    own_gains = attn_own[:, 2 * head_width :].astype(f32)
    out_g_mixed = tails[:, 0]
    out_g_final = tails[:, 1]
    out_g_query = tails[:short_rows, 2]
    out_g_key = tails[:short_rows, 3]
    out_g_input = tails[:, 4] / own_gains[:, 0]
    out_g_feed = tails[:, 5] / own_gains[:, 2]
    return (
        output,
        grad_tokens,
        out_query,
        out_key,
        out_value,
        out_out,
        out_gate,
        out_up,
        out_down,
        out_g_input,
        out_g_query,
        out_g_key,
        out_g_mixed,
        out_g_feed,
        out_g_final,
    )


def solution(mesh):
    by_token = P(("fsdp", "seq"), None)
    by_row = P("fsdp", None)
    by_one = P("fsdp")
    return jax.shard_map(
        partial(body, fsdp=mesh.shape["fsdp"]),
        mesh=mesh,
        in_specs=(by_token,) * 2 + (by_one,) * 2 + (by_row,) * 7 + (by_one,) * 6,
        out_specs=(by_token,) * 2 + (by_row,) * 7 + (by_one,) * 6,
        check_vma=False,
    )
```

```python
from functools import partial

import jax
import jax.numpy as jnp
from jax import lax
from jax.experimental import pallas as pl
from jax.experimental.pallas import tpu as pltpu
from jax.sharding import PartitionSpec as P

epsilon = 1e-06
f32 = jnp.float32
bf16 = jnp.bfloat16
SEQ = 4


def rms_scale(values, gain):
    return values * lax.rsqrt(jnp.mean(values * values, axis=-1, keepdims=True) + epsilon) * gain


def rotate(values, cosine, sine):
    half_width = values.shape[-1] // 2
    first_half = values[..., :half_width]
    second_half = values[..., half_width:]
    return jnp.concatenate(
        [first_half * cosine - second_half * sine, second_half * cosine + first_half * sine],
        axis=-1,
    )


def rope_tables(places, width):
    half_width = width // 2
    inverse = 1.0 / 1000000.0 ** (jnp.arange(half_width, dtype=f32) * 2.0 / width)
    angles = places.astype(f32)[:, None] * inverse[None, :]
    return (jnp.cos(angles), jnp.sin(angles))


def head_norm(raw, gain, cosine, sine):
    return rotate(rms_scale(raw, gain), cosine, sine)


def mult(left, right):
    return jnp.dot(left, right, preferred_element_type=f32)


def inner_rows(left, right):
    return lax.dot_general(left, right, (((0,), (0,)), ((), ())), preferred_element_type=f32)


def outer_cols(left, right):
    return lax.dot_general(left, right, (((1,), (1,)), ((), ())), preferred_element_type=f32)


def to_half(values):
    return values.astype(bf16)


def gated(gate_in, up_in):
    return jax.nn.gelu(gate_in, approximate=True) * up_in


MIB = 2**20


def held(shape):
    return pl.BlockSpec(shape, lambda *at: (0,) * len(shape), pipeline_mode=pl.Buffered(1))


def call(kernel, grid, in_specs, out_specs, outs, flops, limit=60, scratch=(), exps=0):
    shapes = [jax.ShapeDtypeStruct(s, d) for s, d in outs]
    size = sum(o.size * o.dtype.itemsize for o in shapes)
    made = pl.pallas_call(
        kernel,
        grid=grid,
        in_specs=in_specs,
        out_specs=out_specs,
        out_shape=shapes,
        scratch_shapes=list(scratch),
        compiler_params=pltpu.CompilerParams(vmem_limit_bytes=limit * MIB),
        cost_estimate=pl.CostEstimate(
            flops=flops // 50, bytes_accessed=size // 50, transcendentals=exps // 50
        ),
    )
    return lambda *operands: list(made(*operands))


def fused_kernel(function, ins, outs, sums, *refs):
    results = function(*[ref[...] for ref in refs[:ins]])
    for ref, value in zip(refs[ins : ins + outs], results[:outs], strict=True):
        ref[...] = value.astype(ref.dtype)
    for ref, value in zip(refs[ins + outs :], results[outs:], strict=True):

        @pl.when(pl.program_id(0) == 0)
        def _():
            ref[...] = jnp.zeros_like(ref)

        ref[...] += value


def fused(function, by_row, whole, outs, steps, sums=()):
    def split(shape):
        return pl.BlockSpec(
            (shape[0] // steps, *shape[1:]), lambda i: (i, *(0 for _ in shape[1:]))
        )

    return call(
        partial(fused_kernel, function, len(by_row) + len(whole), len(outs), len(sums)),
        (steps,),
        [split(v.shape) for v in by_row] + [held(v.shape) for v in whole],
        [split(s) for s, _ in outs] + [pl.BlockSpec(s, lambda i: (0, 0)) for s in sums],
        [*outs, *((s, f32) for s in sums)],
        flops=0,
    )(*by_row, *whole)


def add_half(first, second, steps):
    function = lambda a, b: (a.astype(f32) + b.astype(f32),)
    return fused(function, [first, second], [], [(first.shape, bf16)], steps)[0]


def rms_back(values, gain, grad):
    r = lax.rsqrt(jnp.mean(values * values, axis=-1, keepdims=True) + epsilon)
    scaled = grad * gain
    mean = jnp.mean(values * scaled, axis=-1, keepdims=True)
    return r * scaled - values * (r * r * r * mean), grad * values * r


def column_sum(values):
    return jnp.sum(values, axis=0, keepdims=True)


def mid_kernel(owners, quarters, me_ref, x_ref, *refs):
    heads = refs[:SEQ]
    weights = refs[SEQ : SEQ + quarters]
    gains_ref, all_ref, w_ref, attn_ref, mixed_ref, fed_ref = refs[SEQ + quarters :]
    width = heads[0].shape[1]
    for r, head in enumerate(heads):
        start = pl.multiple_of(jnp.bitwise_xor(me_ref[0], r) * width, 128)
        all_ref[:, pl.ds(start, width)] = head[...]
    if quarters == 1:
        w_ref[...] = weights[0][...]
    else:
        for r, weight in enumerate(weights):
            size = weight.shape[0] // owners
            for f in range(owners):
                start = (f * SEQ + jnp.bitwise_xor(me_ref[0], r)) * size
                start = pl.multiple_of(start, 16)
                w_ref[pl.ds(start, size), :] = weight[f * size : (f + 1) * size, :]
    attn = mult(all_ref[...], w_ref[...])
    attn_ref[...] = attn
    mixed = x_ref[...].astype(f32) + rms_scale(attn, gains_ref[1:2, :])
    mixed_ref[...] = mixed
    fed_ref[...] = to_half(rms_scale(mixed, gains_ref[2:3, :]))


def mid(me, tokens, heads, weights, gains, owners):
    rows, model = tokens.shape
    width = heads[0].shape[1] * SEQ
    specs = [held(v.shape) for v in [tokens, *heads, *weights, gains]]
    outs = [
        ((rows, width), bf16),
        ((width, model), bf16),
        ((rows, model), f32),
        ((rows, model), f32),
        ((rows, model), bf16),
    ]
    return call(
        partial(mid_kernel, owners, len(weights)),
        (1,),
        [pl.BlockSpec(memory_space=pltpu.SMEM)] + specs,
        [pl.BlockSpec(s, lambda i: (0, 0)) for s, _ in outs],
        outs,
        flops=2 * rows * width * model,
    )(me, tokens, *heads, *weights, gains)


def mid_back_kernel(me_ref, a_ref, b_ref, c_ref, dy_ref, mixed_ref, attn_ref, w_ref, gains_ref, *refs):
    grad_ref, grad_attn_ref = refs[:2]
    outs, sum_ref, heads_ref = refs[2 : 2 + SEQ], refs[2 + SEQ], refs[3 + SEQ]
    grad_fed = a_ref[...].astype(f32) + b_ref[...].astype(f32) + c_ref[...].astype(f32)
    part, _ = rms_back(mixed_ref[...], gains_ref[2:3, :], grad_fed)
    grad_mixed = dy_ref[...].astype(f32) + part
    grad_ref[...] = grad_mixed
    grad_attn, terms = rms_back(attn_ref[...], gains_ref[1:2, :], grad_mixed)
    half = to_half(grad_attn)
    grad_attn_ref[...] = half
    heads_ref[...] = to_half(outer_cols(half, w_ref[...]))
    width = outs[0].shape[1]
    for r, out in enumerate(outs):
        start = pl.multiple_of(jnp.bitwise_xor(me_ref[0], r) * width, 128)
        out[...] = heads_ref[:, pl.ds(start, width)]

    @pl.when(pl.program_id(0) == 0)
    def _():
        sum_ref[...] = jnp.zeros_like(sum_ref)

    sum_ref[...] += column_sum(terms)


def mid_back(me, shares, cotangent, mixed, attn, w_out, gains, steps):
    rows, model = mixed.shape
    total = w_out.shape[0]
    by_row = [*shares, cotangent, mixed, attn]
    row = lambda width: pl.BlockSpec((rows // steps, width), lambda i: (i, 0))
    outs = [((rows, model), f32), ((rows, model), bf16)]
    outs += [((rows, total // SEQ), bf16)] * SEQ
    return call(
        mid_back_kernel,
        (steps,),
        [pl.BlockSpec(memory_space=pltpu.SMEM)]
        + [row(model) for _ in by_row]
        + [held(w_out.shape), held(gains.shape)],
        [row(s[1]) for s, _ in outs] + [pl.BlockSpec((1, model), lambda i: (0, 0))],
        [*outs, ((1, model), f32)],
        flops=2 * rows * model * total,
        scratch=[pltpu.VMEM((rows // steps, total), bf16)],
    )(me, *by_row, w_out, gains)


def turn_back(grad, cosine, sine):
    half = grad.shape[-1] // 2
    a, b = grad[:, :half], grad[:, half:]
    return jnp.concatenate([a * cosine + b * sine, b * cosine - a * sine], axis=-1)


def project_back_kernel(core_ref, *refs):
    dq_ref, keep_ref, come_ref, q_raw_ref, kv_raw_ref, cos_ref, sin_ref, gains_ref, w_ref = refs[:9]
    grad_ref, q_sum_ref, k_sum_ref = refs[9:12]
    outs = refs[12:]
    cosine, sine = cos_ref[...], sin_ref[...]
    head = dq_ref.shape[1]
    first = core_ref[0] == 0
    grad_q, q_terms = rms_back(
        q_raw_ref[...], gains_ref[4:5, :], turn_back(dq_ref[...], cosine, sine)
    )
    grad_kv = keep_ref[...] + come_ref[...].astype(f32)
    grad_k, k_terms = rms_back(
        kv_raw_ref[...], gains_ref[5:6, :], turn_back(grad_kv, cosine, sine)
    )
    grad_ref[:, :head] = to_half(grad_q)
    grad_ref[:, head:] = to_half(jnp.where(first, grad_k, grad_kv))
    share = to_half(outer_cols(grad_ref[...], w_ref[...]))
    for r, out in enumerate(outs):

        @pl.when(pl.program_id(0) == r)
        def _():
            out[...] = share

    @pl.when(pl.program_id(0) == 0)
    def _():
        q_sum_ref[...] = jnp.zeros_like(q_sum_ref)
        k_sum_ref[...] = jnp.zeros_like(k_sum_ref)

    q_sum_ref[...] += column_sum(q_terms)
    k_sum_ref[...] += jnp.where(first, column_sum(k_terms), 0.0)


def project_back(core, dq, keep, come, q_raw, kv_raw, cosine, sine, head_gains, w_own):
    rows, head = dq.shape
    model = w_own.shape[0]
    block = rows // SEQ
    by_row = [dq, keep, come, q_raw, kv_raw, cosine, sine]
    row = lambda width: pl.BlockSpec((block, width), lambda i: (i, 0))
    fixed = lambda shape: pl.BlockSpec(shape, lambda i: (0, 0))
    return call(
        project_back_kernel,
        (SEQ,),
        [pl.BlockSpec(memory_space=pltpu.SMEM)]
        + [row(v.shape[1]) for v in by_row]
        + [held(head_gains.shape), held(w_own.shape)],
        [row(2 * head), fixed((1, head)), fixed((1, head))] + [fixed((block, model))] * SEQ,
        [((rows, 2 * head), bf16), ((1, head), f32), ((1, head), f32)]
        + [((block, model), bf16)] * SEQ,
        flops=4 * rows * head * model,
    )(core, *by_row, head_gains, w_own)


def front_kernel(count, rows, short, packed, meta_ref, *refs):
    tokens = refs[:SEQ]
    pieces = refs[SEQ : SEQ + count]
    cos_ref, sin_ref = refs[SEQ + count : SEQ + count + 2]
    normed_ref, q_ref, kv_ref, q_raw_ref, kv_raw_ref, w_ref, out_ref, gains_ref, head_gains_ref = (
        refs[SEQ + count + 2 : -2]
    )
    x_ref, columns_ref = refs[-2:]
    at = pl.program_id(0)
    head = q_ref.shape[1]

    @pl.when(at == 0)
    def _():
        for j, piece in enumerate(pieces):
            size = piece.shape[0] - 2 * packed
            start = pl.multiple_of(meta_ref[1 + j] * rows, 16)
            w_ref[pl.ds(start, size), :] = piece[:size, : 2 * head]
            columns_ref[pl.ds(start, size), :] = piece[:size, 2 * head :].astype(f32)
            if packed:
                start = pl.multiple_of(meta_ref[1 + j] * packed, 16)
                wide = piece.shape[1]
                rest = out_ref.shape[1] - wide
                out_ref[pl.ds(start, packed), :wide] = piece[size : size + packed, :]
                out_ref[pl.ds(start, packed), wide:] = piece[size + packed :, :rest]
        gains = columns_ref[...].T[:8]
        gains_ref[...] = gains
        model = gains.shape[1]
        from_row = lax.broadcasted_iota(jnp.int32, (model, head), 0)
        to_col = lax.broadcasted_iota(jnp.int32, (model, head), 1)
        owner = to_col >> (short.bit_length() - 1)
        wanted = owner * rows + (to_col & (short - 1))
        pick = jnp.where(from_row == wanted, 1.0, 0.0)
        head_gains_ref[...] = mult(to_half(gains), to_half(pick))

    for r in range(SEQ):

        @pl.when(at == r)
        def _():
            x_ref[...] = tokens[r][...].astype(f32)

    values = x_ref[...]
    normed = to_half(rms_scale(values, gains_ref[0:1, :]))
    normed_ref[...] = normed
    raw = mult(normed, w_ref[...])
    q_raw = raw[:, :head]
    kv_raw = raw[:, head:]
    q_raw_ref[...] = q_raw
    kv_raw_ref[...] = kv_raw
    cosine, sine = cos_ref[...], sin_ref[...]
    q_ref[...] = to_half(head_norm(q_raw, head_gains_ref[4:5, :], cosine, sine))
    keyed = head_norm(kv_raw, head_gains_ref[5:6, :], cosine, sine)
    kv_ref[...] = to_half(jnp.where(meta_ref[0] == 0, keyed, kv_raw))


def front(tokens, pieces, meta, cosine, sine, rows, short, packed):
    block, model = tokens[0].shape
    head = 2 * cosine.shape[1]
    total = block * SEQ
    out_shape = (max(8, packed * len(pieces)), model)
    slab = lambda width: pl.BlockSpec((block, width), lambda i: (i, 0))
    fixed = lambda shape: pl.BlockSpec(shape, lambda i: (0, 0))
    return call(
        partial(front_kernel, len(pieces), rows, short, packed),
        (SEQ,),
        [pl.BlockSpec(memory_space=pltpu.SMEM)]
        + [held(t.shape) for t in tokens]
        + [held(p.shape) for p in pieces]
        + [slab(head // 2)] * 2,
        [slab(model), slab(head), slab(head), slab(head), slab(head)]
        + [fixed((model, 2 * head)), fixed(out_shape), fixed((8, model)), fixed((8, head))],
        [
            ((total, model), bf16),
            ((total, head), bf16),
            ((total, head), bf16),
            ((total, head), f32),
            ((total, head), f32),
            ((model, 2 * head), bf16),
            (out_shape, bf16),
            ((8, model), f32),
            ((8, head), f32),
        ],
        flops=4 * total * model * head,
        scratch=[
            pltpu.VMEM((block, model), f32),
            pltpu.VMEM((model, 128), f32),
        ],
    )(meta, *tokens, *pieces, cosine, sine)


def twins(values):
    size = values.shape[0] // SEQ
    return jnp.concatenate([values[(r ^ 1) * size : (r ^ 1) * size + size] for r in range(SEQ)])


def split_pair(meta_ref, mine_ref, other_ref, keys_ref, values_ref):
    mine, other = mine_ref[...], twins(other_ref[...])
    first = meta_ref[0] == 0

    @pl.when(first)
    def _():
        keys_ref[...] = mine
        values_ref[...] = other

    @pl.when(jnp.logical_not(first))
    def _():
        keys_ref[...] = other
        values_ref[...] = mine


def attend_kernel(
    scale, meta_ref, q_ref, mine_ref, other_ref, code_ref, low_ref, high_ref, *refs
):
    outs, (probs_ref, keys_ref, values_ref) = refs[:SEQ], refs[SEQ:]
    at = pl.program_id(0)

    @pl.when(at == 0)
    def _():
        split_pair(meta_ref, mine_ref, other_ref, keys_ref, values_ref)

    scores = outer_cols(q_ref[...], keys_ref[...])
    code = code_ref[...]
    seen = (code >= low_ref[...]) & (code <= high_ref[...])
    expd = jnp.where(seen, jnp.exp2(scores * (scale * 1.4426950408889634)), 0.0)
    total = jnp.sum(expd, axis=1, keepdims=True)
    probs = to_half(expd * (1.0 / total))
    probs_ref[...] = probs
    out = to_half(mult(probs, values_ref[...]))
    block = out.shape[0]
    steps = outs[0].shape[0] // block
    for r in range(SEQ):
        for s in range(steps):

            @pl.when(at == r * steps + s)
            def _():
                outs[r][s * block : (s + 1) * block, :] = out


def attend(meta, queries, mine, other, code, low, high, scale, block):
    rows, width = queries.shape
    count = mine.shape[0]
    slab = pl.BlockSpec((block, width), lambda i: (i, 0))
    thin = pl.BlockSpec((block, 1), lambda i: (i, 0))
    part = pl.BlockSpec((rows // SEQ, width), lambda i: (0, 0))
    return call(
        partial(attend_kernel, scale),
        (rows // block,),
        [pl.BlockSpec(memory_space=pltpu.SMEM), slab, held(mine.shape), held(mine.shape)]
        + [pl.BlockSpec((1, count), lambda i: (0, 0)), thin, thin],
        [part] * SEQ + [pl.BlockSpec((block, count), lambda i: (i, 0))],
        [((rows // SEQ, width), bf16)] * SEQ + [((rows, count), bf16)],
        flops=4 * rows * count * width,
        exps=rows * count,
        scratch=[pltpu.VMEM((count, width), bf16)] * 2,
    )(meta, queries, mine, other, code, low, high)


def attend_back_kernel(scale, meta_ref, q_ref, mine_ref, other_ref, p_ref, *refs):
    grads_in = refs[:SEQ]
    dq_ref, keep_ref, send_ref, keys_ref, values_ref, dk_ref, dv_ref, g_ref = refs[SEQ:]
    at = pl.program_id(0)

    @pl.when(at == 0)
    def _():
        split_pair(meta_ref, mine_ref, other_ref, keys_ref, values_ref)
        dk_ref[...] = jnp.zeros_like(dk_ref)
        dv_ref[...] = jnp.zeros_like(dv_ref)

    block = g_ref.shape[0]
    steps = grads_in[0].shape[0] // block
    for r in range(SEQ):
        for s in range(steps):

            @pl.when(at == r * steps + s)
            def _():
                g_ref[...] = grads_in[r][s * block : (s + 1) * block, :]

    probs = p_ref[...]
    grads = g_ref[...]
    wide = probs.astype(f32)
    grad_probs = outer_cols(grads, values_ref[...])
    centre = jnp.sum(wide * grad_probs, axis=1, keepdims=True)
    grad_scores = to_half(wide * (grad_probs - centre))
    dq_ref[...] = scale * mult(grad_scores, keys_ref[...])
    dk_ref[...] += scale * inner_rows(grad_scores, q_ref[...])
    dv_ref[...] += inner_rows(probs, grads)

    @pl.when(at == pl.num_programs(0) - 1)
    def _():
        first = meta_ref[0] == 0
        keep_ref[...] = jnp.where(first, dk_ref[...], dv_ref[...])
        send_ref[...] = twins(to_half(jnp.where(first, dv_ref[...], dk_ref[...])))


def attend_back(meta, queries, mine, other, probs, grads, scale, block):
    rows, width = queries.shape
    count = mine.shape[0]
    whole = pl.BlockSpec((count, width), lambda i: (0, 0))
    slab = pl.BlockSpec((block, width), lambda i: (i, 0))
    return call(
        partial(attend_back_kernel, scale),
        (rows // block,),
        [pl.BlockSpec(memory_space=pltpu.SMEM), slab, held(mine.shape), held(mine.shape)]
        + [pl.BlockSpec((block, count), lambda i: (i, 0))]
        + [held(g.shape) for g in grads],
        [slab, whole, whole],
        [((rows, width), f32), ((count, width), f32), ((count, width), bf16)],
        flops=8 * rows * count * width,
        scratch=[pltpu.VMEM((count, width), bf16)] * 2
        + [pltpu.VMEM((count, width), f32)] * 2
        + [pltpu.VMEM((block, width), bf16)],
    )(meta, queries, mine, other, probs, *grads)


def pick_block(blocks, into_ref):
    for r, block in enumerate(blocks):

        @pl.when(pl.program_id(0) == r)
        def _():
            into_ref[...] = block[...]


def gate_up_kernel(count, pieces, meta_ref, *refs):
    parts, outs = refs[count : count + 2 * pieces], refs[count + 2 * pieces :]
    act_ref, value_ref, slope_ref = outs[:3]
    x_ref = outs[-1]
    gate_ref, up_ref = outs[3:5] if pieces == 2 else parts

    if pieces == 2:

        @pl.when(pl.program_id(0) == 0)
        def _():
            for w_ref, own in ((gate_ref, parts[:2]), (up_ref, parts[2:])):
                for half, ref in enumerate(own):
                    size = ref.shape[1]
                    for z in range(ref.shape[0]):
                        start = (2 * z + jnp.bitwise_xor(meta_ref[0], half)) * size
                        w_ref[pl.ds(pl.multiple_of(start, 16), size), :] = ref[z]

    pick_block(refs[:count], x_ref)
    rows = x_ref[...]
    gate = mult(rows, gate_ref[...])
    upper = mult(rows, up_ref[...])
    c = 0.7978845608028654
    square = gate * gate
    bend = jnp.tanh(gate * (c + (c * 0.044715) * square))
    half = 0.5 + 0.5 * bend
    value = gate * half
    slope = half + (0.5 * gate) * (1.0 - bend * bend) * (c + (3 * c * 0.044715) * square)
    act_ref[...] = to_half(value * upper)
    value_ref[...] = to_half(value)
    slope_ref[...] = to_half(slope * upper)


def gate_up(meta, blocks, gate_parts, up_parts):
    block, model = blocks[0].shape
    width = gate_parts[0].shape[-1]
    total = block * len(blocks)
    slab = pl.BlockSpec((block, width), lambda i: (i, 0))
    whole = pl.BlockSpec((model, width), lambda i: (0, 0))
    parts = [*gate_parts, *up_parts]
    made = len(parts) - 2
    out = call(
        partial(gate_up_kernel, len(blocks), len(gate_parts)),
        (len(blocks),),
        [pl.BlockSpec(memory_space=pltpu.SMEM)] + [held(b.shape) for b in [*blocks, *parts]],
        [slab] * 3 + [whole] * made,
        [((total, width), bf16)] * 3 + [((model, width), bf16)] * made,
        flops=4 * total * model * width,
        exps=total * width,
        scratch=[pltpu.VMEM((block, model), bf16)],
        limit=62,
    )(meta, *blocks, *parts)
    return out if made else out + parts


def down_kernel(x_ref, w_ref, *outs):
    out = to_half(mult(x_ref[...], w_ref[...]))
    for r, ref in enumerate(outs):

        @pl.when(pl.program_id(0) == r)
        def _():
            ref[...] = out


def down(rows, w_down, count):
    block = rows.shape[0] // count
    width, model = w_down.shape
    out = pl.BlockSpec((block, model), lambda i: (0, 0))
    return call(
        down_kernel,
        (count,),
        [pl.BlockSpec((block, width), lambda i: (i, 0)), held(w_down.shape)],
        [out] * count,
        [((block, model), bf16)] * count,
        flops=2 * count * block * model * width,
    )(rows, w_down)


def back_kernel(count, *refs):
    y_refs = refs[:count]
    value_ref, slope_ref, down_ref, gate_ref, up_ref, dg_ref, du_ref = refs[count : count + 7]
    outs, y_ref = refs[count + 7 : -1], refs[-1]
    pick_block(y_refs, y_ref)
    grad_act = outer_cols(y_ref[...], down_ref[...])
    dg_ref[...] = to_half(grad_act * slope_ref[...].astype(f32))
    du_ref[...] = to_half(grad_act * value_ref[...].astype(f32))
    out = to_half(outer_cols(dg_ref[...], gate_ref[...]) + outer_cols(du_ref[...], up_ref[...]))
    for r, ref in enumerate(outs):

        @pl.when(pl.program_id(0) == r)
        def _():
            ref[...] = out


def back(blocks, value, slope, w_down, w_gate, w_up):
    block, model = blocks[0].shape
    count = len(blocks)
    width = w_gate.shape[1]
    slab = pl.BlockSpec((block, width), lambda i: (i, 0))
    out = pl.BlockSpec((block, model), lambda i: (0, 0))
    return call(
        partial(back_kernel, count),
        (count,),
        [held(b.shape) for b in blocks]
        + [slab, slab, held(w_down.shape), held(w_gate.shape), held(w_up.shape)],
        [slab, slab] + [out] * count,
        [((block * count, width), bf16)] * 2 + [((block, model), bf16)] * count,
        flops=6 * count * block * model * width,
        scratch=[pltpu.VMEM((block, model), bf16)],
    )(*blocks, value, slope, w_down, w_gate, w_up)


def cut_rows(blocks, many):
    each = many // len(blocks)
    size = blocks[0].shape[0] // each
    return [b[r * size : (r + 1) * size] for b in blocks for r in range(each)]


def rows_sum(left, right):
    total = inner_rows(left[0], right[0])
    for a, b in zip(left[1:], right[1:], strict=True):
        total = total + inner_rows(a, b)
    return total


def rows_kernel(counts, many, meta_ref, *refs):
    total_in = sum(counts)
    results = len(counts) - 1
    values = [ref[...] for ref in refs[:total_in]]
    left = cut_rows(values[: counts[0]], many)
    at = counts[0]
    totals = []
    for count in counts[1:]:
        totals.append(rows_sum(left, cut_rows(values[at : at + count], many)))
        at += count
    if len(refs) == total_in + results:
        for ref, total in zip(refs[total_in:], totals, strict=True):
            ref[...] = to_half(total)
        return
    outs, sums = refs[total_in : total_in + 2 * results], refs[total_in + 2 * results :]
    tile = left[0].shape[1]
    here = pl.ds(pl.multiple_of(pl.program_id(0) * tile, 128), tile)
    for ref, total in zip(sums, totals, strict=True):
        ref[here, :] = total

    @pl.when(pl.program_id(0) == pl.num_programs(0) - 1)
    def _():
        for o in range(results):
            for half, ref in enumerate(outs[2 * o : 2 * o + 2]):
                size = ref.shape[1]
                for z in range(ref.shape[0]):
                    start = (2 * z + jnp.bitwise_xor(meta_ref[0], 1 - half)) * size
                    ref[z] = to_half(sums[o][pl.ds(pl.multiple_of(start, 8), size), :])


def rows_product(meta, left, rights, tile, owners, cut=True):
    counts = [len(v) for v in [left, *rights]]
    many = max(counts)
    height = left[0].shape[1]
    widths = [r[0].shape[1] for r in rights]
    flat = [v for r in rights for v in r]
    steps = pl.cdiv(height, tile)
    shape = lambda w: (owners // 2, height // owners, w)
    if cut:
        specs = [pl.BlockSpec(shape(w), lambda i: (0, 0, 0)) for w in widths for _ in range(2)]
        outs = [(shape(w), bf16) for w in widths for _ in range(2)]
    else:
        specs = [pl.BlockSpec((tile, w), lambda i: (i, 0)) for w in widths]
        outs = [((height, w), bf16) for w in widths]
    return call(
        partial(rows_kernel, counts, many),
        (steps,),
        [pl.BlockSpec(memory_space=pltpu.SMEM)]
        + [pl.BlockSpec((v.shape[0], tile), lambda i: (0, i)) for v in left]
        + [held(v.shape) for v in flat],
        specs,
        outs,
        flops=2 * sum(v.shape[0] for v in left) * height * sum(widths),
        scratch=[pltpu.VMEM((steps * tile, w), f32) for w in widths] if cut else [],
        limit=62,
    )(meta, *left, *flat)


def after(value, *others):
    return lax.optimization_barrier((value, others))[0]


def swap_seq(values, bits):
    return lax.ppermute(values, "seq", [(i, i ^ bits) for i in range(SEQ)])


def gather_seq(own):
    one = swap_seq(own, 1)
    two = swap_seq(own, 2)
    return [own, one, two, swap_seq(two, 1)]


def natural(blocks, me):
    stack = jnp.stack(blocks)
    return [lax.dynamic_index_in_dim(stack, me ^ j, 0, keepdims=False) for j in range(SEQ)]


def reduce_seq(blocks):
    three = swap_seq(blocks[3], 1)
    pair = to_half(blocks[2].astype(f32) + three.astype(f32))
    two = swap_seq(pair, 2)
    one = swap_seq(blocks[1], 1)
    return blocks[0].astype(f32) + one.astype(f32) + two.astype(f32)


class Owners:
    def __init__(self, count):
        self.count = count
        self.rows = count // 2
        self.groups = [[2 * z + y for z in range(self.rows)] for y in range(2)]
        index = lax.axis_index("fsdp")
        self.low = index % 2
        self.high = index // 2
        self.direct = self.rows <= 4

    def swap(self, values):
        return lax.ppermute(values, "fsdp", [(i, i ^ 1) for i in range(self.count)])

    def shift(self, values, by):
        return lax.ppermute(
            values, "fsdp", [(i, (i + 2 * by) % self.count) for i in range(self.count)]
        )

    def gather_row(self, values):
        return lax.all_gather(values, "fsdp", axis=0, tiled=True, axis_index_groups=self.groups)

    def pair(self, mine, other, axis):
        first = jnp.where(self.low == 0, mine, other)
        second = jnp.where(self.low == 0, other, mine)
        return jnp.stack([first, second], axis=axis)

    def gather_pieces(self, own):
        if not self.direct:
            return [lax.all_gather(own, "fsdp", axis=0, tiled=True)], [jnp.int32(0)]
        far = [own] + [self.shift(own, by) for by in range(1, self.rows)]
        near = [self.swap(p) for p in far]
        starts = [lax.rem(self.high - by + self.rows, self.rows) * 2 for by in range(self.rows)]
        places = [s + self.low for s in starts] + [s + 1 - self.low for s in starts]
        return far + near, places

    def gather_wide(self, own, later):
        if not self.direct:
            return [lax.all_gather(own, "fsdp", axis=0, tiled=True)]
        size, width = own.shape
        mine = after(self.gather_row(own), later).reshape(self.rows, size, width)
        return [mine, self.swap(mine)]

    def gather_pair_first(self, own):
        size, width = own.shape
        both = self.pair(own, self.swap(own), 0).reshape(2 * size, width)
        return self.gather_row(both)

    def halves(self, whole):
        size = whole.shape[0] // self.count
        view = whole.reshape(self.rows, 2, size, whole.shape[1])
        away = lax.dynamic_index_in_dim(view, 1 - self.low, 1, keepdims=False)
        here = lax.dynamic_index_in_dim(view, self.low, 1, keepdims=False)
        return away, here

    def product_halves(self, side, left, right, tile):
        if (left[0].shape[1] // self.count) % 8 == 0:
            return rows_product(side, left, [right], tile, self.count)
        return self.halves(rows_product(side, left, [right], tile, self.count, False)[0])

    def fold(self, here, come):
        return add_half(here, come, here.shape[0])

    def scatter_row(self, half):
        return lax.psum_scatter(
            half.reshape(-1, half.shape[2]),
            "fsdp",
            scatter_dimension=0,
            axis_index_groups=self.groups,
            tiled=True,
        )

    def scatter_direct(self, half):
        if not self.direct:
            return self.scatter_row(half).astype(f32)
        total = lax.dynamic_index_in_dim(half, self.high, 0, keepdims=False).astype(f32)
        for by in range(1, self.rows):
            z = lax.rem(self.high + by, self.rows)
            away = lax.dynamic_index_in_dim(half, z, 0, keepdims=False)
            total = total + self.shift(away, by).astype(f32)
        return total


def body(
    tokens,
    cotangent,
    positions,
    segment,
    query_weight,
    key_weight,
    value_weight,
    out_weight,
    gate_weight,
    up_weight,
    down_weight,
    gain_input,
    gain_query,
    gain_key,
    gain_mixed,
    gain_feed,
    gain_final,
    fsdp,
):
    owners = Owners(fsdp)
    me = lax.axis_index("seq")
    core = me & 1
    tok_rows, model = tokens.shape
    group_len = positions.shape[0]
    rows = query_weight.shape[0]
    head_width = key_weight.shape[1]
    hidden = gate_weight.shape[1]
    slab = hidden // fsdp
    part = slab // SEQ
    scale = head_width ** (-0.5)

    head_cols = lax.dynamic_slice_in_dim(query_weight, me * head_width, head_width, axis=1)
    key_or_value = jnp.where(core == 0, key_weight, value_weight)
    short = jnp.stack([gain_query, gain_key], axis=1)
    short = jnp.pad(short, ((0, rows - short.shape[0]), (0, 0)))
    gains_own = jnp.concatenate(
        [jnp.stack([gain_input, gain_mixed, gain_feed, gain_final], axis=1), short], axis=1
    )
    gains_own = jnp.pad(gains_own, ((0, 0), (0, 128 - gains_own.shape[1])))
    out_rows = out_weight.shape[0]
    out_part = out_rows // SEQ
    out_own = lax.dynamic_slice_in_dim(out_weight, me * out_part, out_part, axis=0)
    out_own = to_half(out_own)
    attn_own = jnp.concatenate(
        [to_half(head_cols), to_half(key_or_value), to_half(gains_own)], axis=1
    )
    packed = out_part if owners.direct and out_part % 16 == 0 else 0
    if packed:
        wide = attn_own.shape[1]
        rest = jnp.pad(out_own[:, wide:], ((0, 0), (0, 2 * wide - model)))
        pack_own = jnp.concatenate([attn_own, out_own[:, :wide], rest])
    else:
        pack_own = attn_own

    def columns(weight):
        return to_half(
            jnp.concatenate(
                [
                    lax.dynamic_slice_in_dim(weight, f * slab + me * part, part, axis=1)
                    for f in range(fsdp)
                ],
                axis=1,
            )
        )

    pieces, starts = owners.gather_pieces(pack_own)
    ahead = pieces[: (len(pieces) + 1) // 2]
    tokens_out = after(tokens, pack_own)
    token_blocks = [tokens, swap_seq(tokens_out, 1), swap_seq(tokens_out, 2)]
    token_blocks.append(swap_seq(after(token_blocks[2], *ahead), 1))
    gate_own = columns(after(gate_weight, token_blocks[2], *ahead))
    up_own = columns(after(up_weight, gate_own))
    down_own = lax.dynamic_slice_in_dim(after(down_weight, up_own), me * part, part, axis=0)
    down_own = to_half(down_own)

    def own_order(values):
        return jnp.concatenate(
            [
                lax.dynamic_slice_in_dim(values, (me ^ r) * tok_rows, tok_rows)
                for r in range(SEQ)
            ]
        )

    places = own_order(positions)
    kinds = own_order(segment)
    cosine, sine = rope_tables(places, head_width)
    second = kinds == 2
    code = jnp.where(second, -places, places).astype(f32)[None, :]
    low = jnp.where(second, -places, 0).astype(f32)[:, None]
    high = jnp.where(second, group_len // 2 - 1, places).astype(f32)[:, None]
    short_rows = head_width // fsdp

    meta = jnp.stack([core] + starts).astype(jnp.int32)
    normed16, queries, mine_kv, query_raw, kv_raw, w_own, out_flat, gains, head_gains = front(
        token_blocks, pieces, meta, cosine, sine, rows, short_rows, packed
    )
    gate_parts = owners.gather_wide(gate_own, queries)
    g_input = gains[0]
    other_kv = swap_seq(mine_kv, 1)
    *heads, probs = attend(meta, queries, mine_kv, other_kv, code, low, high, scale, 256)
    up_parts = owners.gather_wide(up_own, probs)
    w_down = owners.gather_pair_first(down_own)
    heads = [heads[0]] + [swap_seq(heads[r], r) for r in range(1, SEQ)]
    self_index = jnp.stack([me]).astype(jnp.int32)
    if packed:
        quarters = gather_seq(after(out_flat, probs))
    else:
        out_flat = lax.all_gather(out_own, "fsdp", axis=0, tiled=True)
        w_out = jnp.stack(natural(gather_seq(out_flat), me)).reshape(SEQ, fsdp, out_part, model)
        quarters = [w_out.transpose(1, 0, 2, 3).reshape(fsdp * out_rows, model)]
    heads[0] = after(heads[0], *gate_parts)
    heads16, w_out, attn, mixed, fed_own = mid(self_index, tokens, heads, quarters, gains, fsdp)
    inputs32 = tokens.astype(f32)

    side = jnp.stack([owners.low]).astype(jnp.int32)
    fed_blocks = [fed_own, swap_seq(fed_own, 1), swap_seq(fed_own, 2)]
    near_act, near_value, near_slope, w_gate, w_up = gate_up(
        side, fed_blocks[:2], gate_parts, up_parts
    )
    fed_two = after(fed_blocks[2], near_act)
    fed_blocks = fed_blocks[:2] + [fed_two, swap_seq(fed_two, 1)]
    far_act, far_value, far_slope, *_ = gate_up(side, fed_blocks[2:], [w_gate], [w_up])
    far_share = down(far_act, w_down, 2)
    near_act = after(near_act, *far_share)
    share = down(near_act, w_down, 2) + far_share
    share_pair = add_half(share[2], swap_seq(share[3], 1), 4)
    shares = [share[0], swap_seq(share[1], 1), swap_seq(share_pair, 2)]

    def feed_end(first, second, third, mixed, grad, gains):
        ffo = first.astype(f32) + second.astype(f32) + third.astype(f32)
        gain = gains[3:4]
        grad_ffo, terms = rms_back(ffo, gain, grad.astype(f32))
        return mixed + rms_scale(ffo, gain), grad_ffo, column_sum(terms)

    output, ffo_own, gain_final_part = fused(
        feed_end,
        [*shares, mixed, cotangent],
        [gains],
        [(tokens.shape, bf16), (tokens.shape, bf16)],
        4,
        [(1, model)],
    )

    ffo_blocks = [ffo_own, swap_seq(ffo_own, 1), swap_seq(ffo_own, 2)]
    near_gate, near_up, *near_share = back(
        ffo_blocks[:2], near_value, near_slope, w_down, w_gate, w_up
    )
    ffo_two = after(ffo_blocks[2], near_gate)
    ffo_blocks = ffo_blocks[:2] + [ffo_two, swap_seq(ffo_two, 1)]
    away_down, here_down = owners.product_halves(side, [near_act, far_act], ffo_blocks, 256)
    come_down = owners.swap(away_down)
    far_blocks = list(lax.optimization_barrier((away_down, *ffo_blocks[2:]))[1:])
    far_gate, far_up, *far_share = back(far_blocks, far_value, far_slope, w_down, w_gate, w_up)
    pair = add_half(far_share[0], swap_seq(far_share[1], 1), 4)
    far_sum = swap_seq(pair, 2)
    near_one = swap_seq(near_share[1], 1)
    fed_left = [after(fed_blocks[0], pair, near_one)] + fed_blocks[1:]
    away_gate, here_gate = owners.product_halves(side, fed_left, [near_gate, far_gate], 384)
    come_gate = owners.swap(away_gate)
    half_down = owners.fold(after(here_down, away_gate), come_down)
    grad_down = owners.scatter_row(half_down)
    fed_left = [after(fed_left[0], half_down)] + fed_left[1:]
    away_up, here_up = owners.product_halves(side, fed_left, [near_up, far_up], 384)
    come_up = owners.swap(away_up)
    shares = [after(near_share[0], away_up), near_one, far_sum]
    grad_mixed, grad_attn16, *grad_heads, gain_mixed_part = mid_back(
        self_index, shares, cotangent, mixed, attn, w_out, gains, 4
    )
    grad_heads = [grad_heads[0]] + [swap_seq(grad_heads[r], r) for r in range(1, SEQ)]

    half_gate = owners.fold(after(here_gate, *grad_heads), come_gate)
    grad_gate = owners.scatter_row(half_gate)
    grad_heads[0] = after(grad_heads[0], half_gate)
    grad_queries, keep_kv, send_kv = attend_back(
        meta, queries, mine_kv, other_kv, probs, grad_heads, scale, 256
    )
    come_kv = swap_seq(send_kv, 1)
    grad_qkv16, gain_query_part, gain_key_part, *normed_blocks = project_back(
        jnp.stack([core]).astype(jnp.int32),
        grad_queries,
        after(keep_kv, grad_down),
        come_kv,
        query_raw,
        kv_raw,
        cosine,
        sine,
        head_gains,
        w_own,
    )
    grad_normed = reduce_seq(normed_blocks)
    grad_proj = to_half(inner_rows(normed16, after(grad_qkv16, normed_blocks[0])))
    grad_out_share = to_half(inner_rows(heads16, after(grad_attn16, grad_proj)))
    grad_out_view = grad_out_share.reshape(fsdp, SEQ, out_part, model)
    grad_out_part = reduce_seq(
        [
            lax.dynamic_index_in_dim(grad_out_view, me ^ r, 1, keepdims=False)
            for r in range(SEQ)
        ]
    )
    extra = out_part * model // rows
    grad_out_part = to_half(grad_out_part).reshape(fsdp * rows, extra)

    short = jnp.stack([gain_query_part[0], gain_key_part[0]], axis=1).reshape(fsdp, short_rows, 2)
    short = jnp.pad(short, ((0, 0), (0, rows - short_rows), (0, 0))).reshape(model, 2)
    gain_parts = jnp.concatenate(
        [jnp.stack([gain_mixed_part[0], gain_final_part[0]], axis=1), short], axis=1
    )
    gain_parts = jnp.pad(gain_parts, ((0, 0), (0, 128 - gain_parts.shape[1])))
    half_up = owners.fold(after(here_up, grad_proj), come_up)
    grad_up = owners.scatter_row(half_up)
    downs = natural(gather_seq(grad_down), me)
    out_down = jnp.concatenate(downs).astype(f32)
    away_small, here_small = owners.halves(
        jnp.concatenate([grad_proj, to_half(gain_parts), grad_out_part], axis=1)
    )
    half_small = owners.fold(here_small, owners.swap(after(away_small, out_down, grad_gate)))
    grad_small = owners.scatter_direct(half_small)
    _, input_back = jax.vjp(lambda v: rms_scale(v, g_input), inputs32)
    (grad_input_part,) = input_back(grad_normed)
    grad_tokens = grad_mixed + grad_input_part

    gates = natural(gather_seq(grad_gate), me)
    ups = natural(gather_seq(grad_up), me)

    def spread(blocks):
        if fsdp <= 8:
            pieces = [
                blocks[t][:, f * part : (f + 1) * part]
                for f in range(fsdp)
                for t in range(SEQ)
            ]
            return jnp.concatenate(pieces, axis=1).astype(f32)
        stack = jnp.stack([b[:, : fsdp * part].reshape(rows, fsdp, part) for b in blocks], axis=2)
        return stack.reshape(rows, hidden).astype(f32)

    out_gate = spread(gates)
    out_up = spread(ups)

    feed_sum = jnp.sum(
        grad_gate.astype(f32) * gate_own.astype(f32)
        + grad_up.astype(f32) * up_own.astype(f32),
        axis=1,
    )
    input_sum = jnp.sum(
        grad_small[:, : 2 * head_width] * attn_own[:, : 2 * head_width].astype(f32), axis=1
    )
    tail = jnp.concatenate(
        [grad_small[:, 2 * head_width : 2 * head_width + 4], jnp.stack([input_sum, feed_sum], axis=1)],
        axis=1,
    )
    tail = jnp.pad(tail, ((0, 0), (0, 128 - tail.shape[1])))
    small = gather_seq(
        to_half(
            jnp.concatenate(
                [grad_small[:, : 2 * head_width], tail, grad_small[:, 2 * head_width + 128 :]], axis=1
            )
        )
    )
    outs = [b[:, 2 * head_width + 128 :].reshape(out_part, model) for b in natural(small, me)]
    out_out = jnp.concatenate(outs).astype(f32)
    out_query = jnp.concatenate([b[:, :head_width] for b in natural(small, me)], axis=1).astype(f32)
    kv = [b[:, head_width : 2 * head_width].astype(f32) for b in small]
    same, cross = kv[0] + kv[2], kv[1] + kv[3]
    out_key = jnp.where(core == 0, same, cross)
    out_value = jnp.where(core == 0, cross, same)
    tails = sum(b[:, 2 * head_width : 2 * head_width + 128].astype(f32) for b in small)
    own_gains = attn_own[:, 2 * head_width : 2 * head_width + 128].astype(f32)
    out_g_mixed = tails[:, 0]
    out_g_final = tails[:, 1]
    out_g_query = tails[:short_rows, 2]
    out_g_key = tails[:short_rows, 3]
    out_g_input = tails[:, 4] / own_gains[:, 0]
    out_g_feed = tails[:, 5] / own_gains[:, 2]
    return (
        output,
        grad_tokens,
        out_query,
        out_key,
        out_value,
        out_out,
        out_gate,
        out_up,
        out_down,
        out_g_input,
        out_g_query,
        out_g_key,
        out_g_mixed,
        out_g_feed,
        out_g_final,
    )


def solution(mesh):
    by_token = P(("fsdp", "seq"), None)
    by_row = P("fsdp", None)
    by_one = P("fsdp")
    return jax.shard_map(
        partial(body, fsdp=mesh.shape["fsdp"]),
        mesh=mesh,
        in_specs=(by_token,) * 2 + (by_one,) * 2 + (by_row,) * 7 + (by_one,) * 6,
        out_specs=(by_token,) * 2 + (by_row,) * 7 + (by_one,) * 6,
        check_vma=False,
    )
```

```python
from functools import partial

import jax
import jax.numpy as jnp
from jax import lax
from jax.experimental import pallas as pl
from jax.experimental.pallas import tpu as pltpu
from jax.sharding import PartitionSpec as P

epsilon = 1e-06
f32 = jnp.float32
bf16 = jnp.bfloat16
SEQ = 4


def rms_scale(values, gain):
    return values * lax.rsqrt(jnp.mean(values * values, axis=-1, keepdims=True) + epsilon) * gain


def rotate(values, cosine, sine):
    half_width = values.shape[-1] // 2
    first_half = values[..., :half_width]
    second_half = values[..., half_width:]
    return jnp.concatenate(
        [first_half * cosine - second_half * sine, second_half * cosine + first_half * sine],
        axis=-1,
    )


def rope_tables(places, width):
    half_width = width // 2
    inverse = 1.0 / 1000000.0 ** (jnp.arange(half_width, dtype=f32) * 2.0 / width)
    angles = places.astype(f32)[:, None] * inverse[None, :]
    return (jnp.cos(angles), jnp.sin(angles))


def head_norm(raw, gain, cosine, sine):
    return rotate(rms_scale(raw, gain), cosine, sine)


def mult(left, right):
    return jnp.dot(left, right, preferred_element_type=f32)


def inner_rows(left, right):
    return lax.dot_general(left, right, (((0,), (0,)), ((), ())), preferred_element_type=f32)


def outer_cols(left, right):
    return lax.dot_general(left, right, (((1,), (1,)), ((), ())), preferred_element_type=f32)


def to_half(values):
    return values.astype(bf16)


def gated(gate_in, up_in):
    return jax.nn.gelu(gate_in, approximate=True) * up_in


MIB = 2**20


def held(shape):
    return pl.BlockSpec(shape, lambda *at: (0,) * len(shape), pipeline_mode=pl.Buffered(1))


def call(kernel, grid, in_specs, out_specs, outs, flops, limit=60, scratch=(), exps=0, same=None):
    shapes = [jax.ShapeDtypeStruct(s, d) for s, d in outs]
    size = sum(o.size * o.dtype.itemsize for o in shapes)
    made = pl.pallas_call(
        kernel,
        grid=grid,
        in_specs=in_specs,
        out_specs=out_specs,
        out_shape=shapes,
        scratch_shapes=list(scratch),
        input_output_aliases=same or {},
        compiler_params=pltpu.CompilerParams(vmem_limit_bytes=limit * MIB),
        cost_estimate=pl.CostEstimate(
            flops=flops // 50, bytes_accessed=size // 50, transcendentals=exps // 50
        ),
    )
    return lambda *operands: list(made(*operands))


def fused_kernel(function, ins, outs, sums, *refs):
    results = function(*[ref[...] for ref in refs[:ins]])
    for ref, value in zip(refs[ins : ins + outs], results[:outs], strict=True):
        ref[...] = value.astype(ref.dtype)
    for ref, value in zip(refs[ins + outs :], results[outs:], strict=True):

        @pl.when(pl.program_id(0) == 0)
        def _():
            ref[...] = jnp.zeros_like(ref)

        ref[...] += value


def fused(function, by_row, whole, outs, steps, sums=()):
    def split(shape):
        return pl.BlockSpec(
            (shape[0] // steps, *shape[1:]), lambda i: (i, *(0 for _ in shape[1:]))
        )

    return call(
        partial(fused_kernel, function, len(by_row) + len(whole), len(outs), len(sums)),
        (steps,),
        [split(v.shape) for v in by_row] + [held(v.shape) for v in whole],
        [split(s) for s, _ in outs] + [pl.BlockSpec(s, lambda i: (0, 0)) for s in sums],
        [*outs, *((s, f32) for s in sums)],
        flops=0,
    )(*by_row, *whole)


def add_half(first, second, steps):
    function = lambda a, b: (a.astype(f32) + b.astype(f32),)
    return fused(function, [first, second], [], [(first.shape, bf16)], steps)[0]


def pair_sum(first, second):
    return to_half(first.astype(f32) + second.astype(f32))


def rms_back(values, gain, grad):
    r = lax.rsqrt(jnp.mean(values * values, axis=-1, keepdims=True) + epsilon)
    scaled = grad * gain
    mean = jnp.mean(values * scaled, axis=-1, keepdims=True)
    return r * scaled - values * (r * r * r * mean), grad * values * r


def column_sum(values):
    return jnp.sum(values, axis=0, keepdims=True)


def mid_kernel(owners, quarters, me_ref, x_ref, *refs):
    heads = refs[:SEQ]
    weights = refs[SEQ : SEQ + quarters]
    gains_ref, all_ref, w_ref, attn_ref, mixed_ref, fed_ref = refs[SEQ + quarters :]
    width = heads[0].shape[1]
    for r, head in enumerate(heads):
        start = pl.multiple_of(jnp.bitwise_xor(me_ref[0], r) * width, 128)
        all_ref[:, pl.ds(start, width)] = head[...]
    if quarters == 1:
        w_ref[...] = weights[0][...]
    else:
        for r, weight in enumerate(weights):
            size = weight.shape[0] // owners
            for f in range(owners):
                start = (f * SEQ + jnp.bitwise_xor(me_ref[0], r)) * size
                start = pl.multiple_of(start, 16)
                w_ref[pl.ds(start, size), :] = weight[f * size : (f + 1) * size, :]
    attn = mult(all_ref[...], w_ref[...])
    attn_ref[...] = attn
    mixed = x_ref[...].astype(f32) + rms_scale(attn, gains_ref[1:2, :])
    mixed_ref[...] = mixed
    fed_ref[...] = to_half(rms_scale(mixed, gains_ref[2:3, :]))


def mid(me, tokens, heads, weights, gains, owners):
    rows, model = tokens.shape
    width = heads[0].shape[1] * SEQ
    specs = [held(v.shape) for v in [tokens, *heads, *weights, gains]]
    outs = [
        ((rows, width), bf16),
        ((width, model), bf16),
        ((rows, model), f32),
        ((rows, model), f32),
        ((rows, model), bf16),
    ]
    return call(
        partial(mid_kernel, owners, len(weights)),
        (1,),
        [pl.BlockSpec(memory_space=pltpu.SMEM)] + specs,
        [pl.BlockSpec(s, lambda i: (0, 0)) for s, _ in outs],
        outs,
        flops=2 * rows * width * model,
    )(me, tokens, *heads, *weights, gains)


def mid_back_kernel(me_ref, a_ref, b_ref, c_ref, dy_ref, mixed_ref, attn_ref, w_ref, gains_ref, *refs):
    grad_ref, grad_attn_ref = refs[:2]
    outs, sum_ref, heads_ref = refs[2 : 2 + SEQ], refs[2 + SEQ], refs[3 + SEQ]
    grad_fed = a_ref[...].astype(f32) + b_ref[...].astype(f32) + c_ref[...].astype(f32)
    part, _ = rms_back(mixed_ref[...], gains_ref[2:3, :], grad_fed)
    grad_mixed = dy_ref[...].astype(f32) + part
    grad_ref[...] = grad_mixed
    grad_attn, terms = rms_back(attn_ref[...], gains_ref[1:2, :], grad_mixed)
    half = to_half(grad_attn)
    grad_attn_ref[...] = half
    heads_ref[...] = to_half(outer_cols(half, w_ref[...]))
    width = outs[0].shape[1]
    for r, out in enumerate(outs):
        start = pl.multiple_of(jnp.bitwise_xor(me_ref[0], r) * width, 128)
        out[...] = heads_ref[:, pl.ds(start, width)]

    @pl.when(pl.program_id(0) == 0)
    def _():
        sum_ref[...] = jnp.zeros_like(sum_ref)

    sum_ref[...] += column_sum(terms)


def mid_back(me, shares, cotangent, mixed, attn, w_out, gains, steps):
    rows, model = mixed.shape
    total = w_out.shape[0]
    by_row = [*shares, cotangent, mixed, attn]
    row = lambda width: pl.BlockSpec((rows // steps, width), lambda i: (i, 0))
    outs = [((rows, model), f32), ((rows, model), bf16)]
    outs += [((rows, total // SEQ), bf16)] * SEQ
    return call(
        mid_back_kernel,
        (steps,),
        [pl.BlockSpec(memory_space=pltpu.SMEM)]
        + [row(model) for _ in by_row]
        + [held(w_out.shape), held(gains.shape)],
        [row(s[1]) for s, _ in outs] + [pl.BlockSpec((1, model), lambda i: (0, 0))],
        [*outs, ((1, model), f32)],
        flops=2 * rows * model * total,
        scratch=[pltpu.VMEM((rows // steps, total), bf16)],
    )(me, *by_row, w_out, gains)


def turn_back(grad, cosine, sine):
    half = grad.shape[-1] // 2
    a, b = grad[:, :half], grad[:, half:]
    return jnp.concatenate([a * cosine + b * sine, b * cosine - a * sine], axis=-1)


def project_back_kernel(core_ref, *refs):
    dq_ref, keep_ref, come_ref, q_raw_ref, kv_raw_ref, cos_ref, sin_ref, gains_ref, w_ref = refs[:9]
    grad_ref, q_sum_ref, k_sum_ref = refs[9:12]
    outs = refs[12:]
    cosine, sine = cos_ref[...], sin_ref[...]
    head = dq_ref.shape[1]
    first = core_ref[0] == 0
    grad_q, q_terms = rms_back(
        q_raw_ref[...], gains_ref[4:5, :], turn_back(dq_ref[...], cosine, sine)
    )
    grad_kv = keep_ref[...] + come_ref[...].astype(f32)
    grad_k, k_terms = rms_back(
        kv_raw_ref[...], gains_ref[5:6, :], turn_back(grad_kv, cosine, sine)
    )
    grad_ref[:, :head] = to_half(grad_q)
    grad_ref[:, head:] = to_half(jnp.where(first, grad_k, grad_kv))
    share = to_half(outer_cols(grad_ref[...], w_ref[...]))
    for r, out in enumerate(outs):

        @pl.when(pl.program_id(0) == r)
        def _():
            out[...] = share

    @pl.when(pl.program_id(0) == 0)
    def _():
        q_sum_ref[...] = jnp.zeros_like(q_sum_ref)
        k_sum_ref[...] = jnp.zeros_like(k_sum_ref)

    q_sum_ref[...] += column_sum(q_terms)
    k_sum_ref[...] += jnp.where(first, column_sum(k_terms), 0.0)


def project_back(core, dq, keep, come, q_raw, kv_raw, cosine, sine, head_gains, w_own):
    rows, head = dq.shape
    model = w_own.shape[0]
    block = rows // SEQ
    by_row = [dq, keep, come, q_raw, kv_raw, cosine, sine]
    row = lambda width: pl.BlockSpec((block, width), lambda i: (i, 0))
    fixed = lambda shape: pl.BlockSpec(shape, lambda i: (0, 0))
    return call(
        project_back_kernel,
        (SEQ,),
        [pl.BlockSpec(memory_space=pltpu.SMEM)]
        + [row(v.shape[1]) for v in by_row]
        + [held(head_gains.shape), held(w_own.shape)],
        [row(2 * head), fixed((1, head)), fixed((1, head))] + [fixed((block, model))] * SEQ,
        [((rows, 2 * head), bf16), ((1, head), f32), ((1, head), f32)]
        + [((block, model), bf16)] * SEQ,
        flops=4 * rows * head * model,
    )(core, *by_row, head_gains, w_own)


def front_kernel(count, rows, short, packed, meta_ref, *refs):
    tokens = refs[:SEQ]
    pieces = refs[SEQ : SEQ + count]
    cos_ref, sin_ref = refs[SEQ + count : SEQ + count + 2]
    normed_ref, q_ref, kv_ref, q_raw_ref, kv_raw_ref, w_ref, out_ref, gains_ref, head_gains_ref = (
        refs[SEQ + count + 2 : -2]
    )
    x_ref, columns_ref = refs[-2:]
    at = pl.program_id(0)
    head = q_ref.shape[1]

    @pl.when(at == 0)
    def _():
        for j, piece in enumerate(pieces):
            size = piece.shape[0] - 2 * packed
            start = pl.multiple_of(meta_ref[1 + j] * rows, 16)
            w_ref[pl.ds(start, size), :] = piece[:size, : 2 * head]
            columns_ref[pl.ds(start, size), :] = piece[:size, 2 * head :].astype(f32)
            if packed:
                start = pl.multiple_of(meta_ref[1 + j] * packed, 16)
                wide = piece.shape[1]
                rest = out_ref.shape[1] - wide
                out_ref[pl.ds(start, packed), :wide] = piece[size : size + packed, :]
                out_ref[pl.ds(start, packed), wide:] = piece[size + packed :, :rest]
        gains = columns_ref[...].T[:8]
        gains_ref[...] = gains
        model = gains.shape[1]
        from_row = lax.broadcasted_iota(jnp.int32, (model, head), 0)
        to_col = lax.broadcasted_iota(jnp.int32, (model, head), 1)
        owner = to_col >> (short.bit_length() - 1)
        wanted = owner * rows + (to_col & (short - 1))
        pick = jnp.where(from_row == wanted, 1.0, 0.0)
        head_gains_ref[...] = mult(to_half(gains), to_half(pick))

    for r in range(SEQ):

        @pl.when(at == r)
        def _():
            x_ref[...] = tokens[r][...].astype(f32)

    values = x_ref[...]
    normed = to_half(rms_scale(values, gains_ref[0:1, :]))
    normed_ref[...] = normed
    raw = mult(normed, w_ref[...])
    q_raw = raw[:, :head]
    kv_raw = raw[:, head:]
    q_raw_ref[...] = q_raw
    kv_raw_ref[...] = kv_raw
    cosine, sine = cos_ref[...], sin_ref[...]
    q_ref[...] = to_half(head_norm(q_raw, head_gains_ref[4:5, :], cosine, sine))
    keyed = head_norm(kv_raw, head_gains_ref[5:6, :], cosine, sine)
    kv_ref[...] = to_half(jnp.where(meta_ref[0] == 0, keyed, kv_raw))


def front(tokens, pieces, meta, cosine, sine, rows, short, packed):
    block, model = tokens[0].shape
    head = 2 * cosine.shape[1]
    total = block * SEQ
    out_shape = (max(8, packed * len(pieces)), model)
    slab = lambda width: pl.BlockSpec((block, width), lambda i: (i, 0))
    fixed = lambda shape: pl.BlockSpec(shape, lambda i: (0, 0))
    return call(
        partial(front_kernel, len(pieces), rows, short, packed),
        (SEQ,),
        [pl.BlockSpec(memory_space=pltpu.SMEM)]
        + [held(t.shape) for t in tokens]
        + [held(p.shape) for p in pieces]
        + [slab(head // 2)] * 2,
        [slab(model), slab(head), slab(head), slab(head), slab(head)]
        + [fixed((model, 2 * head)), fixed(out_shape), fixed((8, model)), fixed((8, head))],
        [
            ((total, model), bf16),
            ((total, head), bf16),
            ((total, head), bf16),
            ((total, head), f32),
            ((total, head), f32),
            ((model, 2 * head), bf16),
            (out_shape, bf16),
            ((8, model), f32),
            ((8, head), f32),
        ],
        flops=4 * total * model * head,
        scratch=[
            pltpu.VMEM((block, model), f32),
            pltpu.VMEM((model, 128), f32),
        ],
    )(meta, *tokens, *pieces, cosine, sine)


def twins(values):
    size = values.shape[0] // SEQ
    return jnp.concatenate([values[(r ^ 1) * size : (r ^ 1) * size + size] for r in range(SEQ)])


def split_pair(meta_ref, mine_ref, other_ref, keys_ref, values_ref):
    mine, other = mine_ref[...], twins(other_ref[...])
    first = meta_ref[0] == 0

    @pl.when(first)
    def _():
        keys_ref[...] = mine
        values_ref[...] = other

    @pl.when(jnp.logical_not(first))
    def _():
        keys_ref[...] = other
        values_ref[...] = mine


def attend_kernel(
    scale, meta_ref, q_ref, mine_ref, other_ref, code_ref, low_ref, high_ref, *refs
):
    outs, (probs_ref, keys_ref, values_ref) = refs[:SEQ], refs[SEQ:]
    at = pl.program_id(0)

    @pl.when(at == 0)
    def _():
        split_pair(meta_ref, mine_ref, other_ref, keys_ref, values_ref)

    scores = outer_cols(q_ref[...], keys_ref[...])
    code = code_ref[...]
    seen = (code >= low_ref[...]) & (code <= high_ref[...])
    expd = jnp.where(seen, jnp.exp2(scores * (scale * 1.4426950408889634)), 0.0)
    total = jnp.sum(expd, axis=1, keepdims=True)
    probs = to_half(expd * (1.0 / total))
    probs_ref[...] = probs
    out = to_half(mult(probs, values_ref[...]))
    block = out.shape[0]
    steps = outs[0].shape[0] // block
    for r in range(SEQ):
        for s in range(steps):

            @pl.when(at == r * steps + s)
            def _():
                outs[r][s * block : (s + 1) * block, :] = out


def attend(meta, queries, mine, other, code, low, high, scale, block):
    rows, width = queries.shape
    count = mine.shape[0]
    slab = pl.BlockSpec((block, width), lambda i: (i, 0))
    thin = pl.BlockSpec((block, 1), lambda i: (i, 0))
    part = pl.BlockSpec((rows // SEQ, width), lambda i: (0, 0))
    return call(
        partial(attend_kernel, scale),
        (rows // block,),
        [pl.BlockSpec(memory_space=pltpu.SMEM), slab, held(mine.shape), held(mine.shape)]
        + [pl.BlockSpec((1, count), lambda i: (0, 0)), thin, thin],
        [part] * SEQ + [pl.BlockSpec((block, count), lambda i: (i, 0))],
        [((rows // SEQ, width), bf16)] * SEQ + [((rows, count), bf16)],
        flops=4 * rows * count * width,
        exps=rows * count,
        scratch=[pltpu.VMEM((count, width), bf16)] * 2,
    )(meta, queries, mine, other, code, low, high)


def attend_back_kernel(scale, meta_ref, q_ref, mine_ref, other_ref, p_ref, *refs):
    grads_in = refs[:SEQ]
    dq_ref, keep_ref, send_ref, keys_ref, values_ref, dk_ref, dv_ref, g_ref = refs[SEQ:]
    at = pl.program_id(0)

    @pl.when(at == 0)
    def _():
        split_pair(meta_ref, mine_ref, other_ref, keys_ref, values_ref)
        dk_ref[...] = jnp.zeros_like(dk_ref)
        dv_ref[...] = jnp.zeros_like(dv_ref)

    block = g_ref.shape[0]
    steps = grads_in[0].shape[0] // block
    for r in range(SEQ):
        for s in range(steps):

            @pl.when(at == r * steps + s)
            def _():
                g_ref[...] = grads_in[r][s * block : (s + 1) * block, :]

    probs = p_ref[...]
    grads = g_ref[...]
    wide = probs.astype(f32)
    grad_probs = outer_cols(grads, values_ref[...])
    centre = jnp.sum(wide * grad_probs, axis=1, keepdims=True)
    grad_scores = to_half(wide * (grad_probs - centre))
    dq_ref[...] = scale * mult(grad_scores, keys_ref[...])
    dk_ref[...] += scale * inner_rows(grad_scores, q_ref[...])
    dv_ref[...] += inner_rows(probs, grads)

    @pl.when(at == pl.num_programs(0) - 1)
    def _():
        first = meta_ref[0] == 0
        keep_ref[...] = jnp.where(first, dk_ref[...], dv_ref[...])
        send_ref[...] = twins(to_half(jnp.where(first, dv_ref[...], dk_ref[...])))


def attend_back(meta, queries, mine, other, probs, grads, scale, block):
    rows, width = queries.shape
    count = mine.shape[0]
    whole = pl.BlockSpec((count, width), lambda i: (0, 0))
    slab = pl.BlockSpec((block, width), lambda i: (i, 0))
    return call(
        partial(attend_back_kernel, scale),
        (rows // block,),
        [pl.BlockSpec(memory_space=pltpu.SMEM), slab, held(mine.shape), held(mine.shape)]
        + [pl.BlockSpec((block, count), lambda i: (i, 0))]
        + [held(g.shape) for g in grads],
        [slab, whole, whole],
        [((rows, width), f32), ((count, width), f32), ((count, width), bf16)],
        flops=8 * rows * count * width,
        scratch=[pltpu.VMEM((count, width), bf16)] * 2
        + [pltpu.VMEM((count, width), f32)] * 2
        + [pltpu.VMEM((block, width), bf16)],
    )(meta, queries, mine, other, probs, *grads)


def spread_kernel(owners, me_ref, *refs):
    blocks, out_ref, all_ref = refs[:SEQ], refs[SEQ], refs[SEQ + 1]
    for r, block in enumerate(blocks):
        all_ref[jnp.bitwise_xor(me_ref[0], r)] = block[...].astype(f32)
    part = blocks[0].shape[1] // owners
    out_ref[...] = jnp.concatenate(
        [all_ref[t][:, f * part : (f + 1) * part] for f in range(owners) for t in range(SEQ)],
        axis=1,
    )


def spread_columns(me, blocks, owners):
    rows, width = blocks[0].shape
    steps = 3 if rows % 48 == 0 else 1
    step = rows // steps
    row = lambda w: pl.BlockSpec((step, w), lambda i: (i, 0))
    return call(
        partial(spread_kernel, owners),
        (steps,),
        [pl.BlockSpec(memory_space=pltpu.SMEM)] + [row(width)] * SEQ,
        [row(SEQ * width)],
        [((rows, SEQ * width), f32)],
        flops=0,
        scratch=[pltpu.VMEM((SEQ, step, width), f32)],
    )(me, *blocks)[0]


def pick_block(blocks, into_ref):
    for r, block in enumerate(blocks):

        @pl.when(pl.program_id(0) == r)
        def _():
            into_ref[...] = block[...]


def feed_rows(x_ref, gate_ref, up_ref, act_ref, value_ref, slope_ref):
    rows = x_ref[...]
    gate = mult(rows, gate_ref[...])
    upper = mult(rows, up_ref[...])
    c = 0.7978845608028654
    square = gate * gate
    bend = jnp.tanh(gate * (c + (c * 0.044715) * square))
    half = 0.5 + 0.5 * bend
    value = gate * half
    slope = half + (0.5 * gate) * (1.0 - bend * bend) * (c + (3 * c * 0.044715) * square)
    act_ref[...] = to_half(value * upper)
    value_ref[...] = to_half(value)
    slope_ref[...] = to_half(slope * upper)


def gate_up_kernel(count, pieces, kept, meta_ref, *refs):
    parts, outs = refs[count : count + 2 * pieces], refs[count + 2 * pieces + kept :]
    act_ref, value_ref, slope_ref = outs[:3]
    x_ref = outs[-1]
    gate_ref, up_ref = outs[3:5] if pieces == 2 else parts

    if pieces == 2:

        @pl.when(pl.program_id(0) == 0)
        def _():
            for w_ref, own in ((gate_ref, parts[:2]), (up_ref, parts[2:])):
                for half, ref in enumerate(own):
                    size = ref.shape[1]
                    for z in range(ref.shape[0]):
                        start = (2 * z + jnp.bitwise_xor(meta_ref[0], half)) * size
                        w_ref[pl.ds(pl.multiple_of(start, 16), size), :] = ref[z]

    pick_block(refs[:count], x_ref)
    feed_rows(x_ref, gate_ref, up_ref, act_ref, value_ref, slope_ref)


def gate_up(meta, blocks, gate_parts, up_parts, first, saved):
    block, model = blocks[0].shape
    width = gate_parts[0].shape[-1]
    total = block * SEQ
    slab = pl.BlockSpec((block, width), lambda i: (i + first, 0))
    whole = pl.BlockSpec((model, width), lambda i: (0, 0))
    parts = [*gate_parts, *up_parts]
    made = len(parts) - 2
    ins = 1 + len(blocks) + len(parts)
    out = call(
        partial(gate_up_kernel, len(blocks), len(gate_parts), len(saved)),
        (len(blocks),),
        [pl.BlockSpec(memory_space=pltpu.SMEM)]
        + [held(b.shape) for b in [*blocks, *parts]]
        + [pl.BlockSpec(memory_space=pl.ANY)] * len(saved),
        [slab] * 3 + [whole] * made,
        [((total, width), bf16)] * 3 + [((model, width), bf16)] * made,
        flops=4 * total * model * width,
        exps=total * width,
        scratch=[pltpu.VMEM((block, model), bf16)],
        limit=62,
        same={ins + i: i for i in range(len(saved))},
    )(meta, *blocks, *parts, *saved)
    return out if made else out + parts


def feed_kernel(x_ref, gate_ref, up_ref, down_ref, *refs):
    act_ref, value_ref, slope_ref, out_ref = refs[3:]
    feed_rows(x_ref, gate_ref, up_ref, act_ref, value_ref, slope_ref)
    out_ref[...] = to_half(mult(act_ref[...], down_ref[...]))


def feed_first(rows, w_gate, w_up, w_down, saved):
    block, model = rows.shape
    width = w_gate.shape[1]
    slab = pl.BlockSpec((block, width), lambda i: (0, 0))
    return call(
        feed_kernel,
        (1,),
        [held(v.shape) for v in [rows, w_gate, w_up, w_down]]
        + [pl.BlockSpec(memory_space=pl.ANY)] * 3,
        [slab] * 3 + [pl.BlockSpec((block, model), lambda i: (0, 0))],
        [(v.shape, bf16) for v in saved] + [((block, model), bf16)],
        flops=6 * block * model * width,
        limit=62,
        same={4: 0, 5: 1, 6: 2},
    )(rows, w_gate, w_up, w_down, *saved)


def down_kernel(x_ref, w_ref, *outs):
    out = to_half(mult(x_ref[...], w_ref[...]))
    for r, ref in enumerate(outs):

        @pl.when(pl.program_id(0) == r)
        def _():
            ref[...] = out


def down(rows, w_down, count):
    block = rows.shape[0] // (count + 1)
    width, model = w_down.shape
    out = pl.BlockSpec((block, model), lambda i: (0, 0))
    return call(
        down_kernel,
        (count,),
        [pl.BlockSpec((block, width), lambda i: (i + 1, 0)), held(w_down.shape)],
        [out] * count,
        [((block, model), bf16)] * count,
        flops=2 * count * block * model * width,
    )(rows, w_down)


def back_kernel(count, *refs):
    y_refs = refs[:count]
    value_ref, slope_ref, down_ref, gate_ref, up_ref, dg_ref, du_ref = refs[count : count + 7]
    outs, y_ref = refs[count + 7 : -1], refs[-1]
    pick_block(y_refs, y_ref)
    grad_act = outer_cols(y_ref[...], down_ref[...])
    dg_ref[...] = to_half(grad_act * slope_ref[...].astype(f32))
    du_ref[...] = to_half(grad_act * value_ref[...].astype(f32))
    out = to_half(outer_cols(dg_ref[...], gate_ref[...]) + outer_cols(du_ref[...], up_ref[...]))
    for r, ref in enumerate(outs):

        @pl.when(pl.program_id(0) == r)
        def _():
            ref[...] = out


def back(blocks, value, slope, w_down, w_gate, w_up, first):
    block, model = blocks[0].shape
    count = len(blocks)
    width = w_gate.shape[1]
    ahead = pl.BlockSpec((block, width), lambda i: (i + first, 0))
    slab = pl.BlockSpec((block, width), lambda i: (i, 0))
    out = pl.BlockSpec((block, model), lambda i: (0, 0))
    return call(
        partial(back_kernel, count),
        (count,),
        [held(b.shape) for b in blocks]
        + [ahead, ahead, held(w_down.shape), held(w_gate.shape), held(w_up.shape)],
        [slab, slab] + [out] * count,
        [((block * count, width), bf16)] * 2 + [((block, model), bf16)] * count,
        flops=6 * count * block * model * width,
        scratch=[pltpu.VMEM((block, model), bf16)],
    )(*blocks, value, slope, w_down, w_gate, w_up)


def cut_rows(blocks, many):
    each = many // len(blocks)
    size = blocks[0].shape[0] // each
    return [b[r * size : (r + 1) * size] for b in blocks for r in range(each)]


def rows_sum(left, right):
    total = inner_rows(left[0], right[0])
    for a, b in zip(left[1:], right[1:], strict=True):
        total = total + inner_rows(a, b)
    return total


def rows_kernel(counts, many, meta_ref, *refs):
    total_in = sum(counts)
    results = len(counts) - 1
    values = [ref[...] for ref in refs[:total_in]]
    left = cut_rows(values[: counts[0]], many)
    at = counts[0]
    totals = []
    for count in counts[1:]:
        totals.append(rows_sum(left, cut_rows(values[at : at + count], many)))
        at += count
    if len(refs) == total_in + results:
        for ref, total in zip(refs[total_in:], totals, strict=True):
            ref[...] = to_half(total)
        return
    outs, sums = refs[total_in : total_in + 2 * results], refs[total_in + 2 * results :]
    tile = left[0].shape[1]
    here = pl.ds(pl.multiple_of(pl.program_id(0) * tile, 128), tile)
    for ref, total in zip(sums, totals, strict=True):
        ref[here, :] = total

    @pl.when(pl.program_id(0) == pl.num_programs(0) - 1)
    def _():
        for o in range(results):
            for half, ref in enumerate(outs[2 * o : 2 * o + 2]):
                size = ref.shape[1]
                for z in range(ref.shape[0]):
                    start = (2 * z + jnp.bitwise_xor(meta_ref[0], 1 - half)) * size
                    ref[z] = to_half(sums[o][pl.ds(pl.multiple_of(start, 8), size), :])


def rows_product(meta, left, rights, tile, owners, cut=True):
    counts = [len(v) for v in [left, *rights]]
    many = max(counts)
    height = left[0].shape[1]
    widths = [r[0].shape[1] for r in rights]
    flat = [v for r in rights for v in r]
    steps = pl.cdiv(height, tile)
    shape = lambda w: (owners // 2, height // owners, w)
    if cut:
        specs = [pl.BlockSpec(shape(w), lambda i: (0, 0, 0)) for w in widths for _ in range(2)]
        outs = [(shape(w), bf16) for w in widths for _ in range(2)]
    else:
        specs = [pl.BlockSpec((tile, w), lambda i: (i, 0)) for w in widths]
        outs = [((height, w), bf16) for w in widths]
    return call(
        partial(rows_kernel, counts, many),
        (steps,),
        [pl.BlockSpec(memory_space=pltpu.SMEM)]
        + [pl.BlockSpec((v.shape[0], tile), lambda i: (0, i)) for v in left]
        + [held(v.shape) for v in flat],
        specs,
        outs,
        flops=2 * sum(v.shape[0] for v in left) * height * sum(widths),
        scratch=[pltpu.VMEM((steps * tile, w), f32) for w in widths] if cut else [],
        limit=62,
    )(meta, *left, *flat)


def after(value, *others):
    return lax.optimization_barrier((value, others))[0]


def swap_seq(values, bits):
    return lax.ppermute(values, "seq", [(i, i ^ bits) for i in range(SEQ)])


def gather_seq(own):
    one = swap_seq(own, 1)
    two = swap_seq(own, 2)
    return [own, one, two, swap_seq(two, 1)]


def natural(blocks, me):
    stack = jnp.stack(blocks)
    return [lax.dynamic_index_in_dim(stack, me ^ j, 0, keepdims=False) for j in range(SEQ)]


def reduce_seq(blocks):
    three = swap_seq(blocks[3], 1)
    pair = to_half(blocks[2].astype(f32) + three.astype(f32))
    two = swap_seq(pair, 2)
    one = swap_seq(blocks[1], 1)
    return blocks[0].astype(f32) + one.astype(f32) + two.astype(f32)


class Owners:
    def __init__(self, count):
        self.count = count
        self.rows = count // 2
        self.groups = [[2 * z + y for z in range(self.rows)] for y in range(2)]
        index = lax.axis_index("fsdp")
        self.low = index % 2
        self.high = index // 2
        self.direct = self.rows <= 4

    def swap(self, values):
        return lax.ppermute(values, "fsdp", [(i, i ^ 1) for i in range(self.count)])

    def shift(self, values, by):
        return lax.ppermute(
            values, "fsdp", [(i, (i + 2 * by) % self.count) for i in range(self.count)]
        )

    def gather_row(self, values):
        return lax.all_gather(values, "fsdp", axis=0, tiled=True, axis_index_groups=self.groups)

    def pair(self, mine, other, axis):
        first = jnp.where(self.low == 0, mine, other)
        second = jnp.where(self.low == 0, other, mine)
        return jnp.stack([first, second], axis=axis)

    def gather_pieces(self, own):
        if not self.direct:
            return [lax.all_gather(own, "fsdp", axis=0, tiled=True)], [jnp.int32(0)]
        far = [own] + [self.shift(own, by) for by in range(1, self.rows)]
        near = [self.swap(p) for p in far]
        starts = [lax.rem(self.high - by + self.rows, self.rows) * 2 for by in range(self.rows)]
        places = [s + self.low for s in starts] + [s + 1 - self.low for s in starts]
        return far + near, places

    def gather_wide(self, own, later):
        if not self.direct:
            return [lax.all_gather(own, "fsdp", axis=0, tiled=True)]
        size, width = own.shape
        mine = after(self.gather_row(own), later).reshape(self.rows, size, width)
        return [mine, self.swap(mine)]

    def gather_pair_first(self, own):
        size, width = own.shape
        both = self.pair(own, self.swap(own), 0).reshape(2 * size, width)
        return self.gather_row(both)

    def halves(self, whole):
        size = whole.shape[0] // self.count
        view = whole.reshape(self.rows, 2, size, whole.shape[1])
        away = lax.dynamic_index_in_dim(view, 1 - self.low, 1, keepdims=False)
        here = lax.dynamic_index_in_dim(view, self.low, 1, keepdims=False)
        return away, here

    def product_halves(self, side, left, rights, tile):
        if (left[0].shape[1] // self.count) % 8 == 0:
            return rows_product(side, left, rights, tile, self.count)
        whole = rows_product(side, left, rights, tile, self.count, False)
        return [half for value in whole for half in self.halves(value)]

    def fold(self, here, come):
        return add_half(here, come, here.shape[0])

    def scatter_row(self, half):
        return lax.psum_scatter(
            half.reshape(-1, half.shape[2]),
            "fsdp",
            scatter_dimension=0,
            axis_index_groups=self.groups,
            tiled=True,
        )

    def scatter_direct(self, half):
        if not self.direct:
            return self.scatter_row(half).astype(f32)
        total = lax.dynamic_index_in_dim(half, self.high, 0, keepdims=False).astype(f32)
        for by in range(1, self.rows):
            z = lax.rem(self.high + by, self.rows)
            away = lax.dynamic_index_in_dim(half, z, 0, keepdims=False)
            total = total + self.shift(away, by).astype(f32)
        return total


def body(
    tokens,
    cotangent,
    positions,
    segment,
    query_weight,
    key_weight,
    value_weight,
    out_weight,
    gate_weight,
    up_weight,
    down_weight,
    gain_input,
    gain_query,
    gain_key,
    gain_mixed,
    gain_feed,
    gain_final,
    fsdp,
):
    owners = Owners(fsdp)
    me = lax.axis_index("seq")
    core = me & 1
    tok_rows, model = tokens.shape
    group_len = positions.shape[0]
    rows = query_weight.shape[0]
    head_width = key_weight.shape[1]
    hidden = gate_weight.shape[1]
    slab = hidden // fsdp
    part = slab // SEQ
    scale = head_width ** (-0.5)

    head_cols = lax.dynamic_slice_in_dim(query_weight, me * head_width, head_width, axis=1)
    key_or_value = jnp.where(core == 0, key_weight, value_weight)
    short = jnp.stack([gain_query, gain_key], axis=1)
    short = jnp.pad(short, ((0, rows - short.shape[0]), (0, 0)))
    gains_own = jnp.concatenate(
        [jnp.stack([gain_input, gain_mixed, gain_feed, gain_final], axis=1), short], axis=1
    )
    gains_own = jnp.pad(gains_own, ((0, 0), (0, 128 - gains_own.shape[1])))
    out_rows = out_weight.shape[0]
    out_part = out_rows // SEQ
    out_own = lax.dynamic_slice_in_dim(out_weight, me * out_part, out_part, axis=0)
    out_own = to_half(out_own)
    attn_own = jnp.concatenate(
        [to_half(head_cols), to_half(key_or_value), to_half(gains_own)], axis=1
    )
    packed = out_part if owners.direct and out_part % 16 == 0 else 0
    if packed:
        wide = attn_own.shape[1]
        rest = jnp.pad(out_own[:, wide:], ((0, 0), (0, 2 * wide - model)))
        pack_own = jnp.concatenate([attn_own, out_own[:, :wide], rest])
    else:
        pack_own = attn_own

    def columns(weight):
        return to_half(
            jnp.concatenate(
                [
                    lax.dynamic_slice_in_dim(weight, f * slab + me * part, part, axis=1)
                    for f in range(fsdp)
                ],
                axis=1,
            )
        )

    pieces, starts = owners.gather_pieces(pack_own)
    ahead = pieces[: (len(pieces) + 1) // 2]
    tokens_out = after(tokens, pack_own)
    token_blocks = [tokens, swap_seq(tokens_out, 1), swap_seq(tokens_out, 2)]
    token_blocks.append(swap_seq(after(token_blocks[2], *ahead), 1))
    gate_own = columns(after(gate_weight, token_blocks[2], *ahead))
    up_own = columns(after(up_weight, gate_own))
    down_own = lax.dynamic_slice_in_dim(after(down_weight, up_own), me * part, part, axis=0)
    down_own = to_half(down_own)

    def own_order(values):
        return jnp.concatenate(
            [
                lax.dynamic_slice_in_dim(values, (me ^ r) * tok_rows, tok_rows)
                for r in range(SEQ)
            ]
        )

    places = own_order(positions)
    kinds = own_order(segment)
    cosine, sine = rope_tables(places, head_width)
    second = kinds == 2
    code = jnp.where(second, -places, places).astype(f32)[None, :]
    low = jnp.where(second, -places, 0).astype(f32)[:, None]
    high = jnp.where(second, group_len // 2 - 1, places).astype(f32)[:, None]
    short_rows = head_width // fsdp

    meta = jnp.stack([core] + starts).astype(jnp.int32)
    normed16, queries, mine_kv, query_raw, kv_raw, w_own, out_flat, gains, head_gains = front(
        token_blocks, pieces, meta, cosine, sine, rows, short_rows, packed
    )
    gate_parts = owners.gather_wide(gate_own, queries)
    other_kv = swap_seq(mine_kv, 1)
    *heads, probs = attend(meta, queries, mine_kv, other_kv, code, low, high, scale, 256)
    up_parts = owners.gather_wide(up_own, probs)
    w_down = owners.gather_pair_first(down_own)
    heads = [heads[0]] + [swap_seq(heads[r], r) for r in range(1, SEQ)]
    self_index = jnp.stack([me]).astype(jnp.int32)
    if packed:
        quarters = gather_seq(after(out_flat, probs))
    else:
        out_flat = lax.all_gather(out_own, "fsdp", axis=0, tiled=True)
        w_out = jnp.stack(natural(gather_seq(out_flat), me)).reshape(SEQ, fsdp, out_part, model)
        quarters = [w_out.transpose(1, 0, 2, 3).reshape(fsdp * out_rows, model)]
    heads[0] = after(heads[0], *gate_parts)
    heads16, w_out, attn, mixed, fed_own = mid(self_index, tokens, heads, quarters, gains, fsdp)

    side = jnp.stack([owners.low]).astype(jnp.int32)
    fed_blocks = [fed_own, swap_seq(fed_own, 1), swap_seq(fed_own, 2)]
    *saved, w_gate, w_up = gate_up(side, fed_blocks[1:2], gate_parts, up_parts, 1, [])
    fed_two = after(fed_blocks[2], saved[0])
    fed_blocks = fed_blocks[:2] + [fed_two, swap_seq(fed_two, 1)]
    *saved, w_gate, w_up = gate_up(side, fed_blocks[2:], [w_gate], [w_up], 2, saved)
    share_one, share_two, share_three = down(saved[0], w_down, 3)
    share_one = swap_seq(share_one, 1)
    share_pair = pair_sum(share_two, swap_seq(share_three, 1))
    fed_first = after(fed_blocks[0], share_pair, share_one)
    act16, value16, slope16, share = feed_first(fed_first, w_gate, w_up, w_down, saved)
    shares = [share, share_one, swap_seq(share_pair, 2)]

    def feed_end(first, second, third, mixed, grad, gains):
        ffo = first.astype(f32) + second.astype(f32) + third.astype(f32)
        gain = gains[3:4]
        grad_ffo, terms = rms_back(ffo, gain, grad.astype(f32))
        return mixed + rms_scale(ffo, gain), grad_ffo, column_sum(terms)

    output, ffo_own, gain_final_part = fused(
        feed_end,
        [*shares, mixed, cotangent],
        [gains],
        [(tokens.shape, bf16), (tokens.shape, bf16)],
        4,
        [(1, model)],
    )

    ffo_blocks = [ffo_own, swap_seq(ffo_own, 1), swap_seq(ffo_own, 2)]
    near_gate, near_up, *near_share = back(
        ffo_blocks[:2], value16, slope16, w_down, w_gate, w_up, 0
    )
    ffo_two = after(ffo_blocks[2], near_gate)
    ffo_blocks = ffo_blocks[:2] + [ffo_two, swap_seq(ffo_two, 1)]
    away_down, here_down = owners.product_halves(side, [act16], [ffo_blocks], 256)
    come_down = owners.swap(away_down)
    far_blocks = list(lax.optimization_barrier((away_down, *ffo_blocks[2:]))[1:])
    far_gate, far_up, *far_share = back(far_blocks, value16, slope16, w_down, w_gate, w_up, 2)
    pair = add_half(far_share[0], swap_seq(far_share[1], 1), 4)
    far_sum = swap_seq(pair, 2)
    near_one = swap_seq(near_share[1], 1)
    fed_left = [after(fed_blocks[0], pair, near_one)] + fed_blocks[1:]
    away_gate, here_gate = owners.product_halves(side, fed_left, [[near_gate, far_gate]], 384)
    come_gate = owners.swap(away_gate)
    half_down = owners.fold(after(here_down, away_gate), come_down)
    grad_down = owners.scatter_row(half_down)
    fed_left = [after(fed_left[0], half_down)] + fed_left[1:]
    away_up, here_up = owners.product_halves(side, fed_left, [[near_up, far_up]], 384)
    come_up = owners.swap(away_up)
    shares = [after(near_share[0], away_up), near_one, far_sum]
    grad_mixed, grad_attn16, *grad_heads, gain_mixed_part = mid_back(
        self_index, shares, cotangent, mixed, attn, w_out, gains, 4
    )
    grad_heads = [grad_heads[0]] + [swap_seq(grad_heads[r], r) for r in range(1, SEQ)]

    half_gate = owners.fold(after(here_gate, *grad_heads), come_gate)
    grad_gate = owners.scatter_row(half_gate)
    grad_heads[0] = after(grad_heads[0], half_gate)
    grad_queries, keep_kv, send_kv = attend_back(
        meta, queries, mine_kv, other_kv, probs, grad_heads, scale, 256
    )
    come_kv = swap_seq(send_kv, 1)
    grad_qkv16, gain_query_part, gain_key_part, *normed_blocks = project_back(
        jnp.stack([core]).astype(jnp.int32),
        grad_queries,
        after(keep_kv, grad_down),
        come_kv,
        query_raw,
        kv_raw,
        cosine,
        sine,
        head_gains,
        w_own,
    )
    half_up = owners.fold(after(here_up, grad_qkv16), come_up)
    grad_up = owners.scatter_row(half_up)
    grad_out_share = to_half(inner_rows(heads16, after(grad_attn16, half_up)))
    grad_out_view = grad_out_share.reshape(fsdp, SEQ, out_part, model)
    out_blocks = [
        lax.dynamic_index_in_dim(grad_out_view, me ^ r, 1, keepdims=False) for r in range(SEQ)
    ]
    out_pair = pair_sum(out_blocks[2], swap_seq(out_blocks[3], 1))
    out_one = pair_sum(out_blocks[0], swap_seq(out_blocks[1], 1))
    out_two = swap_seq(out_pair, 2)
    proj_left = after(normed16, out_pair, out_one)
    away_proj, here_proj = owners.product_halves(side, [proj_left], [[grad_qkv16]], 384)
    grad_out_part = pair_sum(out_one, after(out_two, away_proj))
    normed_pair = pair_sum(normed_blocks[2], swap_seq(normed_blocks[3], 1))
    normed_two = swap_seq(normed_pair, 2)
    normed_one = swap_seq(normed_blocks[1], 1)
    out_down = jnp.concatenate(natural(gather_seq(after(grad_down, away_proj)), me)).astype(f32)

    short = jnp.stack([gain_query_part[0], gain_key_part[0]], axis=1).reshape(fsdp, short_rows, 2)
    short = jnp.pad(short, ((0, 0), (0, rows - short_rows), (0, 0))).reshape(model, 2)
    gain_parts = jnp.concatenate(
        [jnp.stack([gain_mixed_part[0], gain_final_part[0]], axis=1), short], axis=1
    )
    gain_parts = jnp.pad(gain_parts, ((0, 0), (0, 128 - gain_parts.shape[1])))
    away_gains, here_gains = owners.halves(to_half(gain_parts))
    away_out, here_out = owners.halves(grad_out_part.reshape(fsdp * out_part, model))
    wide = 2 * head_width + 128

    def pile(proj, gains, out):
        upper = jnp.concatenate([proj, gains], axis=2)
        rest = jnp.pad(out[:, :, wide:], ((0, 0), (0, 0), (0, 2 * wide - model)))
        return jnp.concatenate([upper, out[:, :, :wide], rest], axis=1)

    away_small = pile(away_proj, away_gains, away_out)
    here_small = pile(here_proj, here_gains, here_out)
    come_small = owners.swap(after(away_small, grad_gate))
    half_small = owners.fold(here_small, come_small)
    grad_small = owners.scatter_direct(half_small)

    def input_end(first, second, third, values, grad, gains):
        total = first.astype(f32) + second.astype(f32) + third.astype(f32)
        return (grad + rms_back(values.astype(f32), gains[0:1], total)[0],)

    (grad_tokens,) = fused(
        input_end,
        [normed_blocks[0], normed_one, normed_two, tokens, grad_mixed],
        [gains],
        [(tokens.shape, f32)],
        4,
    )

    def spread(own):
        blocks = gather_seq(own)
        if fsdp <= 8:
            return spread_columns(self_index, blocks, fsdp)
        stack = jnp.stack([b.reshape(rows, fsdp, part) for b in natural(blocks, me)], axis=2)
        return stack.reshape(rows, hidden).astype(f32)

    out_gate = spread(grad_gate)
    out_up = spread(grad_up)

    feed_sum = jnp.sum(
        grad_gate.astype(f32) * gate_own.astype(f32)
        + grad_up.astype(f32) * up_own.astype(f32),
        axis=1,
    )
    upper = grad_small[:rows]
    input_sum = jnp.sum(
        upper[:, : 2 * head_width] * attn_own[:, : 2 * head_width].astype(f32), axis=1
    )
    tail = jnp.concatenate(
        [upper[:, 2 * head_width : 2 * head_width + 4], jnp.stack([input_sum, feed_sum], axis=1)],
        axis=1,
    )
    tail = jnp.pad(tail, ((0, 0), (0, 128 - tail.shape[1])))
    small = gather_seq(
        jnp.concatenate(
            [
                to_half(jnp.concatenate([upper[:, : 2 * head_width], tail], axis=1)),
                to_half(after(grad_small, out_up, out_gate, out_down, grad_tokens)[rows:]),
            ]
        )
    )
    lower = [b[rows:] for b in natural(small, me)]
    out_out = jnp.concatenate(
        [
            jnp.concatenate([b[:out_part], b[out_part:, : model - wide]], axis=1)
            for b in lower
        ]
    ).astype(f32)
    small = [b[:rows] for b in small]
    out_query = jnp.concatenate([b[:, :head_width] for b in natural(small, me)], axis=1).astype(f32)
    kv = [b[:, head_width : 2 * head_width].astype(f32) for b in small]
    same, cross = kv[0] + kv[2], kv[1] + kv[3]
    out_key = jnp.where(core == 0, same, cross)
    out_value = jnp.where(core == 0, cross, same)
    tails = sum(b[:, 2 * head_width :].astype(f32) for b in small)
    own_gains = attn_own[:, 2 * head_width : 2 * head_width + 128].astype(f32)
    out_g_mixed = tails[:, 0]
    out_g_final = tails[:, 1]
    out_g_query = tails[:short_rows, 2]
    out_g_key = tails[:short_rows, 3]
    out_g_input = tails[:, 4] / own_gains[:, 0]
    out_g_feed = tails[:, 5] / own_gains[:, 2]
    return (
        output,
        grad_tokens,
        out_query,
        out_key,
        out_value,
        out_out,
        out_gate,
        out_up,
        out_down,
        out_g_input,
        out_g_query,
        out_g_key,
        out_g_mixed,
        out_g_feed,
        out_g_final,
    )


def solution(mesh):
    by_token = P(("fsdp", "seq"), None)
    by_row = P("fsdp", None)
    by_one = P("fsdp")
    return jax.shard_map(
        partial(body, fsdp=mesh.shape["fsdp"]),
        mesh=mesh,
        in_specs=(by_token,) * 2 + (by_one,) * 2 + (by_row,) * 7 + (by_one,) * 6,
        out_specs=(by_token,) * 2 + (by_row,) * 7 + (by_one,) * 6,
        check_vma=False,
    )
```

```python
from functools import partial

import jax
import jax.numpy as jnp
from jax import lax
from jax.experimental import pallas as pl
from jax.experimental.pallas import tpu as pltpu
from jax.sharding import PartitionSpec as P

epsilon = 1e-06
f32 = jnp.float32
bf16 = jnp.bfloat16
SEQ = 4


def rms_scale(values, gain):
    return values * lax.rsqrt(jnp.mean(values * values, axis=-1, keepdims=True) + epsilon) * gain


def rotate(values, cosine, sine):
    half_width = values.shape[-1] // 2
    first_half = values[..., :half_width]
    second_half = values[..., half_width:]
    return jnp.concatenate(
        [first_half * cosine - second_half * sine, second_half * cosine + first_half * sine],
        axis=-1,
    )


def rope_tables(places, width):
    half_width = width // 2
    inverse = 1.0 / 1000000.0 ** (jnp.arange(half_width, dtype=f32) * 2.0 / width)
    angles = places.astype(f32)[:, None] * inverse[None, :]
    return (jnp.cos(angles), jnp.sin(angles))


def head_norm(raw, gain, cosine, sine):
    return rotate(rms_scale(raw, gain), cosine, sine)


def mult(left, right):
    return jnp.dot(left, right, preferred_element_type=f32)


def inner_rows(left, right):
    return lax.dot_general(left, right, (((0,), (0,)), ((), ())), preferred_element_type=f32)


def outer_cols(left, right):
    return lax.dot_general(left, right, (((1,), (1,)), ((), ())), preferred_element_type=f32)


def to_half(values):
    return values.astype(bf16)


def gated(gate_in, up_in):
    return jax.nn.gelu(gate_in, approximate=True) * up_in


MIB = 2**20


def held(shape):
    return pl.BlockSpec(shape, lambda *at: (0,) * len(shape), pipeline_mode=pl.Buffered(1))


def call(kernel, grid, in_specs, out_specs, outs, flops, limit=60, scratch=(), exps=0, same=None):
    shapes = [jax.ShapeDtypeStruct(s, d) for s, d in outs]
    size = sum(o.size * o.dtype.itemsize for o in shapes)
    made = pl.pallas_call(
        kernel,
        grid=grid,
        in_specs=in_specs,
        out_specs=out_specs,
        out_shape=shapes,
        scratch_shapes=list(scratch),
        input_output_aliases=same or {},
        compiler_params=pltpu.CompilerParams(vmem_limit_bytes=limit * MIB),
        cost_estimate=pl.CostEstimate(
            flops=flops // 50, bytes_accessed=size // 50, transcendentals=exps // 50
        ),
    )
    return lambda *operands: list(made(*operands))


def fused_kernel(function, ins, outs, sums, *refs):
    results = function(*[ref[...] for ref in refs[:ins]])
    for ref, value in zip(refs[ins : ins + outs], results[:outs], strict=True):
        ref[...] = value.astype(ref.dtype)
    for ref, value in zip(refs[ins + outs :], results[outs:], strict=True):

        @pl.when(pl.program_id(0) == 0)
        def _():
            ref[...] = jnp.zeros_like(ref)

        ref[...] += value


def fused(function, by_row, whole, outs, steps, sums=()):
    def split(shape):
        return pl.BlockSpec(
            (shape[0] // steps, *shape[1:]), lambda i: (i, *(0 for _ in shape[1:]))
        )

    return call(
        partial(fused_kernel, function, len(by_row) + len(whole), len(outs), len(sums)),
        (steps,),
        [split(v.shape) for v in by_row] + [held(v.shape) for v in whole],
        [split(s) for s, _ in outs] + [pl.BlockSpec(s, lambda i: (0, 0)) for s in sums],
        [*outs, *((s, f32) for s in sums)],
        flops=0,
    )(*by_row, *whole)


def add_half(first, second, steps):
    function = lambda a, b: (a.astype(f32) + b.astype(f32),)
    return fused(function, [first, second], [], [(first.shape, bf16)], steps)[0]


def pair_sum(first, second):
    return to_half(first.astype(f32) + second.astype(f32))


def rms_back(values, gain, grad):
    r = lax.rsqrt(jnp.mean(values * values, axis=-1, keepdims=True) + epsilon)
    scaled = grad * gain
    mean = jnp.mean(values * scaled, axis=-1, keepdims=True)
    return r * scaled - values * (r * r * r * mean), grad * values * r


def column_sum(values):
    return jnp.sum(values, axis=0, keepdims=True)


def mid_kernel(owners, quarters, me_ref, x_ref, *refs):
    heads = refs[:SEQ]
    weights = refs[SEQ : SEQ + quarters]
    gains_ref, all_ref, w_ref, attn_ref, mixed_ref, fed_ref = refs[SEQ + quarters :]
    width = heads[0].shape[1]
    for r, head in enumerate(heads):
        start = pl.multiple_of(jnp.bitwise_xor(me_ref[0], r) * width, 128)
        all_ref[:, pl.ds(start, width)] = head[...]
    if quarters == 1:
        w_ref[...] = weights[0][...]
    else:
        for r, weight in enumerate(weights):
            size = weight.shape[0] // owners
            for f in range(owners):
                start = (f * SEQ + jnp.bitwise_xor(me_ref[0], r)) * size
                start = pl.multiple_of(start, 16)
                w_ref[pl.ds(start, size), :] = weight[f * size : (f + 1) * size, :]
    attn = mult(all_ref[...], w_ref[...])
    attn_ref[...] = attn
    mixed = x_ref[...].astype(f32) + rms_scale(attn, gains_ref[1:2, :])
    mixed_ref[...] = mixed
    fed_ref[...] = to_half(rms_scale(mixed, gains_ref[2:3, :]))


def mid(me, tokens, heads, weights, gains, owners):
    rows, model = tokens.shape
    width = heads[0].shape[1] * SEQ
    specs = [held(v.shape) for v in [tokens, *heads, *weights, gains]]
    outs = [
        ((rows, width), bf16),
        ((width, model), bf16),
        ((rows, model), f32),
        ((rows, model), f32),
        ((rows, model), bf16),
    ]
    return call(
        partial(mid_kernel, owners, len(weights)),
        (1,),
        [pl.BlockSpec(memory_space=pltpu.SMEM)] + specs,
        [pl.BlockSpec(s, lambda i: (0, 0)) for s, _ in outs],
        outs,
        flops=2 * rows * width * model,
    )(me, tokens, *heads, *weights, gains)


def mid_back_kernel(me_ref, a_ref, b_ref, c_ref, dy_ref, mixed_ref, attn_ref, w_ref, gains_ref, *refs):
    grad_ref, grad_attn_ref = refs[:2]
    outs, sum_ref, heads_ref = refs[2 : 2 + SEQ], refs[2 + SEQ], refs[3 + SEQ]
    grad_fed = a_ref[...].astype(f32) + b_ref[...].astype(f32) + c_ref[...].astype(f32)
    part, _ = rms_back(mixed_ref[...], gains_ref[2:3, :], grad_fed)
    grad_mixed = dy_ref[...].astype(f32) + part
    grad_ref[...] = grad_mixed
    grad_attn, terms = rms_back(attn_ref[...], gains_ref[1:2, :], grad_mixed)
    half = to_half(grad_attn)
    grad_attn_ref[...] = half
    heads_ref[...] = to_half(outer_cols(half, w_ref[...]))
    width = outs[0].shape[1]
    for r, out in enumerate(outs):
        start = pl.multiple_of(jnp.bitwise_xor(me_ref[0], r) * width, 128)
        out[...] = heads_ref[:, pl.ds(start, width)]

    @pl.when(pl.program_id(0) == 0)
    def _():
        sum_ref[...] = jnp.zeros_like(sum_ref)

    sum_ref[...] += column_sum(terms)


def mid_back(me, shares, cotangent, mixed, attn, w_out, gains, steps):
    rows, model = mixed.shape
    total = w_out.shape[0]
    by_row = [*shares, cotangent, mixed, attn]
    row = lambda width: pl.BlockSpec((rows // steps, width), lambda i: (i, 0))
    outs = [((rows, model), f32), ((rows, model), bf16)]
    outs += [((rows, total // SEQ), bf16)] * SEQ
    return call(
        mid_back_kernel,
        (steps,),
        [pl.BlockSpec(memory_space=pltpu.SMEM)]
        + [row(model) for _ in by_row]
        + [held(w_out.shape), held(gains.shape)],
        [row(s[1]) for s, _ in outs] + [pl.BlockSpec((1, model), lambda i: (0, 0))],
        [*outs, ((1, model), f32)],
        flops=2 * rows * model * total,
        scratch=[pltpu.VMEM((rows // steps, total), bf16)],
    )(me, *by_row, w_out, gains)


def turn_back(grad, cosine, sine):
    half = grad.shape[-1] // 2
    a, b = grad[:, :half], grad[:, half:]
    return jnp.concatenate([a * cosine + b * sine, b * cosine - a * sine], axis=-1)


def project_back_kernel(core_ref, *refs):
    dq_ref, keep_ref, come_ref, q_raw_ref, kv_raw_ref, cos_ref, sin_ref, gains_ref, w_ref = refs[:9]
    grad_ref, q_sum_ref, k_sum_ref = refs[9:12]
    outs = refs[12:]
    cosine, sine = cos_ref[...], sin_ref[...]
    head = dq_ref.shape[1]
    first = core_ref[0] == 0
    grad_q, q_terms = rms_back(
        q_raw_ref[...], gains_ref[4:5, :], turn_back(dq_ref[...], cosine, sine)
    )
    grad_kv = keep_ref[...] + come_ref[...].astype(f32)
    grad_k, k_terms = rms_back(
        kv_raw_ref[...], gains_ref[5:6, :], turn_back(grad_kv, cosine, sine)
    )
    grad_ref[:, :head] = to_half(grad_q)
    grad_ref[:, head:] = to_half(jnp.where(first, grad_k, grad_kv))
    share = to_half(outer_cols(grad_ref[...], w_ref[...]))
    for r, out in enumerate(outs):

        @pl.when(pl.program_id(0) == r)
        def _():
            out[...] = share

    @pl.when(pl.program_id(0) == 0)
    def _():
        q_sum_ref[...] = jnp.zeros_like(q_sum_ref)
        k_sum_ref[...] = jnp.zeros_like(k_sum_ref)

    q_sum_ref[...] += column_sum(q_terms)
    k_sum_ref[...] += jnp.where(first, column_sum(k_terms), 0.0)


def project_back(core, dq, keep, come, q_raw, kv_raw, cosine, sine, head_gains, w_own):
    rows, head = dq.shape
    model = w_own.shape[0]
    block = rows // SEQ
    by_row = [dq, keep, come, q_raw, kv_raw, cosine, sine]
    row = lambda width: pl.BlockSpec((block, width), lambda i: (i, 0))
    fixed = lambda shape: pl.BlockSpec(shape, lambda i: (0, 0))
    return call(
        project_back_kernel,
        (SEQ,),
        [pl.BlockSpec(memory_space=pltpu.SMEM)]
        + [row(v.shape[1]) for v in by_row]
        + [held(head_gains.shape), held(w_own.shape)],
        [row(2 * head), fixed((1, head)), fixed((1, head))] + [fixed((block, model))] * SEQ,
        [((rows, 2 * head), bf16), ((1, head), f32), ((1, head), f32)]
        + [((block, model), bf16)] * SEQ,
        flops=4 * rows * head * model,
    )(core, *by_row, head_gains, w_own)


def front_kernel(count, rows, short, packed, meta_ref, *refs):
    tokens = refs[:SEQ]
    pieces = refs[SEQ : SEQ + count]
    cos_ref, sin_ref = refs[SEQ + count : SEQ + count + 2]
    normed_ref, q_ref, kv_ref, q_raw_ref, kv_raw_ref, w_ref, out_ref, gains_ref, head_gains_ref = (
        refs[SEQ + count + 2 : -2]
    )
    x_ref, columns_ref = refs[-2:]
    at = pl.program_id(0)
    head = q_ref.shape[1]

    @pl.when(at == 0)
    def _():
        for j, piece in enumerate(pieces):
            size = piece.shape[0] - 2 * packed
            start = pl.multiple_of(meta_ref[1 + j] * rows, 16)
            w_ref[pl.ds(start, size), :] = piece[:size, : 2 * head]
            columns_ref[pl.ds(start, size), :] = piece[:size, 2 * head :].astype(f32)
            if packed:
                start = pl.multiple_of(meta_ref[1 + j] * packed, 16)
                wide = piece.shape[1]
                rest = out_ref.shape[1] - wide
                out_ref[pl.ds(start, packed), :wide] = piece[size : size + packed, :]
                out_ref[pl.ds(start, packed), wide:] = piece[size + packed :, :rest]
        gains = columns_ref[...].T[:8]
        gains_ref[...] = gains
        model = gains.shape[1]
        from_row = lax.broadcasted_iota(jnp.int32, (model, head), 0)
        to_col = lax.broadcasted_iota(jnp.int32, (model, head), 1)
        owner = to_col >> (short.bit_length() - 1)
        wanted = owner * rows + (to_col & (short - 1))
        pick = jnp.where(from_row == wanted, 1.0, 0.0)
        head_gains_ref[...] = mult(to_half(gains), to_half(pick))

    for r in range(SEQ):

        @pl.when(at == r)
        def _():
            x_ref[...] = tokens[r][...].astype(f32)

    values = x_ref[...]
    normed = to_half(rms_scale(values, gains_ref[0:1, :]))
    normed_ref[...] = normed
    raw = mult(normed, w_ref[...])
    q_raw = raw[:, :head]
    kv_raw = raw[:, head:]
    q_raw_ref[...] = q_raw
    kv_raw_ref[...] = kv_raw
    cosine, sine = cos_ref[...], sin_ref[...]
    q_ref[...] = to_half(head_norm(q_raw, head_gains_ref[4:5, :], cosine, sine))
    keyed = head_norm(kv_raw, head_gains_ref[5:6, :], cosine, sine)
    kv_ref[...] = to_half(jnp.where(meta_ref[0] == 0, keyed, kv_raw))


def front(tokens, pieces, meta, cosine, sine, rows, short, packed):
    block, model = tokens[0].shape
    head = 2 * cosine.shape[1]
    total = block * SEQ
    out_shape = (max(8, packed * len(pieces)), model)
    slab = lambda width: pl.BlockSpec((block, width), lambda i: (i, 0))
    fixed = lambda shape: pl.BlockSpec(shape, lambda i: (0, 0))
    return call(
        partial(front_kernel, len(pieces), rows, short, packed),
        (SEQ,),
        [pl.BlockSpec(memory_space=pltpu.SMEM)]
        + [held(t.shape) for t in tokens]
        + [held(p.shape) for p in pieces]
        + [slab(head // 2)] * 2,
        [slab(model), slab(head), slab(head), slab(head), slab(head)]
        + [fixed((model, 2 * head)), fixed(out_shape), fixed((8, model)), fixed((8, head))],
        [
            ((total, model), bf16),
            ((total, head), bf16),
            ((total, head), bf16),
            ((total, head), f32),
            ((total, head), f32),
            ((model, 2 * head), bf16),
            (out_shape, bf16),
            ((8, model), f32),
            ((8, head), f32),
        ],
        flops=4 * total * model * head,
        scratch=[
            pltpu.VMEM((block, model), f32),
            pltpu.VMEM((model, 128), f32),
        ],
    )(meta, *tokens, *pieces, cosine, sine)


def twins(values):
    size = values.shape[0] // SEQ
    return jnp.concatenate([values[(r ^ 1) * size : (r ^ 1) * size + size] for r in range(SEQ)])


def split_pair(meta_ref, mine_ref, other_ref, keys_ref, values_ref):
    mine, other = mine_ref[...], twins(other_ref[...])
    first = meta_ref[0] == 0

    @pl.when(first)
    def _():
        keys_ref[...] = mine
        values_ref[...] = other

    @pl.when(jnp.logical_not(first))
    def _():
        keys_ref[...] = other
        values_ref[...] = mine


def attend_kernel(
    scale, meta_ref, q_ref, mine_ref, other_ref, code_ref, low_ref, high_ref, *refs
):
    outs, (probs_ref, keys_ref, values_ref) = refs[:SEQ], refs[SEQ:]
    at = pl.program_id(0)

    @pl.when(at == 0)
    def _():
        split_pair(meta_ref, mine_ref, other_ref, keys_ref, values_ref)

    scores = outer_cols(q_ref[...], keys_ref[...])
    code = code_ref[...]
    seen = (code >= low_ref[...]) & (code <= high_ref[...])
    expd = jnp.where(seen, jnp.exp2(scores * (scale * 1.4426950408889634)), 0.0)
    total = jnp.sum(expd, axis=1, keepdims=True)
    probs = to_half(expd * (1.0 / total))
    probs_ref[...] = probs
    out = to_half(mult(probs, values_ref[...]))
    block = out.shape[0]
    steps = outs[0].shape[0] // block
    for r in range(SEQ):
        for s in range(steps):

            @pl.when(at == r * steps + s)
            def _():
                outs[r][s * block : (s + 1) * block, :] = out


def attend(meta, queries, mine, other, code, low, high, scale, block):
    rows, width = queries.shape
    count = mine.shape[0]
    slab = pl.BlockSpec((block, width), lambda i: (i, 0))
    thin = pl.BlockSpec((block, 1), lambda i: (i, 0))
    part = pl.BlockSpec((rows // SEQ, width), lambda i: (0, 0))
    return call(
        partial(attend_kernel, scale),
        (rows // block,),
        [pl.BlockSpec(memory_space=pltpu.SMEM), slab, held(mine.shape), held(mine.shape)]
        + [pl.BlockSpec((1, count), lambda i: (0, 0)), thin, thin],
        [part] * SEQ + [pl.BlockSpec((block, count), lambda i: (i, 0))],
        [((rows // SEQ, width), bf16)] * SEQ + [((rows, count), bf16)],
        flops=4 * rows * count * width,
        exps=rows * count,
        scratch=[pltpu.VMEM((count, width), bf16)] * 2,
    )(meta, queries, mine, other, code, low, high)


def attend_back_kernel(scale, meta_ref, q_ref, mine_ref, other_ref, p_ref, *refs):
    grads_in = refs[:SEQ]
    dq_ref, keep_ref, send_ref, keys_ref, values_ref, dk_ref, dv_ref, g_ref = refs[SEQ:]
    at = pl.program_id(0)

    @pl.when(at == 0)
    def _():
        split_pair(meta_ref, mine_ref, other_ref, keys_ref, values_ref)
        dk_ref[...] = jnp.zeros_like(dk_ref)
        dv_ref[...] = jnp.zeros_like(dv_ref)

    block = g_ref.shape[0]
    steps = grads_in[0].shape[0] // block
    for r in range(SEQ):
        for s in range(steps):

            @pl.when(at == r * steps + s)
            def _():
                g_ref[...] = grads_in[r][s * block : (s + 1) * block, :]

    probs = p_ref[...]
    grads = g_ref[...]
    wide = probs.astype(f32)
    grad_probs = outer_cols(grads, values_ref[...])
    centre = jnp.sum(wide * grad_probs, axis=1, keepdims=True)
    grad_scores = to_half(wide * (grad_probs - centre))
    dq_ref[...] = scale * mult(grad_scores, keys_ref[...])
    dk_ref[...] += scale * inner_rows(grad_scores, q_ref[...])
    dv_ref[...] += inner_rows(probs, grads)

    @pl.when(at == pl.num_programs(0) - 1)
    def _():
        first = meta_ref[0] == 0
        keep_ref[...] = jnp.where(first, dk_ref[...], dv_ref[...])
        send_ref[...] = twins(to_half(jnp.where(first, dv_ref[...], dk_ref[...])))


def attend_back(meta, queries, mine, other, probs, grads, scale, block):
    rows, width = queries.shape
    count = mine.shape[0]
    whole = pl.BlockSpec((count, width), lambda i: (0, 0))
    slab = pl.BlockSpec((block, width), lambda i: (i, 0))
    return call(
        partial(attend_back_kernel, scale),
        (rows // block,),
        [pl.BlockSpec(memory_space=pltpu.SMEM), slab, held(mine.shape), held(mine.shape)]
        + [pl.BlockSpec((block, count), lambda i: (i, 0))]
        + [held(g.shape) for g in grads],
        [slab, whole, whole],
        [((rows, width), f32), ((count, width), f32), ((count, width), bf16)],
        flops=8 * rows * count * width,
        scratch=[pltpu.VMEM((count, width), bf16)] * 2
        + [pltpu.VMEM((count, width), f32)] * 2
        + [pltpu.VMEM((block, width), bf16)],
    )(meta, queries, mine, other, probs, *grads)


def spread_kernel(owners, me_ref, *refs):
    blocks, out_ref, all_ref = refs[:SEQ], refs[SEQ], refs[SEQ + 1]
    for r, block in enumerate(blocks):
        all_ref[jnp.bitwise_xor(me_ref[0], r)] = block[...].astype(f32)
    part = blocks[0].shape[1] // owners
    out_ref[...] = jnp.concatenate(
        [all_ref[t][:, f * part : (f + 1) * part] for f in range(owners) for t in range(SEQ)],
        axis=1,
    )


def spread_columns(me, blocks, owners):
    rows, width = blocks[0].shape
    steps = 3 if rows % 48 == 0 else 1
    step = rows // steps
    row = lambda w: pl.BlockSpec((step, w), lambda i: (i, 0))
    return call(
        partial(spread_kernel, owners),
        (steps,),
        [pl.BlockSpec(memory_space=pltpu.SMEM)] + [row(width)] * SEQ,
        [row(SEQ * width)],
        [((rows, SEQ * width), f32)],
        flops=0,
        scratch=[pltpu.VMEM((SEQ, step, width), f32)],
    )(me, *blocks)[0]


def pick_block(blocks, into_ref):
    for r, block in enumerate(blocks):

        @pl.when(pl.program_id(0) == r)
        def _():
            into_ref[...] = block[...]


def feed_rows(x_ref, gate_ref, up_ref, act_ref, value_ref, slope_ref):
    rows = x_ref[...]
    gate = mult(rows, gate_ref[...])
    upper = mult(rows, up_ref[...])
    c = 0.7978845608028654
    square = gate * gate
    bend = jnp.tanh(gate * (c + (c * 0.044715) * square))
    half = 0.5 + 0.5 * bend
    value = gate * half
    slope = half + (0.5 * gate) * (1.0 - bend * bend) * (c + (3 * c * 0.044715) * square)
    act_ref[...] = to_half(value * upper)
    value_ref[...] = to_half(value)
    slope_ref[...] = to_half(slope * upper)


def gate_up_kernel(count, pieces, kept, meta_ref, *refs):
    parts, outs = refs[count : count + 2 * pieces], refs[count + 2 * pieces + kept :]
    act_ref, value_ref, slope_ref = outs[:3]
    x_ref = outs[-1]
    gate_ref, up_ref = outs[3:5] if pieces == 2 else parts

    if pieces == 2:

        @pl.when(pl.program_id(0) == 0)
        def _():
            for w_ref, own in ((gate_ref, parts[:2]), (up_ref, parts[2:])):
                for half, ref in enumerate(own):
                    size = ref.shape[1]
                    for z in range(ref.shape[0]):
                        start = (2 * z + jnp.bitwise_xor(meta_ref[0], half)) * size
                        w_ref[pl.ds(pl.multiple_of(start, 16), size), :] = ref[z]

    pick_block(refs[:count], x_ref)
    feed_rows(x_ref, gate_ref, up_ref, act_ref, value_ref, slope_ref)


def gate_up(meta, blocks, gate_parts, up_parts, first, saved):
    block, model = blocks[0].shape
    width = gate_parts[0].shape[-1]
    total = block * SEQ
    slab = pl.BlockSpec((block, width), lambda i: (i + first, 0))
    whole = pl.BlockSpec((model, width), lambda i: (0, 0))
    parts = [*gate_parts, *up_parts]
    made = len(parts) - 2
    ins = 1 + len(blocks) + len(parts)
    out = call(
        partial(gate_up_kernel, len(blocks), len(gate_parts), len(saved)),
        (len(blocks),),
        [pl.BlockSpec(memory_space=pltpu.SMEM)]
        + [held(b.shape) for b in [*blocks, *parts]]
        + [pl.BlockSpec(memory_space=pl.ANY)] * len(saved),
        [slab] * 3 + [whole] * made,
        [((total, width), bf16)] * 3 + [((model, width), bf16)] * made,
        flops=4 * total * model * width,
        exps=total * width,
        scratch=[pltpu.VMEM((block, model), bf16)],
        limit=62,
        same={ins + i: i for i in range(len(saved))},
    )(meta, *blocks, *parts, *saved)
    return out if made else out + parts


def feed_kernel(x_ref, gate_ref, up_ref, down_ref, *refs):
    act_ref, value_ref, slope_ref, out_ref = refs[3:]
    feed_rows(x_ref, gate_ref, up_ref, act_ref, value_ref, slope_ref)
    out_ref[...] = to_half(mult(act_ref[...], down_ref[...]))


def feed_first(rows, w_gate, w_up, w_down, saved):
    block, model = rows.shape
    width = w_gate.shape[1]
    slab = pl.BlockSpec((block, width), lambda i: (0, 0))
    return call(
        feed_kernel,
        (1,),
        [held(v.shape) for v in [rows, w_gate, w_up, w_down]]
        + [pl.BlockSpec(memory_space=pl.ANY)] * 3,
        [slab] * 3 + [pl.BlockSpec((block, model), lambda i: (0, 0))],
        [(v.shape, bf16) for v in saved] + [((block, model), bf16)],
        flops=6 * block * model * width,
        limit=62,
        same={4: 0, 5: 1, 6: 2},
    )(rows, w_gate, w_up, w_down, *saved)


def down_kernel(x_ref, w_ref, *outs):
    out = to_half(mult(x_ref[...], w_ref[...]))
    for r, ref in enumerate(outs):

        @pl.when(pl.program_id(0) == r)
        def _():
            ref[...] = out


def down(rows, w_down, count):
    block = rows.shape[0] // (count + 1)
    width, model = w_down.shape
    out = pl.BlockSpec((block, model), lambda i: (0, 0))
    return call(
        down_kernel,
        (count,),
        [pl.BlockSpec((block, width), lambda i: (i + 1, 0)), held(w_down.shape)],
        [out] * count,
        [((block, model), bf16)] * count,
        flops=2 * count * block * model * width,
    )(rows, w_down)


def back_kernel(count, *refs):
    y_refs = refs[:count]
    value_ref, slope_ref, down_ref, gate_ref, up_ref, dg_ref, du_ref = refs[count : count + 7]
    outs, y_ref = refs[count + 7 : -1], refs[-1]
    pick_block(y_refs, y_ref)
    grad_act = outer_cols(y_ref[...], down_ref[...])
    dg_ref[...] = to_half(grad_act * slope_ref[...].astype(f32))
    du_ref[...] = to_half(grad_act * value_ref[...].astype(f32))
    out = to_half(outer_cols(dg_ref[...], gate_ref[...]) + outer_cols(du_ref[...], up_ref[...]))
    for r, ref in enumerate(outs):

        @pl.when(pl.program_id(0) == r)
        def _():
            ref[...] = out


def back(blocks, value, slope, w_down, w_gate, w_up, first):
    block, model = blocks[0].shape
    count = len(blocks)
    width = w_gate.shape[1]
    ahead = pl.BlockSpec((block, width), lambda i: (i + first, 0))
    slab = pl.BlockSpec((block, width), lambda i: (i, 0))
    out = pl.BlockSpec((block, model), lambda i: (0, 0))
    return call(
        partial(back_kernel, count),
        (count,),
        [held(b.shape) for b in blocks]
        + [ahead, ahead, held(w_down.shape), held(w_gate.shape), held(w_up.shape)],
        [slab, slab] + [out] * count,
        [((block * count, width), bf16)] * 2 + [((block, model), bf16)] * count,
        flops=6 * count * block * model * width,
        scratch=[pltpu.VMEM((block, model), bf16)],
    )(*blocks, value, slope, w_down, w_gate, w_up)


def cut_rows(blocks, many):
    each = many // len(blocks)
    size = blocks[0].shape[0] // each
    return [b[r * size : (r + 1) * size] for b in blocks for r in range(each)]


def rows_sum(left, right):
    total = inner_rows(left[0], right[0])
    for a, b in zip(left[1:], right[1:], strict=True):
        total = total + inner_rows(a, b)
    return total


def rows_kernel(counts, many, meta_ref, *refs):
    total_in = sum(counts)
    results = len(counts) - 1
    values = [ref[...] for ref in refs[:total_in]]
    left = cut_rows(values[: counts[0]], many)
    at = counts[0]
    totals = []
    for count in counts[1:]:
        totals.append(rows_sum(left, cut_rows(values[at : at + count], many)))
        at += count
    if len(refs) == total_in + results:
        for ref, total in zip(refs[total_in:], totals, strict=True):
            ref[...] = to_half(total)
        return
    outs, sums = refs[total_in : total_in + 2 * results], refs[total_in + 2 * results :]
    tile = left[0].shape[1]
    here = pl.ds(pl.multiple_of(pl.program_id(0) * tile, 128), tile)
    for ref, total in zip(sums, totals, strict=True):
        ref[here, :] = total

    @pl.when(pl.program_id(0) == pl.num_programs(0) - 1)
    def _():
        for o in range(results):
            for half, ref in enumerate(outs[2 * o : 2 * o + 2]):
                size = ref.shape[1]
                for z in range(ref.shape[0]):
                    start = (2 * z + jnp.bitwise_xor(meta_ref[0], 1 - half)) * size
                    ref[z] = to_half(sums[o][pl.ds(pl.multiple_of(start, 8), size), :])


def rows_product(meta, left, rights, tile, owners, cut=True):
    counts = [len(v) for v in [left, *rights]]
    many = max(counts)
    height = left[0].shape[1]
    widths = [r[0].shape[1] for r in rights]
    flat = [v for r in rights for v in r]
    steps = pl.cdiv(height, tile)
    shape = lambda w: (owners // 2, height // owners, w)
    if cut:
        specs = [pl.BlockSpec(shape(w), lambda i: (0, 0, 0)) for w in widths for _ in range(2)]
        outs = [(shape(w), bf16) for w in widths for _ in range(2)]
    else:
        specs = [pl.BlockSpec((tile, w), lambda i: (i, 0)) for w in widths]
        outs = [((height, w), bf16) for w in widths]
    return call(
        partial(rows_kernel, counts, many),
        (steps,),
        [pl.BlockSpec(memory_space=pltpu.SMEM)]
        + [pl.BlockSpec((v.shape[0], tile), lambda i: (0, i)) for v in left]
        + [held(v.shape) for v in flat],
        specs,
        outs,
        flops=2 * sum(v.shape[0] for v in left) * height * sum(widths),
        scratch=[pltpu.VMEM((steps * tile, w), f32) for w in widths] if cut else [],
        limit=62,
    )(meta, *left, *flat)


def after(value, *others):
    return lax.optimization_barrier((value, others))[0]


def swap_seq(values, bits):
    return lax.ppermute(values, "seq", [(i, i ^ bits) for i in range(SEQ)])


def gather_seq(own):
    one = swap_seq(own, 1)
    two = swap_seq(own, 2)
    return [own, one, two, swap_seq(two, 1)]


def natural(blocks, me):
    stack = jnp.stack(blocks)
    return [lax.dynamic_index_in_dim(stack, me ^ j, 0, keepdims=False) for j in range(SEQ)]


def reduce_seq(blocks):
    three = swap_seq(blocks[3], 1)
    pair = to_half(blocks[2].astype(f32) + three.astype(f32))
    two = swap_seq(pair, 2)
    one = swap_seq(blocks[1], 1)
    return blocks[0].astype(f32) + one.astype(f32) + two.astype(f32)


class Owners:
    def __init__(self, count):
        self.count = count
        self.rows = count // 2
        self.groups = [[2 * z + y for z in range(self.rows)] for y in range(2)]
        index = lax.axis_index("fsdp")
        self.low = index % 2
        self.high = index // 2
        self.direct = self.rows <= 4

    def swap(self, values):
        return lax.ppermute(values, "fsdp", [(i, i ^ 1) for i in range(self.count)])

    def shift(self, values, by):
        return lax.ppermute(
            values, "fsdp", [(i, (i + 2 * by) % self.count) for i in range(self.count)]
        )

    def gather_row(self, values):
        return lax.all_gather(values, "fsdp", axis=0, tiled=True, axis_index_groups=self.groups)

    def pair(self, mine, other, axis):
        first = jnp.where(self.low == 0, mine, other)
        second = jnp.where(self.low == 0, other, mine)
        return jnp.stack([first, second], axis=axis)

    def gather_pieces(self, own):
        if not self.direct:
            return [lax.all_gather(own, "fsdp", axis=0, tiled=True)], [jnp.int32(0)]
        far = [own] + [self.shift(own, by) for by in range(1, self.rows)]
        near = [self.swap(p) for p in far]
        starts = [lax.rem(self.high - by + self.rows, self.rows) * 2 for by in range(self.rows)]
        places = [s + self.low for s in starts] + [s + 1 - self.low for s in starts]
        return far + near, places

    def gather_wide(self, own, later):
        if not self.direct:
            return [lax.all_gather(own, "fsdp", axis=0, tiled=True)]
        size, width = own.shape
        mine = after(self.gather_row(own), later).reshape(self.rows, size, width)
        return [mine, self.swap(mine)]

    def gather_pair_first(self, own, later):
        size, width = own.shape
        both = self.pair(own, after(self.swap(own), later), 0).reshape(2 * size, width)
        return self.gather_row(both)

    def halves(self, whole):
        size = whole.shape[0] // self.count
        view = whole.reshape(self.rows, 2, size, whole.shape[1])
        away = lax.dynamic_index_in_dim(view, 1 - self.low, 1, keepdims=False)
        here = lax.dynamic_index_in_dim(view, self.low, 1, keepdims=False)
        return away, here

    def product_halves(self, side, left, rights, tile):
        if (left[0].shape[1] // self.count) % 8 == 0:
            return rows_product(side, left, rights, tile, self.count)
        whole = rows_product(side, left, rights, tile, self.count, False)
        return [half for value in whole for half in self.halves(value)]

    def fold(self, here, come):
        return add_half(here, come, here.shape[0])

    def scatter_row(self, half):
        return lax.psum_scatter(
            half.reshape(-1, half.shape[2]),
            "fsdp",
            scatter_dimension=0,
            axis_index_groups=self.groups,
            tiled=True,
        )

    def scatter_direct(self, half):
        if not self.direct:
            return self.scatter_row(half).astype(f32)
        total = lax.dynamic_index_in_dim(half, self.high, 0, keepdims=False).astype(f32)
        for by in range(1, self.rows):
            z = lax.rem(self.high + by, self.rows)
            away = lax.dynamic_index_in_dim(half, z, 0, keepdims=False)
            total = total + self.shift(away, by).astype(f32)
        return total


def body(
    tokens,
    cotangent,
    positions,
    segment,
    query_weight,
    key_weight,
    value_weight,
    out_weight,
    gate_weight,
    up_weight,
    down_weight,
    gain_input,
    gain_query,
    gain_key,
    gain_mixed,
    gain_feed,
    gain_final,
    fsdp,
):
    owners = Owners(fsdp)
    me = lax.axis_index("seq")
    core = me & 1
    tok_rows, model = tokens.shape
    group_len = positions.shape[0]
    rows = query_weight.shape[0]
    head_width = key_weight.shape[1]
    hidden = gate_weight.shape[1]
    slab = hidden // fsdp
    part = slab // SEQ
    scale = head_width ** (-0.5)

    head_cols = lax.dynamic_slice_in_dim(query_weight, me * head_width, head_width, axis=1)
    key_or_value = jnp.where(core == 0, key_weight, value_weight)
    short = jnp.stack([gain_query, gain_key], axis=1)
    short = jnp.pad(short, ((0, rows - short.shape[0]), (0, 0)))
    gains_own = jnp.concatenate(
        [jnp.stack([gain_input, gain_mixed, gain_feed, gain_final], axis=1), short], axis=1
    )
    gains_own = jnp.pad(gains_own, ((0, 0), (0, 128 - gains_own.shape[1])))
    out_rows = out_weight.shape[0]
    out_part = out_rows // SEQ
    out_own = lax.dynamic_slice_in_dim(out_weight, me * out_part, out_part, axis=0)
    out_own = to_half(out_own)
    attn_own = jnp.concatenate(
        [to_half(head_cols), to_half(key_or_value), to_half(gains_own)], axis=1
    )
    packed = out_part if owners.direct and out_part % 16 == 0 else 0
    if packed:
        wide = attn_own.shape[1]
        rest = jnp.pad(out_own[:, wide:], ((0, 0), (0, 2 * wide - model)))
        pack_own = jnp.concatenate([attn_own, out_own[:, :wide], rest])
    else:
        pack_own = attn_own

    def columns(weight):
        return to_half(
            jnp.concatenate(
                [
                    lax.dynamic_slice_in_dim(weight, f * slab + me * part, part, axis=1)
                    for f in range(fsdp)
                ],
                axis=1,
            )
        )

    pieces, starts = owners.gather_pieces(pack_own)
    ahead = pieces[: (len(pieces) + 1) // 2]
    tokens_out = after(tokens, pack_own)
    token_blocks = [tokens, swap_seq(tokens_out, 1), swap_seq(tokens_out, 2)]
    token_blocks.append(swap_seq(after(token_blocks[2], *ahead), 1))
    gate_own = columns(after(gate_weight, token_blocks[2], *ahead))
    up_own = columns(after(up_weight, gate_own))
    down_own = lax.dynamic_slice_in_dim(after(down_weight, up_own), me * part, part, axis=0)
    down_own = to_half(down_own)

    def own_order(values):
        return jnp.concatenate(
            [
                lax.dynamic_slice_in_dim(values, (me ^ r) * tok_rows, tok_rows)
                for r in range(SEQ)
            ]
        )

    places = own_order(positions)
    kinds = own_order(segment)
    cosine, sine = rope_tables(places, head_width)
    second = kinds == 2
    code = jnp.where(second, -places, places).astype(f32)[None, :]
    low = jnp.where(second, -places, 0).astype(f32)[:, None]
    high = jnp.where(second, group_len // 2 - 1, places).astype(f32)[:, None]
    short_rows = head_width // fsdp

    meta = jnp.stack([core] + starts).astype(jnp.int32)
    normed16, queries, mine_kv, query_raw, kv_raw, w_own, out_flat, gains, head_gains = front(
        token_blocks, pieces, meta, cosine, sine, rows, short_rows, packed
    )
    gate_parts = owners.gather_wide(gate_own, queries)
    other_kv = swap_seq(mine_kv, 1)
    *heads, probs = attend(meta, queries, mine_kv, other_kv, code, low, high, scale, 256)
    up_parts = owners.gather_wide(up_own, probs)
    w_down = owners.gather_pair_first(down_own, queries)
    heads = [heads[0]] + [swap_seq(heads[r], r) for r in range(1, SEQ)]
    self_index = jnp.stack([me]).astype(jnp.int32)
    if packed:
        quarters = gather_seq(after(out_flat, probs))
    else:
        out_flat = lax.all_gather(out_own, "fsdp", axis=0, tiled=True)
        w_out = jnp.stack(natural(gather_seq(out_flat), me)).reshape(SEQ, fsdp, out_part, model)
        quarters = [w_out.transpose(1, 0, 2, 3).reshape(fsdp * out_rows, model)]
    heads[0] = after(heads[0], *gate_parts)
    heads16, w_out, attn, mixed, fed_own = mid(self_index, tokens, heads, quarters, gains, fsdp)

    side = jnp.stack([owners.low]).astype(jnp.int32)
    fed_blocks = [fed_own, swap_seq(fed_own, 1), swap_seq(fed_own, 2)]
    *saved, w_gate, w_up = gate_up(side, fed_blocks[1:2], gate_parts, up_parts, 1, [])
    fed_two = after(fed_blocks[2], saved[0])
    fed_blocks = fed_blocks[:2] + [fed_two, swap_seq(fed_two, 1)]
    *saved, w_gate, w_up = gate_up(side, fed_blocks[2:], [w_gate], [w_up], 2, saved)
    share_one, share_two, share_three = down(saved[0], w_down, 3)
    share_one = swap_seq(share_one, 1)
    share_pair = pair_sum(share_two, swap_seq(share_three, 1))
    fed_first = after(fed_blocks[0], share_pair, share_one)
    act16, value16, slope16, share = feed_first(fed_first, w_gate, w_up, w_down, saved)
    shares = [share, share_one, swap_seq(share_pair, 2)]

    def feed_end(first, second, third, mixed, grad, gains):
        ffo = first.astype(f32) + second.astype(f32) + third.astype(f32)
        gain = gains[3:4]
        grad_ffo, terms = rms_back(ffo, gain, grad.astype(f32))
        return mixed + rms_scale(ffo, gain), grad_ffo, column_sum(terms)

    output, ffo_own, gain_final_part = fused(
        feed_end,
        [*shares, mixed, cotangent],
        [gains],
        [(tokens.shape, bf16), (tokens.shape, bf16)],
        4,
        [(1, model)],
    )

    ffo_blocks = [ffo_own, swap_seq(ffo_own, 1), swap_seq(ffo_own, 2)]
    near_gate, near_up, *near_share = back(
        ffo_blocks[:2], value16, slope16, w_down, w_gate, w_up, 0
    )
    ffo_two = after(ffo_blocks[2], near_gate)
    ffo_blocks = ffo_blocks[:2] + [ffo_two, swap_seq(ffo_two, 1)]
    away_down, here_down = owners.product_halves(side, [act16], [ffo_blocks], 256)
    come_down = owners.swap(away_down)
    far_blocks = list(lax.optimization_barrier((away_down, *ffo_blocks[2:]))[1:])
    far_gate, far_up, *far_share = back(far_blocks, value16, slope16, w_down, w_gate, w_up, 2)
    pair = add_half(far_share[0], swap_seq(far_share[1], 1), 4)
    far_sum = swap_seq(pair, 2)
    near_one = swap_seq(near_share[1], 1)
    fed_left = [after(fed_blocks[0], pair, near_one)] + fed_blocks[1:]
    away_gate, here_gate = owners.product_halves(side, fed_left, [[near_gate, far_gate]], 384)
    come_gate = owners.swap(away_gate)
    half_down = owners.fold(after(here_down, away_gate), come_down)
    grad_down = owners.scatter_row(half_down)
    fed_left = [after(fed_left[0], half_down)] + fed_left[1:]
    away_up, here_up = owners.product_halves(side, fed_left, [[near_up, far_up]], 384)
    come_up = owners.swap(away_up)
    shares = [after(near_share[0], away_up), near_one, far_sum]
    grad_mixed, grad_attn16, *grad_heads, gain_mixed_part = mid_back(
        self_index, shares, cotangent, mixed, attn, w_out, gains, 4
    )
    grad_heads = [grad_heads[0]] + [swap_seq(grad_heads[r], r) for r in range(1, SEQ)]

    half_gate = owners.fold(after(here_gate, *grad_heads), come_gate)
    grad_gate = owners.scatter_row(half_gate)
    grad_heads[0] = after(grad_heads[0], half_gate)
    grad_queries, keep_kv, send_kv = attend_back(
        meta, queries, mine_kv, other_kv, probs, grad_heads, scale, 256
    )
    come_kv = swap_seq(send_kv, 1)
    grad_qkv16, gain_query_part, gain_key_part, *normed_blocks = project_back(
        jnp.stack([core]).astype(jnp.int32),
        grad_queries,
        after(keep_kv, grad_down),
        come_kv,
        query_raw,
        kv_raw,
        cosine,
        sine,
        head_gains,
        w_own,
    )
    half_up = owners.fold(after(here_up, grad_qkv16), come_up)
    grad_up = owners.scatter_row(half_up)
    grad_out_share = to_half(inner_rows(heads16, after(grad_attn16, half_up)))
    grad_out_view = grad_out_share.reshape(fsdp, SEQ, out_part, model)
    out_blocks = [
        lax.dynamic_index_in_dim(grad_out_view, me ^ r, 1, keepdims=False) for r in range(SEQ)
    ]
    out_pair = pair_sum(out_blocks[2], swap_seq(out_blocks[3], 1))
    out_one = pair_sum(out_blocks[0], swap_seq(out_blocks[1], 1))
    out_two = swap_seq(out_pair, 2)
    proj_left = after(normed16, out_pair, out_one)
    away_proj, here_proj = owners.product_halves(side, [proj_left], [[grad_qkv16]], 384)
    grad_out_part = pair_sum(out_one, after(out_two, away_proj))
    normed_pair = pair_sum(normed_blocks[2], swap_seq(normed_blocks[3], 1))
    normed_two = swap_seq(normed_pair, 2)
    normed_one = swap_seq(normed_blocks[1], 1)

    short = jnp.stack([gain_query_part[0], gain_key_part[0]], axis=1).reshape(fsdp, short_rows, 2)
    short = jnp.pad(short, ((0, 0), (0, rows - short_rows), (0, 0))).reshape(model, 2)
    gain_parts = jnp.concatenate(
        [jnp.stack([gain_mixed_part[0], gain_final_part[0]], axis=1), short], axis=1
    )
    gain_parts = jnp.pad(gain_parts, ((0, 0), (0, 128 - gain_parts.shape[1])))
    away_gains, here_gains = owners.halves(to_half(gain_parts))
    away_out, here_out = owners.halves(grad_out_part.reshape(fsdp * out_part, model))
    wide = 2 * head_width + 128

    def pile(proj, gains, out):
        upper = jnp.concatenate([proj, gains], axis=2)
        rest = jnp.pad(out[:, :, wide:], ((0, 0), (0, 0), (0, 2 * wide - model)))
        return jnp.concatenate([upper, out[:, :, :wide], rest], axis=1)

    away_small = pile(away_proj, away_gains, away_out)
    here_small = pile(here_proj, here_gains, here_out)
    come_small = owners.swap(after(away_small, grad_gate))
    out_down = natural(gather_seq(after(grad_down, away_small)), me)
    out_down = jnp.concatenate(out_down).astype(f32)
    half_small = owners.fold(here_small, come_small)
    grad_small = owners.scatter_direct(half_small)

    def input_end(first, second, third, values, grad, gains):
        total = first.astype(f32) + second.astype(f32) + third.astype(f32)
        return (grad + rms_back(values.astype(f32), gains[0:1], total)[0],)

    (grad_tokens,) = fused(
        input_end,
        [normed_blocks[0], normed_one, normed_two, tokens, grad_mixed],
        [gains],
        [(tokens.shape, f32)],
        4,
    )

    def spread(own, *later):
        blocks = gather_seq(own)
        if later:
            blocks[0] = after(blocks[0], *later)
        if fsdp <= 8:
            return spread_columns(self_index, blocks, fsdp)
        stack = jnp.stack([b.reshape(rows, fsdp, part) for b in natural(blocks, me)], axis=2)
        return stack.reshape(rows, hidden).astype(f32)

    out_gate = spread(grad_gate)

    feed_sum = jnp.sum(
        grad_gate.astype(f32) * gate_own.astype(f32)
        + grad_up.astype(f32) * up_own.astype(f32),
        axis=1,
    )
    upper = grad_small[:rows]
    input_sum = jnp.sum(
        upper[:, : 2 * head_width] * attn_own[:, : 2 * head_width].astype(f32), axis=1
    )
    tail = jnp.concatenate(
        [upper[:, 2 * head_width : 2 * head_width + 4], jnp.stack([input_sum, feed_sum], axis=1)],
        axis=1,
    )
    tail = jnp.pad(tail, ((0, 0), (0, 128 - tail.shape[1])))
    small = jnp.concatenate(
        [
            to_half(jnp.concatenate([upper[:, : 2 * head_width], tail], axis=1)),
            to_half(after(grad_small, out_gate, out_down, grad_tokens)[rows:]),
        ]
    )
    out_up = spread(grad_up, small)
    small = gather_seq(small)
    lower = [b[rows:] for b in natural(small, me)]
    out_out = jnp.concatenate(
        [
            jnp.concatenate([b[:out_part], b[out_part:, : model - wide]], axis=1)
            for b in lower
        ]
    ).astype(f32)
    small = [b[:rows] for b in small]
    out_query = jnp.concatenate([b[:, :head_width] for b in natural(small, me)], axis=1).astype(f32)
    kv = [b[:, head_width : 2 * head_width].astype(f32) for b in small]
    same, cross = kv[0] + kv[2], kv[1] + kv[3]
    out_key = jnp.where(core == 0, same, cross)
    out_value = jnp.where(core == 0, cross, same)
    tails = sum(b[:, 2 * head_width :].astype(f32) for b in small)
    own_gains = attn_own[:, 2 * head_width : 2 * head_width + 128].astype(f32)
    out_g_mixed = tails[:, 0]
    out_g_final = tails[:, 1]
    out_g_query = tails[:short_rows, 2]
    out_g_key = tails[:short_rows, 3]
    out_g_input = tails[:, 4] / own_gains[:, 0]
    out_g_feed = tails[:, 5] / own_gains[:, 2]
    return (
        output,
        grad_tokens,
        out_query,
        out_key,
        out_value,
        out_out,
        out_gate,
        out_up,
        out_down,
        out_g_input,
        out_g_query,
        out_g_key,
        out_g_mixed,
        out_g_feed,
        out_g_final,
    )


def solution(mesh):
    by_token = P(("fsdp", "seq"), None)
    by_row = P("fsdp", None)
    by_one = P("fsdp")
    return jax.shard_map(
        partial(body, fsdp=mesh.shape["fsdp"]),
        mesh=mesh,
        in_specs=(by_token,) * 2 + (by_one,) * 2 + (by_row,) * 7 + (by_one,) * 6,
        out_specs=(by_token,) * 2 + (by_row,) * 7 + (by_one,) * 6,
        check_vma=False,
    )
```

```python
from functools import partial

import jax
import jax.numpy as jnp
from jax import lax
from jax.experimental import pallas as pl
from jax.experimental.pallas import tpu as pltpu
from jax.sharding import PartitionSpec as P

epsilon = 1e-06
f32 = jnp.float32
bf16 = jnp.bfloat16
SEQ = 4


def rms_scale(values, gain):
    return values * lax.rsqrt(jnp.mean(values * values, axis=-1, keepdims=True) + epsilon) * gain


def rotate(values, cosine, sine):
    half_width = values.shape[-1] // 2
    first_half = values[..., :half_width]
    second_half = values[..., half_width:]
    return jnp.concatenate(
        [first_half * cosine - second_half * sine, second_half * cosine + first_half * sine],
        axis=-1,
    )


def rope_tables(places, width):
    half_width = width // 2
    inverse = 1.0 / 1000000.0 ** (jnp.arange(half_width, dtype=f32) * 2.0 / width)
    angles = places.astype(f32)[:, None] * inverse[None, :]
    return (jnp.cos(angles), jnp.sin(angles))


def head_norm(raw, gain, cosine, sine):
    return rotate(rms_scale(raw, gain), cosine, sine)


def mult(left, right):
    return jnp.dot(left, right, preferred_element_type=f32)


def inner_rows(left, right):
    return lax.dot_general(left, right, (((0,), (0,)), ((), ())), preferred_element_type=f32)


def outer_cols(left, right):
    return lax.dot_general(left, right, (((1,), (1,)), ((), ())), preferred_element_type=f32)


def to_half(values):
    return values.astype(bf16)


def gated(gate_in, up_in):
    return jax.nn.gelu(gate_in, approximate=True) * up_in


MIB = 2**20


def held(shape):
    return pl.BlockSpec(shape, lambda *at: (0,) * len(shape), pipeline_mode=pl.Buffered(1))


def call(kernel, grid, in_specs, out_specs, outs, flops, limit=60, scratch=(), exps=0, same=None):
    shapes = [jax.ShapeDtypeStruct(s, d) for s, d in outs]
    size = sum(o.size * o.dtype.itemsize for o in shapes)
    made = pl.pallas_call(
        kernel,
        grid=grid,
        in_specs=in_specs,
        out_specs=out_specs,
        out_shape=shapes,
        scratch_shapes=list(scratch),
        input_output_aliases=same or {},
        compiler_params=pltpu.CompilerParams(vmem_limit_bytes=limit * MIB),
        cost_estimate=pl.CostEstimate(
            flops=flops // 50, bytes_accessed=size // 50, transcendentals=exps // 50
        ),
    )
    return lambda *operands: list(made(*operands))


def fused_kernel(function, ins, outs, sums, *refs):
    results = function(*[ref[...] for ref in refs[:ins]])
    for ref, value in zip(refs[ins : ins + outs], results[:outs], strict=True):
        ref[...] = value.astype(ref.dtype)
    for ref, value in zip(refs[ins + outs :], results[outs:], strict=True):

        @pl.when(pl.program_id(0) == 0)
        def _():
            ref[...] = jnp.zeros_like(ref)

        ref[...] += value


def fused(function, by_row, whole, outs, steps, sums=()):
    def split(shape):
        return pl.BlockSpec(
            (shape[0] // steps, *shape[1:]), lambda i: (i, *(0 for _ in shape[1:]))
        )

    return call(
        partial(fused_kernel, function, len(by_row) + len(whole), len(outs), len(sums)),
        (steps,),
        [split(v.shape) for v in by_row] + [held(v.shape) for v in whole],
        [split(s) for s, _ in outs] + [pl.BlockSpec(s, lambda i: (0, 0)) for s in sums],
        [*outs, *((s, f32) for s in sums)],
        flops=0,
    )(*by_row, *whole)


def add_half(first, second, steps):
    function = lambda a, b: (a.astype(f32) + b.astype(f32),)
    return fused(function, [first, second], [], [(first.shape, bf16)], steps)[0]


def pair_sum(first, second):
    return to_half(first.astype(f32) + second.astype(f32))


def rms_back(values, gain, grad):
    r = lax.rsqrt(jnp.mean(values * values, axis=-1, keepdims=True) + epsilon)
    scaled = grad * gain
    mean = jnp.mean(values * scaled, axis=-1, keepdims=True)
    return r * scaled - values * (r * r * r * mean), grad * values * r


def column_sum(values):
    return jnp.sum(values, axis=0, keepdims=True)


def mid_kernel(owners, quarters, me_ref, x_ref, *refs):
    heads = refs[:SEQ]
    weights = refs[SEQ : SEQ + quarters]
    gains_ref, all_ref, w_ref, attn_ref, mixed_ref, fed_ref = refs[SEQ + quarters :]
    width = heads[0].shape[1]
    for r, head in enumerate(heads):
        start = pl.multiple_of(jnp.bitwise_xor(me_ref[0], r) * width, 128)
        all_ref[:, pl.ds(start, width)] = head[...]
    if quarters == 1:
        w_ref[...] = weights[0][...]
    else:
        for r, weight in enumerate(weights):
            size = weight.shape[0] // owners
            for f in range(owners):
                start = (f * SEQ + jnp.bitwise_xor(me_ref[0], r)) * size
                start = pl.multiple_of(start, 16)
                w_ref[pl.ds(start, size), :] = weight[f * size : (f + 1) * size, :]
    attn = mult(all_ref[...], w_ref[...])
    attn_ref[...] = attn
    mixed = x_ref[...].astype(f32) + rms_scale(attn, gains_ref[1:2, :])
    mixed_ref[...] = mixed
    fed_ref[...] = to_half(rms_scale(mixed, gains_ref[2:3, :]))


def mid(me, tokens, heads, weights, gains, owners):
    rows, model = tokens.shape
    width = heads[0].shape[1] * SEQ
    specs = [held(v.shape) for v in [tokens, *heads, *weights, gains]]
    outs = [
        ((rows, width), bf16),
        ((width, model), bf16),
        ((rows, model), f32),
        ((rows, model), f32),
        ((rows, model), bf16),
    ]
    return call(
        partial(mid_kernel, owners, len(weights)),
        (1,),
        [pl.BlockSpec(memory_space=pltpu.SMEM)] + specs,
        [pl.BlockSpec(s, lambda i: (0, 0)) for s, _ in outs],
        outs,
        flops=2 * rows * width * model,
    )(me, tokens, *heads, *weights, gains)


def mid_back_kernel(me_ref, a_ref, b_ref, c_ref, dy_ref, mixed_ref, attn_ref, w_ref, gains_ref, *refs):
    grad_ref, grad_attn_ref = refs[:2]
    outs, sum_ref, heads_ref = refs[2 : 2 + SEQ], refs[2 + SEQ], refs[3 + SEQ]
    grad_fed = a_ref[...].astype(f32) + b_ref[...].astype(f32) + c_ref[...].astype(f32)
    part, _ = rms_back(mixed_ref[...], gains_ref[2:3, :], grad_fed)
    grad_mixed = dy_ref[...].astype(f32) + part
    grad_ref[...] = grad_mixed
    grad_attn, terms = rms_back(attn_ref[...], gains_ref[1:2, :], grad_mixed)
    half = to_half(grad_attn)
    grad_attn_ref[...] = half
    heads_ref[...] = to_half(outer_cols(half, w_ref[...]))
    width = outs[0].shape[1]
    for r, out in enumerate(outs):
        start = pl.multiple_of(jnp.bitwise_xor(me_ref[0], r) * width, 128)
        out[...] = heads_ref[:, pl.ds(start, width)]

    @pl.when(pl.program_id(0) == 0)
    def _():
        sum_ref[...] = jnp.zeros_like(sum_ref)

    sum_ref[...] += column_sum(terms)


def mid_back(me, shares, cotangent, mixed, attn, w_out, gains, steps):
    rows, model = mixed.shape
    total = w_out.shape[0]
    by_row = [*shares, cotangent, mixed, attn]
    row = lambda width: pl.BlockSpec((rows // steps, width), lambda i: (i, 0))
    outs = [((rows, model), f32), ((rows, model), bf16)]
    outs += [((rows, total // SEQ), bf16)] * SEQ
    return call(
        mid_back_kernel,
        (steps,),
        [pl.BlockSpec(memory_space=pltpu.SMEM)]
        + [row(model) for _ in by_row]
        + [held(w_out.shape), held(gains.shape)],
        [row(s[1]) for s, _ in outs] + [pl.BlockSpec((1, model), lambda i: (0, 0))],
        [*outs, ((1, model), f32)],
        flops=2 * rows * model * total,
        scratch=[pltpu.VMEM((rows // steps, total), bf16)],
    )(me, *by_row, w_out, gains)


def turn_back(grad, cosine, sine):
    half = grad.shape[-1] // 2
    a, b = grad[:, :half], grad[:, half:]
    return jnp.concatenate([a * cosine + b * sine, b * cosine - a * sine], axis=-1)


def project_back_kernel(core_ref, *refs):
    dq_ref, keep_ref, come_ref, q_raw_ref, kv_raw_ref, cos_ref, sin_ref, gains_ref, w_ref = refs[:9]
    grad_ref, q_sum_ref, k_sum_ref = refs[9:12]
    outs = refs[12:]
    cosine, sine = cos_ref[...], sin_ref[...]
    head = dq_ref.shape[1]
    first = core_ref[0] == 0
    grad_q, q_terms = rms_back(
        q_raw_ref[...], gains_ref[4:5, :], turn_back(dq_ref[...], cosine, sine)
    )
    grad_kv = keep_ref[...] + come_ref[...].astype(f32)
    grad_k, k_terms = rms_back(
        kv_raw_ref[...], gains_ref[5:6, :], turn_back(grad_kv, cosine, sine)
    )
    grad_ref[:, :head] = to_half(grad_q)
    grad_ref[:, head:] = to_half(jnp.where(first, grad_k, grad_kv))
    share = to_half(outer_cols(grad_ref[...], w_ref[...]))
    for r, out in enumerate(outs):

        @pl.when(pl.program_id(0) == r)
        def _():
            out[...] = share

    @pl.when(pl.program_id(0) == 0)
    def _():
        q_sum_ref[...] = jnp.zeros_like(q_sum_ref)
        k_sum_ref[...] = jnp.zeros_like(k_sum_ref)

    q_sum_ref[...] += column_sum(q_terms)
    k_sum_ref[...] += jnp.where(first, column_sum(k_terms), 0.0)


def project_back(core, dq, keep, come, q_raw, kv_raw, cosine, sine, head_gains, w_own):
    rows, head = dq.shape
    model = w_own.shape[0]
    block = rows // SEQ
    by_row = [dq, keep, come, q_raw, kv_raw, cosine, sine]
    row = lambda width: pl.BlockSpec((block, width), lambda i: (i, 0))
    fixed = lambda shape: pl.BlockSpec(shape, lambda i: (0, 0))
    return call(
        project_back_kernel,
        (SEQ,),
        [pl.BlockSpec(memory_space=pltpu.SMEM)]
        + [row(v.shape[1]) for v in by_row]
        + [held(head_gains.shape), held(w_own.shape)],
        [row(2 * head), fixed((1, head)), fixed((1, head))] + [fixed((block, model))] * SEQ,
        [((rows, 2 * head), bf16), ((1, head), f32), ((1, head), f32)]
        + [((block, model), bf16)] * SEQ,
        flops=4 * rows * head * model,
    )(core, *by_row, head_gains, w_own)


def front_kernel(count, rows, short, packed, meta_ref, *refs):
    tokens = refs[:SEQ]
    pieces = refs[SEQ : SEQ + count]
    cos_ref, sin_ref = refs[SEQ + count : SEQ + count + 2]
    normed_ref, q_ref, kv_ref, q_raw_ref, kv_raw_ref, w_ref, out_ref, gains_ref, head_gains_ref = (
        refs[SEQ + count + 2 : -2]
    )
    x_ref, columns_ref = refs[-2:]
    at = pl.program_id(0)
    head = q_ref.shape[1]

    @pl.when(at == 0)
    def _():
        for j, piece in enumerate(pieces):
            size = piece.shape[0] - 2 * packed
            start = pl.multiple_of(meta_ref[1 + j] * rows, 16)
            w_ref[pl.ds(start, size), :] = piece[:size, : 2 * head]
            columns_ref[pl.ds(start, size), :] = piece[:size, 2 * head :].astype(f32)
            if packed:
                start = pl.multiple_of(meta_ref[1 + j] * packed, 16)
                wide = piece.shape[1]
                rest = out_ref.shape[1] - wide
                out_ref[pl.ds(start, packed), :wide] = piece[size : size + packed, :]
                out_ref[pl.ds(start, packed), wide:] = piece[size + packed :, :rest]
        gains = columns_ref[...].T[:8]
        gains_ref[...] = gains
        model = gains.shape[1]
        from_row = lax.broadcasted_iota(jnp.int32, (model, head), 0)
        to_col = lax.broadcasted_iota(jnp.int32, (model, head), 1)
        owner = to_col >> (short.bit_length() - 1)
        wanted = owner * rows + (to_col & (short - 1))
        pick = jnp.where(from_row == wanted, 1.0, 0.0)
        head_gains_ref[...] = mult(to_half(gains), to_half(pick))

    for r in range(SEQ):

        @pl.when(at == r)
        def _():
            x_ref[...] = tokens[r][...].astype(f32)

    values = x_ref[...]
    normed = to_half(rms_scale(values, gains_ref[0:1, :]))
    normed_ref[...] = normed
    raw = mult(normed, w_ref[...])
    q_raw = raw[:, :head]
    kv_raw = raw[:, head:]
    q_raw_ref[...] = q_raw
    kv_raw_ref[...] = kv_raw
    cosine, sine = cos_ref[...], sin_ref[...]
    q_ref[...] = to_half(head_norm(q_raw, head_gains_ref[4:5, :], cosine, sine))
    keyed = head_norm(kv_raw, head_gains_ref[5:6, :], cosine, sine)
    kv_ref[...] = to_half(jnp.where(meta_ref[0] == 0, keyed, kv_raw))


def front(tokens, pieces, meta, cosine, sine, rows, short, packed):
    block, model = tokens[0].shape
    head = 2 * cosine.shape[1]
    total = block * SEQ
    out_shape = (max(8, packed * len(pieces)), model)
    slab = lambda width: pl.BlockSpec((block, width), lambda i: (i, 0))
    fixed = lambda shape: pl.BlockSpec(shape, lambda i: (0, 0))
    return call(
        partial(front_kernel, len(pieces), rows, short, packed),
        (SEQ,),
        [pl.BlockSpec(memory_space=pltpu.SMEM)]
        + [held(t.shape) for t in tokens]
        + [held(p.shape) for p in pieces]
        + [slab(head // 2)] * 2,
        [slab(model), slab(head), slab(head), slab(head), slab(head)]
        + [fixed((model, 2 * head)), fixed(out_shape), fixed((8, model)), fixed((8, head))],
        [
            ((total, model), bf16),
            ((total, head), bf16),
            ((total, head), bf16),
            ((total, head), f32),
            ((total, head), f32),
            ((model, 2 * head), bf16),
            (out_shape, bf16),
            ((8, model), f32),
            ((8, head), f32),
        ],
        flops=4 * total * model * head,
        scratch=[
            pltpu.VMEM((block, model), f32),
            pltpu.VMEM((model, 128), f32),
        ],
    )(meta, *tokens, *pieces, cosine, sine)


def twins(values):
    size = values.shape[0] // SEQ
    return jnp.concatenate([values[(r ^ 1) * size : (r ^ 1) * size + size] for r in range(SEQ)])


def split_pair(meta_ref, mine_ref, other_ref, keys_ref, values_ref):
    mine, other = mine_ref[...], twins(other_ref[...])
    first = meta_ref[0] == 0

    @pl.when(first)
    def _():
        keys_ref[...] = mine
        values_ref[...] = other

    @pl.when(jnp.logical_not(first))
    def _():
        keys_ref[...] = other
        values_ref[...] = mine


def attend_kernel(
    scale, meta_ref, q_ref, mine_ref, other_ref, code_ref, low_ref, high_ref, *refs
):
    outs, (probs_ref, keys_ref, values_ref) = refs[:SEQ], refs[SEQ:]
    at = pl.program_id(0)

    @pl.when(at == 0)
    def _():
        split_pair(meta_ref, mine_ref, other_ref, keys_ref, values_ref)

    scores = outer_cols(q_ref[...], keys_ref[...])
    code = code_ref[...]
    seen = (code >= low_ref[...]) & (code <= high_ref[...])
    expd = jnp.where(seen, jnp.exp2(scores * (scale * 1.4426950408889634)), 0.0)
    total = jnp.sum(expd, axis=1, keepdims=True)
    probs = to_half(expd * (1.0 / total))
    probs_ref[...] = probs
    out = to_half(mult(probs, values_ref[...]))
    block = out.shape[0]
    steps = outs[0].shape[0] // block
    for r in range(SEQ):
        for s in range(steps):

            @pl.when(at == r * steps + s)
            def _():
                outs[r][s * block : (s + 1) * block, :] = out


def attend(meta, queries, mine, other, code, low, high, scale, block):
    rows, width = queries.shape
    count = mine.shape[0]
    slab = pl.BlockSpec((block, width), lambda i: (i, 0))
    thin = pl.BlockSpec((block, 1), lambda i: (i, 0))
    part = pl.BlockSpec((rows // SEQ, width), lambda i: (0, 0))
    return call(
        partial(attend_kernel, scale),
        (rows // block,),
        [pl.BlockSpec(memory_space=pltpu.SMEM), slab, held(mine.shape), held(mine.shape)]
        + [pl.BlockSpec((1, count), lambda i: (0, 0)), thin, thin],
        [part] * SEQ + [pl.BlockSpec((block, count), lambda i: (i, 0))],
        [((rows // SEQ, width), bf16)] * SEQ + [((rows, count), bf16)],
        flops=4 * rows * count * width,
        exps=rows * count,
        scratch=[pltpu.VMEM((count, width), bf16)] * 2,
    )(meta, queries, mine, other, code, low, high)


def attend_back_kernel(scale, meta_ref, q_ref, mine_ref, other_ref, p_ref, *refs):
    grads_in = refs[:SEQ]
    dq_ref, keep_ref, send_ref, keys_ref, values_ref, dk_ref, dv_ref, g_ref = refs[SEQ:]
    at = pl.program_id(0)

    @pl.when(at == 0)
    def _():
        split_pair(meta_ref, mine_ref, other_ref, keys_ref, values_ref)
        dk_ref[...] = jnp.zeros_like(dk_ref)
        dv_ref[...] = jnp.zeros_like(dv_ref)

    block = g_ref.shape[0]
    steps = grads_in[0].shape[0] // block
    for r in range(SEQ):
        for s in range(steps):

            @pl.when(at == r * steps + s)
            def _():
                g_ref[...] = grads_in[r][s * block : (s + 1) * block, :]

    probs = p_ref[...]
    grads = g_ref[...]
    wide = probs.astype(f32)
    grad_probs = outer_cols(grads, values_ref[...])
    centre = jnp.sum(wide * grad_probs, axis=1, keepdims=True)
    grad_scores = to_half(wide * (grad_probs - centre))
    dq_ref[...] = scale * mult(grad_scores, keys_ref[...])
    dk_ref[...] += scale * inner_rows(grad_scores, q_ref[...])
    dv_ref[...] += inner_rows(probs, grads)

    @pl.when(at == pl.num_programs(0) - 1)
    def _():
        first = meta_ref[0] == 0
        keep_ref[...] = jnp.where(first, dk_ref[...], dv_ref[...])
        send_ref[...] = twins(to_half(jnp.where(first, dv_ref[...], dk_ref[...])))


def attend_back(meta, queries, mine, other, probs, grads, scale, block):
    rows, width = queries.shape
    count = mine.shape[0]
    whole = pl.BlockSpec((count, width), lambda i: (0, 0))
    slab = pl.BlockSpec((block, width), lambda i: (i, 0))
    return call(
        partial(attend_back_kernel, scale),
        (rows // block,),
        [pl.BlockSpec(memory_space=pltpu.SMEM), slab, held(mine.shape), held(mine.shape)]
        + [pl.BlockSpec((block, count), lambda i: (i, 0))]
        + [held(g.shape) for g in grads],
        [slab, whole, whole],
        [((rows, width), f32), ((count, width), f32), ((count, width), bf16)],
        flops=8 * rows * count * width,
        scratch=[pltpu.VMEM((count, width), bf16)] * 2
        + [pltpu.VMEM((count, width), f32)] * 2
        + [pltpu.VMEM((block, width), bf16)],
    )(meta, queries, mine, other, probs, *grads)


def spread_kernel(owners, me_ref, *refs):
    blocks, out_ref, all_ref = refs[:SEQ], refs[SEQ], refs[SEQ + 1]
    for r, block in enumerate(blocks):
        all_ref[jnp.bitwise_xor(me_ref[0], r)] = block[...].astype(f32)
    part = blocks[0].shape[1] // owners
    out_ref[...] = jnp.concatenate(
        [all_ref[t][:, f * part : (f + 1) * part] for f in range(owners) for t in range(SEQ)],
        axis=1,
    )


def spread_columns(me, blocks, owners):
    rows, width = blocks[0].shape
    steps = 3 if rows % 48 == 0 else 1
    step = rows // steps
    row = lambda w: pl.BlockSpec((step, w), lambda i: (i, 0))
    return call(
        partial(spread_kernel, owners),
        (steps,),
        [pl.BlockSpec(memory_space=pltpu.SMEM)] + [row(width)] * SEQ,
        [row(SEQ * width)],
        [((rows, SEQ * width), f32)],
        flops=0,
        scratch=[pltpu.VMEM((SEQ, step, width), f32)],
    )(me, *blocks)[0]


def pick_block(blocks, into_ref):
    for r, block in enumerate(blocks):

        @pl.when(pl.program_id(0) == r)
        def _():
            into_ref[...] = block[...]


def feed_rows(x_ref, gate_ref, up_ref, act_ref, value_ref, slope_ref):
    rows = x_ref[...]
    gate = mult(rows, gate_ref[...])
    upper = mult(rows, up_ref[...])
    c = 0.7978845608028654
    square = gate * gate
    bend = jnp.tanh(gate * (c + (c * 0.044715) * square))
    half = 0.5 + 0.5 * bend
    value = gate * half
    slope = half + (0.5 * gate) * (1.0 - bend * bend) * (c + (3 * c * 0.044715) * square)
    act_ref[...] = to_half(value * upper)
    value_ref[...] = to_half(value)
    slope_ref[...] = to_half(slope * upper)


def gate_up_kernel(count, pieces, kept, meta_ref, *refs):
    parts, outs = refs[count : count + 2 * pieces], refs[count + 2 * pieces + kept :]
    act_ref, value_ref, slope_ref = outs[:3]
    x_ref = outs[-1]
    gate_ref, up_ref = outs[3:5] if pieces == 2 else parts

    if pieces == 2:

        @pl.when(pl.program_id(0) == 0)
        def _():
            for w_ref, own in ((gate_ref, parts[:2]), (up_ref, parts[2:])):
                for half, ref in enumerate(own):
                    size = ref.shape[1]
                    for z in range(ref.shape[0]):
                        start = (2 * z + jnp.bitwise_xor(meta_ref[0], half)) * size
                        w_ref[pl.ds(pl.multiple_of(start, 16), size), :] = ref[z]

    pick_block(refs[:count], x_ref)
    feed_rows(x_ref, gate_ref, up_ref, act_ref, value_ref, slope_ref)


def gate_up(meta, blocks, gate_parts, up_parts, first, saved):
    block, model = blocks[0].shape
    width = gate_parts[0].shape[-1]
    total = block * SEQ
    slab = pl.BlockSpec((block, width), lambda i: (i + first, 0))
    whole = pl.BlockSpec((model, width), lambda i: (0, 0))
    parts = [*gate_parts, *up_parts]
    made = len(parts) - 2
    ins = 1 + len(blocks) + len(parts)
    out = call(
        partial(gate_up_kernel, len(blocks), len(gate_parts), len(saved)),
        (len(blocks),),
        [pl.BlockSpec(memory_space=pltpu.SMEM)]
        + [held(b.shape) for b in [*blocks, *parts]]
        + [pl.BlockSpec(memory_space=pl.ANY)] * len(saved),
        [slab] * 3 + [whole] * made,
        [((total, width), bf16)] * 3 + [((model, width), bf16)] * made,
        flops=4 * total * model * width,
        exps=total * width,
        scratch=[pltpu.VMEM((block, model), bf16)],
        limit=62,
        same={ins + i: i for i in range(len(saved))},
    )(meta, *blocks, *parts, *saved)
    return out if made else out + parts


def feed_kernel(x_ref, gate_ref, up_ref, down_ref, *refs):
    act_ref, value_ref, slope_ref, out_ref = refs[3:]
    feed_rows(x_ref, gate_ref, up_ref, act_ref, value_ref, slope_ref)
    out_ref[...] = to_half(mult(act_ref[...], down_ref[...]))


def feed_first(rows, w_gate, w_up, w_down, saved):
    block, model = rows.shape
    width = w_gate.shape[1]
    slab = pl.BlockSpec((block, width), lambda i: (0, 0))
    return call(
        feed_kernel,
        (1,),
        [held(v.shape) for v in [rows, w_gate, w_up, w_down]]
        + [pl.BlockSpec(memory_space=pl.ANY)] * 3,
        [slab] * 3 + [pl.BlockSpec((block, model), lambda i: (0, 0))],
        [(v.shape, bf16) for v in saved] + [((block, model), bf16)],
        flops=6 * block * model * width,
        limit=62,
        same={4: 0, 5: 1, 6: 2},
    )(rows, w_gate, w_up, w_down, *saved)


def down_kernel(x_ref, w_ref, *outs):
    out = to_half(mult(x_ref[...], w_ref[...]))
    for r, ref in enumerate(outs):

        @pl.when(pl.program_id(0) == r)
        def _():
            ref[...] = out


def down(rows, w_down, count):
    block = rows.shape[0] // (count + 1)
    width, model = w_down.shape
    out = pl.BlockSpec((block, model), lambda i: (0, 0))
    return call(
        down_kernel,
        (count,),
        [pl.BlockSpec((block, width), lambda i: (i + 1, 0)), held(w_down.shape)],
        [out] * count,
        [((block, model), bf16)] * count,
        flops=2 * count * block * model * width,
    )(rows, w_down)


def back_kernel(count, *refs):
    y_refs = refs[:count]
    value_ref, slope_ref, down_ref, gate_ref, up_ref, dg_ref, du_ref = refs[count : count + 7]
    outs, y_ref = refs[count + 7 : -1], refs[-1]
    pick_block(y_refs, y_ref)
    grad_act = outer_cols(y_ref[...], down_ref[...])
    dg_ref[...] = to_half(grad_act * slope_ref[...].astype(f32))
    du_ref[...] = to_half(grad_act * value_ref[...].astype(f32))
    out = to_half(outer_cols(dg_ref[...], gate_ref[...]) + outer_cols(du_ref[...], up_ref[...]))
    for r, ref in enumerate(outs):

        @pl.when(pl.program_id(0) == r)
        def _():
            ref[...] = out


def back(blocks, value, slope, w_down, w_gate, w_up, first):
    block, model = blocks[0].shape
    count = len(blocks)
    width = w_gate.shape[1]
    ahead = pl.BlockSpec((block, width), lambda i: (i + first, 0))
    slab = pl.BlockSpec((block, width), lambda i: (i, 0))
    out = pl.BlockSpec((block, model), lambda i: (0, 0))
    return call(
        partial(back_kernel, count),
        (count,),
        [held(b.shape) for b in blocks]
        + [ahead, ahead, held(w_down.shape), held(w_gate.shape), held(w_up.shape)],
        [slab, slab] + [out] * count,
        [((block * count, width), bf16)] * 2 + [((block, model), bf16)] * count,
        flops=6 * count * block * model * width,
        scratch=[pltpu.VMEM((block, model), bf16)],
    )(*blocks, value, slope, w_down, w_gate, w_up)


def cut_rows(blocks, many):
    each = many // len(blocks)
    size = blocks[0].shape[0] // each
    return [b[r * size : (r + 1) * size] for b in blocks for r in range(each)]


def rows_sum(left, right):
    total = inner_rows(left[0], right[0])
    for a, b in zip(left[1:], right[1:], strict=True):
        total = total + inner_rows(a, b)
    return total


def rows_kernel(counts, many, meta_ref, *refs):
    total_in = sum(counts)
    results = len(counts) - 1
    values = [ref[...] for ref in refs[:total_in]]
    left = cut_rows(values[: counts[0]], many)
    at = counts[0]
    totals = []
    for count in counts[1:]:
        totals.append(rows_sum(left, cut_rows(values[at : at + count], many)))
        at += count
    if len(refs) == total_in + results:
        for ref, total in zip(refs[total_in:], totals, strict=True):
            ref[...] = to_half(total)
        return
    outs, sums = refs[total_in : total_in + 2 * results], refs[total_in + 2 * results :]
    tile = left[0].shape[1]
    here = pl.ds(pl.multiple_of(pl.program_id(0) * tile, 128), tile)
    for ref, total in zip(sums, totals, strict=True):
        ref[here, :] = total

    @pl.when(pl.program_id(0) == pl.num_programs(0) - 1)
    def _():
        for o in range(results):
            for half, ref in enumerate(outs[2 * o : 2 * o + 2]):
                size = ref.shape[1]
                for z in range(ref.shape[0]):
                    start = (2 * z + jnp.bitwise_xor(meta_ref[0], 1 - half)) * size
                    ref[z] = to_half(sums[o][pl.ds(pl.multiple_of(start, 8), size), :])


def rows_product(meta, left, rights, tile, owners, cut=True):
    counts = [len(v) for v in [left, *rights]]
    many = max(counts)
    height = left[0].shape[1]
    widths = [r[0].shape[1] for r in rights]
    flat = [v for r in rights for v in r]
    steps = pl.cdiv(height, tile)
    shape = lambda w: (owners // 2, height // owners, w)
    if cut:
        specs = [pl.BlockSpec(shape(w), lambda i: (0, 0, 0)) for w in widths for _ in range(2)]
        outs = [(shape(w), bf16) for w in widths for _ in range(2)]
    else:
        specs = [pl.BlockSpec((tile, w), lambda i: (i, 0)) for w in widths]
        outs = [((height, w), bf16) for w in widths]
    return call(
        partial(rows_kernel, counts, many),
        (steps,),
        [pl.BlockSpec(memory_space=pltpu.SMEM)]
        + [pl.BlockSpec((v.shape[0], tile), lambda i: (0, i)) for v in left]
        + [held(v.shape) for v in flat],
        specs,
        outs,
        flops=2 * sum(v.shape[0] for v in left) * height * sum(widths),
        scratch=[pltpu.VMEM((steps * tile, w), f32) for w in widths] if cut else [],
        limit=62,
    )(meta, *left, *flat)


def after(value, *others):
    return lax.optimization_barrier((value, others))[0]


def swap_seq(values, bits):
    return lax.ppermute(values, "seq", [(i, i ^ bits) for i in range(SEQ)])


def gather_seq(own):
    one = swap_seq(own, 1)
    two = swap_seq(own, 2)
    return [own, one, two, swap_seq(two, 1)]


def natural(blocks, me):
    stack = jnp.stack(blocks)
    return [lax.dynamic_index_in_dim(stack, me ^ j, 0, keepdims=False) for j in range(SEQ)]


def reduce_seq(blocks):
    three = swap_seq(blocks[3], 1)
    pair = to_half(blocks[2].astype(f32) + three.astype(f32))
    two = swap_seq(pair, 2)
    one = swap_seq(blocks[1], 1)
    return blocks[0].astype(f32) + one.astype(f32) + two.astype(f32)


class Owners:
    def __init__(self, count):
        self.count = count
        self.rows = count // 2
        self.groups = [[2 * z + y for z in range(self.rows)] for y in range(2)]
        index = lax.axis_index("fsdp")
        self.low = index % 2
        self.high = index // 2
        self.direct = self.rows <= 4

    def swap(self, values):
        return lax.ppermute(values, "fsdp", [(i, i ^ 1) for i in range(self.count)])

    def shift(self, values, by):
        return lax.ppermute(
            values, "fsdp", [(i, (i + 2 * by) % self.count) for i in range(self.count)]
        )

    def gather_row(self, values):
        return lax.all_gather(values, "fsdp", axis=0, tiled=True, axis_index_groups=self.groups)

    def pair(self, mine, other, axis):
        first = jnp.where(self.low == 0, mine, other)
        second = jnp.where(self.low == 0, other, mine)
        return jnp.stack([first, second], axis=axis)

    def gather_pieces(self, own):
        if not self.direct:
            return [lax.all_gather(own, "fsdp", axis=0, tiled=True)], [jnp.int32(0)]
        far = [own] + [self.shift(own, by) for by in range(1, self.rows)]
        near = [self.swap(p) for p in far]
        starts = [lax.rem(self.high - by + self.rows, self.rows) * 2 for by in range(self.rows)]
        places = [s + self.low for s in starts] + [s + 1 - self.low for s in starts]
        return far + near, places

    def gather_wide(self, own, later):
        if not self.direct:
            return [lax.all_gather(own, "fsdp", axis=0, tiled=True)]
        size, width = own.shape
        mine = after(self.gather_row(own), later).reshape(self.rows, size, width)
        return [mine, self.swap(mine)]

    def gather_pair_first(self, own, later):
        size, width = own.shape
        both = self.pair(own, after(self.swap(own), later), 0).reshape(2 * size, width)
        return self.gather_row(both)

    def halves(self, whole):
        size = whole.shape[0] // self.count
        view = whole.reshape(self.rows, 2, size, whole.shape[1])
        away = lax.dynamic_index_in_dim(view, 1 - self.low, 1, keepdims=False)
        here = lax.dynamic_index_in_dim(view, self.low, 1, keepdims=False)
        return away, here

    def product_halves(self, side, left, rights, tile):
        if (left[0].shape[1] // self.count) % 8 == 0:
            return rows_product(side, left, rights, tile, self.count)
        whole = rows_product(side, left, rights, tile, self.count, False)
        return [half for value in whole for half in self.halves(value)]

    def fold(self, here, come):
        return add_half(here, come, 2 if here.shape[0] % 2 == 0 else 1)

    def scatter_row(self, half):
        return lax.psum_scatter(
            half.reshape(-1, half.shape[2]),
            "fsdp",
            scatter_dimension=0,
            axis_index_groups=self.groups,
            tiled=True,
        )

    def scatter_direct(self, half):
        if not self.direct:
            return self.scatter_row(half).astype(f32)
        total = lax.dynamic_index_in_dim(half, self.high, 0, keepdims=False).astype(f32)
        for by in range(1, self.rows):
            z = lax.rem(self.high + by, self.rows)
            away = lax.dynamic_index_in_dim(half, z, 0, keepdims=False)
            total = total + self.shift(away, by).astype(f32)
        return total


def body(
    tokens,
    cotangent,
    positions,
    segment,
    query_weight,
    key_weight,
    value_weight,
    out_weight,
    gate_weight,
    up_weight,
    down_weight,
    gain_input,
    gain_query,
    gain_key,
    gain_mixed,
    gain_feed,
    gain_final,
    fsdp,
):
    owners = Owners(fsdp)
    me = lax.axis_index("seq")
    core = me & 1
    tok_rows, model = tokens.shape
    group_len = positions.shape[0]
    rows = query_weight.shape[0]
    head_width = key_weight.shape[1]
    hidden = gate_weight.shape[1]
    slab = hidden // fsdp
    part = slab // SEQ
    scale = head_width ** (-0.5)

    head_cols = lax.dynamic_slice_in_dim(query_weight, me * head_width, head_width, axis=1)
    key_or_value = jnp.where(core == 0, key_weight, value_weight)
    short = jnp.stack([gain_query, gain_key], axis=1)
    short = jnp.pad(short, ((0, rows - short.shape[0]), (0, 0)))
    gains_own = jnp.concatenate(
        [jnp.stack([gain_input, gain_mixed, gain_feed, gain_final], axis=1), short], axis=1
    )
    gains_own = jnp.pad(gains_own, ((0, 0), (0, 128 - gains_own.shape[1])))
    out_rows = out_weight.shape[0]
    out_part = out_rows // SEQ
    out_own = lax.dynamic_slice_in_dim(out_weight, me * out_part, out_part, axis=0)
    out_own = to_half(out_own)
    attn_own = jnp.concatenate(
        [to_half(head_cols), to_half(key_or_value), to_half(gains_own)], axis=1
    )
    packed = out_part if owners.direct and out_part % 16 == 0 else 0
    if packed:
        wide = attn_own.shape[1]
        rest = jnp.pad(out_own[:, wide:], ((0, 0), (0, 2 * wide - model)))
        pack_own = jnp.concatenate([attn_own, out_own[:, :wide], rest])
    else:
        pack_own = attn_own

    def columns(weight):
        return to_half(
            jnp.concatenate(
                [
                    lax.dynamic_slice_in_dim(weight, f * slab + me * part, part, axis=1)
                    for f in range(fsdp)
                ],
                axis=1,
            )
        )

    pieces, starts = owners.gather_pieces(pack_own)
    ahead = pieces[: (len(pieces) + 1) // 2]
    tokens_out = after(tokens, pack_own)
    token_blocks = [tokens, swap_seq(tokens_out, 1), swap_seq(tokens_out, 2)]
    token_blocks.append(swap_seq(after(token_blocks[2], *ahead), 1))
    gate_own = columns(after(gate_weight, token_blocks[2], *ahead))
    up_own = columns(after(up_weight, gate_own))
    down_own = lax.dynamic_slice_in_dim(after(down_weight, up_own), me * part, part, axis=0)
    down_own = to_half(down_own)

    def own_order(values):
        return jnp.concatenate(
            [
                lax.dynamic_slice_in_dim(values, (me ^ r) * tok_rows, tok_rows)
                for r in range(SEQ)
            ]
        )

    places = own_order(positions)
    kinds = own_order(segment)
    cosine, sine = rope_tables(places, head_width)
    second = kinds == 2
    code = jnp.where(second, -places, places).astype(f32)[None, :]
    low = jnp.where(second, -places, 0).astype(f32)[:, None]
    high = jnp.where(second, group_len // 2 - 1, places).astype(f32)[:, None]
    short_rows = head_width // fsdp

    meta = jnp.stack([core] + starts).astype(jnp.int32)
    normed16, queries, mine_kv, query_raw, kv_raw, w_own, out_flat, gains, head_gains = front(
        token_blocks, pieces, meta, cosine, sine, rows, short_rows, packed
    )
    gate_parts = owners.gather_wide(gate_own, queries)
    other_kv = swap_seq(mine_kv, 1)
    *heads, probs = attend(meta, queries, mine_kv, other_kv, code, low, high, scale, 256)
    up_parts = owners.gather_wide(up_own, probs)
    w_down = owners.gather_pair_first(down_own, queries)
    heads = [heads[0]] + [swap_seq(heads[r], r) for r in range(1, SEQ)]
    self_index = jnp.stack([me]).astype(jnp.int32)
    if packed:
        quarters = gather_seq(after(out_flat, probs))
    else:
        out_flat = lax.all_gather(out_own, "fsdp", axis=0, tiled=True)
        w_out = jnp.stack(natural(gather_seq(out_flat), me)).reshape(SEQ, fsdp, out_part, model)
        quarters = [w_out.transpose(1, 0, 2, 3).reshape(fsdp * out_rows, model)]
    heads[0] = after(heads[0], *gate_parts)
    heads16, w_out, attn, mixed, fed_own = mid(self_index, tokens, heads, quarters, gains, fsdp)

    side = jnp.stack([owners.low]).astype(jnp.int32)
    fed_blocks = [fed_own, swap_seq(fed_own, 1), swap_seq(fed_own, 2)]
    *saved, w_gate, w_up = gate_up(side, fed_blocks[1:2], gate_parts, up_parts, 1, [])
    fed_two = after(fed_blocks[2], saved[0])
    fed_blocks = fed_blocks[:2] + [fed_two, swap_seq(fed_two, 1)]
    *saved, w_gate, w_up = gate_up(side, fed_blocks[2:], [w_gate], [w_up], 2, saved)
    share_one, share_two, share_three = down(saved[0], w_down, 3)
    share_one = swap_seq(share_one, 1)
    share_pair = pair_sum(share_two, swap_seq(share_three, 1))
    fed_first = after(fed_blocks[0], share_pair, share_one)
    act16, value16, slope16, share = feed_first(fed_first, w_gate, w_up, w_down, saved)
    shares = [share, share_one, swap_seq(share_pair, 2)]

    def feed_end(first, second, third, mixed, grad, gains):
        ffo = first.astype(f32) + second.astype(f32) + third.astype(f32)
        gain = gains[3:4]
        grad_ffo, terms = rms_back(ffo, gain, grad.astype(f32))
        return mixed + rms_scale(ffo, gain), grad_ffo, column_sum(terms)

    output, ffo_own, gain_final_part = fused(
        feed_end,
        [*shares, mixed, cotangent],
        [gains],
        [(tokens.shape, bf16), (tokens.shape, bf16)],
        2,
        [(1, model)],
    )

    ffo_blocks = [ffo_own, swap_seq(ffo_own, 1), swap_seq(ffo_own, 2)]
    near_gate, near_up, *near_share = back(
        ffo_blocks[:2], value16, slope16, w_down, w_gate, w_up, 0
    )
    ffo_two = after(ffo_blocks[2], near_gate)
    ffo_blocks = ffo_blocks[:2] + [ffo_two, swap_seq(ffo_two, 1)]
    away_down, here_down = owners.product_halves(side, [act16], [ffo_blocks], 256)
    come_down = owners.swap(away_down)
    far_blocks = list(lax.optimization_barrier((away_down, *ffo_blocks[2:]))[1:])
    far_gate, far_up, *far_share = back(far_blocks, value16, slope16, w_down, w_gate, w_up, 2)
    pair = add_half(far_share[0], swap_seq(far_share[1], 1), 2)
    far_sum = swap_seq(pair, 2)
    near_one = swap_seq(near_share[1], 1)
    fed_left = [after(fed_blocks[0], pair, near_one)] + fed_blocks[1:]
    away_gate, here_gate = owners.product_halves(side, fed_left, [[near_gate, far_gate]], 384)
    come_gate = owners.swap(away_gate)
    half_down = owners.fold(after(here_down, away_gate), come_down)
    grad_down = owners.scatter_row(half_down)
    fed_left = [after(fed_left[0], half_down)] + fed_left[1:]
    away_up, here_up = owners.product_halves(side, fed_left, [[near_up, far_up]], 384)
    come_up = owners.swap(away_up)
    shares = [after(near_share[0], away_up), near_one, far_sum]
    grad_mixed, grad_attn16, *grad_heads, gain_mixed_part = mid_back(
        self_index, shares, cotangent, mixed, attn, w_out, gains, 2
    )
    grad_heads = [grad_heads[0]] + [swap_seq(grad_heads[r], r) for r in range(1, SEQ)]

    half_gate = owners.fold(after(here_gate, *grad_heads), come_gate)
    grad_gate = owners.scatter_row(half_gate)
    grad_heads[0] = after(grad_heads[0], half_gate)
    grad_queries, keep_kv, send_kv = attend_back(
        meta, queries, mine_kv, other_kv, probs, grad_heads, scale, 512
    )
    come_kv = swap_seq(send_kv, 1)
    grad_qkv16, gain_query_part, gain_key_part, *normed_blocks = project_back(
        jnp.stack([core]).astype(jnp.int32),
        grad_queries,
        after(keep_kv, grad_down),
        come_kv,
        query_raw,
        kv_raw,
        cosine,
        sine,
        head_gains,
        w_own,
    )
    half_up = owners.fold(after(here_up, grad_qkv16), come_up)
    grad_up = owners.scatter_row(half_up)
    grad_out_share = to_half(inner_rows(heads16, after(grad_attn16, half_up)))
    grad_out_view = grad_out_share.reshape(fsdp, SEQ, out_part, model)
    out_blocks = [
        lax.dynamic_index_in_dim(grad_out_view, me ^ r, 1, keepdims=False) for r in range(SEQ)
    ]
    out_pair = pair_sum(out_blocks[2], swap_seq(out_blocks[3], 1))
    out_one = pair_sum(out_blocks[0], swap_seq(out_blocks[1], 1))
    out_two = swap_seq(out_pair, 2)
    proj_left = after(normed16, out_pair, out_one)
    away_proj, here_proj = owners.product_halves(side, [proj_left], [[grad_qkv16]], 384)
    grad_out_part = pair_sum(out_one, after(out_two, away_proj))
    normed_pair = pair_sum(normed_blocks[2], swap_seq(normed_blocks[3], 1))
    normed_two = swap_seq(normed_pair, 2)
    normed_one = swap_seq(normed_blocks[1], 1)

    short = jnp.stack([gain_query_part[0], gain_key_part[0]], axis=1).reshape(fsdp, short_rows, 2)
    short = jnp.pad(short, ((0, 0), (0, rows - short_rows), (0, 0))).reshape(model, 2)
    gain_parts = jnp.concatenate(
        [jnp.stack([gain_mixed_part[0], gain_final_part[0]], axis=1), short], axis=1
    )
    gain_parts = jnp.pad(gain_parts, ((0, 0), (0, 128 - gain_parts.shape[1])))
    away_gains, here_gains = owners.halves(to_half(gain_parts))
    away_out, here_out = owners.halves(grad_out_part.reshape(fsdp * out_part, model))
    wide = 2 * head_width + 128

    def pile(proj, gains, out):
        upper = jnp.concatenate([proj, gains], axis=2)
        rest = jnp.pad(out[:, :, wide:], ((0, 0), (0, 0), (0, 2 * wide - model)))
        return jnp.concatenate([upper, out[:, :, :wide], rest], axis=1)

    away_small = pile(away_proj, away_gains, away_out)
    here_small = pile(here_proj, here_gains, here_out)
    come_small = owners.swap(after(away_small, grad_gate))
    out_down = natural(gather_seq(after(grad_down, away_small)), me)
    out_down = jnp.concatenate(out_down).astype(f32)
    half_small = owners.fold(here_small, come_small)
    grad_small = owners.scatter_direct(half_small)

    def input_end(first, second, third, values, grad, gains):
        total = first.astype(f32) + second.astype(f32) + third.astype(f32)
        return (grad + rms_back(values.astype(f32), gains[0:1], total)[0],)

    (grad_tokens,) = fused(
        input_end,
        [normed_blocks[0], normed_one, normed_two, tokens, grad_mixed],
        [gains],
        [(tokens.shape, f32)],
        4,
    )

    def spread(own, *later):
        blocks = gather_seq(own)
        if later:
            blocks[0] = after(blocks[0], *later)
        if fsdp <= 8:
            return spread_columns(self_index, blocks, fsdp)
        stack = jnp.stack([b.reshape(rows, fsdp, part) for b in natural(blocks, me)], axis=2)
        return stack.reshape(rows, hidden).astype(f32)

    out_gate = spread(grad_gate)

    feed_sum = jnp.sum(
        grad_gate.astype(f32) * gate_own.astype(f32)
        + grad_up.astype(f32) * up_own.astype(f32),
        axis=1,
    )
    upper = grad_small[:rows]
    input_sum = jnp.sum(
        upper[:, : 2 * head_width] * attn_own[:, : 2 * head_width].astype(f32), axis=1
    )
    tail = jnp.concatenate(
        [upper[:, 2 * head_width : 2 * head_width + 4], jnp.stack([input_sum, feed_sum], axis=1)],
        axis=1,
    )
    tail = jnp.pad(tail, ((0, 0), (0, 128 - tail.shape[1])))
    small = jnp.concatenate(
        [
            to_half(jnp.concatenate([upper[:, : 2 * head_width], tail], axis=1)),
            to_half(after(grad_small, out_gate, out_down, grad_tokens)[rows:]),
        ]
    )
    out_up = spread(grad_up, small)
    small = gather_seq(small)
    lower = [b[rows:] for b in natural(small, me)]
    out_out = jnp.concatenate(
        [
            jnp.concatenate([b[:out_part], b[out_part:, : model - wide]], axis=1)
            for b in lower
        ]
    ).astype(f32)
    small = [b[:rows] for b in small]
    out_query = jnp.concatenate([b[:, :head_width] for b in natural(small, me)], axis=1).astype(f32)
    kv = [b[:, head_width : 2 * head_width].astype(f32) for b in small]
    same, cross = kv[0] + kv[2], kv[1] + kv[3]
    out_key = jnp.where(core == 0, same, cross)
    out_value = jnp.where(core == 0, cross, same)
    tails = sum(b[:, 2 * head_width :].astype(f32) for b in small)
    own_gains = attn_own[:, 2 * head_width : 2 * head_width + 128].astype(f32)
    out_g_mixed = tails[:, 0]
    out_g_final = tails[:, 1]
    out_g_query = tails[:short_rows, 2]
    out_g_key = tails[:short_rows, 3]
    out_g_input = tails[:, 4] / own_gains[:, 0]
    out_g_feed = tails[:, 5] / own_gains[:, 2]
    return (
        output,
        grad_tokens,
        out_query,
        out_key,
        out_value,
        out_out,
        out_gate,
        out_up,
        out_down,
        out_g_input,
        out_g_query,
        out_g_key,
        out_g_mixed,
        out_g_feed,
        out_g_final,
    )


def solution(mesh):
    by_token = P(("fsdp", "seq"), None)
    by_row = P("fsdp", None)
    by_one = P("fsdp")
    return jax.shard_map(
        partial(body, fsdp=mesh.shape["fsdp"]),
        mesh=mesh,
        in_specs=(by_token,) * 2 + (by_one,) * 2 + (by_row,) * 7 + (by_one,) * 6,
        out_specs=(by_token,) * 2 + (by_row,) * 7 + (by_one,) * 6,
        check_vma=False,
    )
```
